32 devices in a mesh: gx: 8 (over z, x), gy: 4 (over y, core).
Axes of the slice: x: 2, y: 2, z: 4, core: 2. Of those that a mesh axis runs over, the one named last changes fastest.
Arguments:
- position: float32 [2, 64, 64, 128], P(None, 'gx', 'gy'), may hold values from 0 to 1
- velocity: float32 [2, 64, 64, 128], P(None, 'gx', 'gy'), may hold values from -12 to 12
- volume: float32 [64, 64, 128], P('gx', 'gy'), may hold values from 0.5 to 2
- pressure_prev: float32 [64, 64, 128], P('gx', 'gy'), may hold values from -6 to 6
- fill: int32 [64, 64], P('gx', 'gy'), may hold values from 1 to 128, as said below
- drift_from: int32 [64, 64], P('gx', 'gy'), may hold values from 0 to 8
Outputs:
- pressure: float32 [64, 64, 128], P('gx', 'gy')
- velocity_new: float32 [2, 64, 64, 128], P(None, 'gx', 'gy')
The draws below stay inside these ranges and needn't reach their ends.
Inputs may be any that keep to these rules, and one draw needn't show every extreme that they name: fill lies in 1 to 128, and some bin holds 128 live particles. `drift_from`: code c names the bin at offset (c // 3 - 1, c % 3 - 1).
All inputs are finite; a program needn't handle non-finite values. Where the reference program divides by a largest or mean magnitude, that divisor is 1e-20 or more.
Results may differ from the reference program's by a relative error of at most 0.0035.
Values may be sent and summed in bfloat16 or wider, within the bound.
No kernel may reach another device: no remote copies, remote signals or barrier semaphores. Data moves between devices by JAX's collectives and lax.ppermute only.
A program may use at most 256 MiB of HBM per device.

```python
import math
import jax
import jax.numpy as jnp
import numpy as np
from jax import lax

P_SIZE = 128
SWEEPS = 4
GX = 64
GY = 64


def draw_fill(key, part):
    key = jax.random.fold_in(key, 11)
    raw = jax.random.randint(key, (GX, GY), 1, 2 * P_SIZE, dtype=jnp.int32)
    return jnp.minimum(raw, P_SIZE)


def draw_velocity(key, part):
    key = jax.random.fold_in(key, 23)
    along = 1.0 + 2.0 * jnp.arange(GX, dtype=jnp.float32) / max(GX - 1, 1)
    scale = along[None, :, None, None]
    base = jnp.clip(jax.random.normal(key, (2, GX, GY, P_SIZE), jnp.float32), -4.0, 4.0)
    return (base * scale).astype(jnp.float32)


def plant(drawn, own_key, least, largest):
    extent = drawn.shape
    place = [jax.random.randint(jax.random.fold_in(own_key, axis), (), 0, extent[axis]) for axis in range(len(extent))]
    drawn = drawn.at[tuple(place)].set(least)
    longest = extent.index(max(extent))
    place[longest] = (place[longest] + 1) % extent[longest]
    return drawn.at[tuple(place)].set(largest)


def steps_of(own_key, extent, shards, low, largest):
    level = 1.0
    for dim, parts in shards:
        heights = jax.random.uniform(jax.random.fold_in(jax.random.fold_in(own_key, 6), dim), (parts,), jnp.float32, low / len(shards), largest / len(shards))
        level = level * jnp.repeat(jnp.exp(heights), extent[dim] // parts).reshape((-1,) + (1,) * (len(extent) - 1 - dim))
    return level


def scatter_about(stream_key, shape, scale, bound, cuts=(), held_as=jnp.bfloat16):
    array = scale * jax.random.normal(stream_key, shape, jnp.float32)
    if cuts:
        array = array * steps_of(stream_key, shape, cuts, -0.22, 0.18)
    return jnp.clip(array, -bound, bound).astype(held_as)


def setup_inputs(seed: int = 0) -> dict:
    key_list = jax.random.split(jax.random.key(seed), 7)
    return {
        "position": jnp.clip(1.0 * jax.random.uniform(key_list[0], (2, GX, GY, P_SIZE), jnp.float32) ** steps_of(key_list[0], (2, GX, GY, P_SIZE), ((1, 8), (2, 4)), -0.2, 0.2), 0.0, 1.0),
        "velocity": draw_velocity(jax.random.fold_in(key_list[6], 71), 0),
        "volume": jnp.clip(jnp.exp(math.log(2.0) - 1.3862944 * jax.random.uniform(key_list[2], (GX, GY, P_SIZE), jnp.float32) ** steps_of(key_list[2], (GX, GY, P_SIZE), ((0, 8), (1, 4)), -0.2, 0.2)), 0.5, 2.0),
        "pressure_prev": scatter_about(key_list[3], (GX, GY, P_SIZE), 1.0, 6.0, ((0, 8), (1, 4)), jnp.float32),
        "fill": draw_fill(jax.random.fold_in(key_list[6], 71), 0),
        "drift_from": plant(jax.random.randint(key_list[5], (GX, GY), 0, 9), jax.random.fold_in(key_list[5], 1), 0, 8).astype(jnp.int32),
    }


cfl_number = 0.25
speed_eps = 1e-06
soft_sq = 0.01
shift_term = 1.0

def drift_bins(extended, codes, step):
    rows = codes.shape[0]
    cols = codes.shape[1]
    result = jnp.zeros((extended.shape[0], rows, cols, extended.shape[3]), extended.dtype)
    for offset in range(9):
        shift_x = offset // 3
        shift_y = offset % 3
        source = extended[:, shift_x:shift_x + rows, shift_y:shift_y + cols, :]
        moved_x = source[0] + float(shift_x - 1) + step * source[2]
        moved_y = source[1] + float(shift_y - 1) + step * source[3]
        moved = jnp.concatenate([moved_x[None], moved_y[None], source[2:]], axis=0)
        chosen = (codes == offset + 1)[None, :, :, None]
        result = result + jnp.where(chosen, moved, 0.0)
    return result

def gather_row(extended, row, cols):
    axis_pos = extended.ndim - 3
    block = lax.dynamic_slice_in_dim(extended, row, 3, axis=axis_pos)
    center = block[..., 1, 1:1 + cols, :]
    pieces = [block[..., code // 3, code % 3:code % 3 + cols, :] for code in range(9)]
    beside_all = jnp.stack(pieces, axis=-2)
    beside_all = beside_all.reshape(beside_all.shape[:-2] + (9 * beside_all.shape[-1],))
    return (center, beside_all)

def geometry(center, beside_all):
    width = center.shape[-1]
    off_x = jnp.asarray(np.repeat(np.arange(9) // 3 - 1, width).astype(np.float32))
    off_y = jnp.asarray(np.repeat(np.arange(9) % 3 - 1, width).astype(np.float32))
    delta_x = center[0][:, :, None] - (beside_all[0][:, None, :] + off_x)
    delta_y = center[1][:, :, None] - (beside_all[1][:, None, :] + off_y)
    dist_sq = delta_x * delta_x + delta_y * delta_y
    remain = jnp.maximum(1.0 - jnp.sqrt(dist_sq), 0.0)
    cubed = remain * remain * remain
    return (delta_x, delta_y, dist_sq, cubed)

def coefficients(center, beside_all, kappa):
    delta_x, delta_y, dist_sq, cubed = geometry(center, beside_all)
    lap = kappa * 40.0 * beside_all[4][:, None, :] * dist_sq * cubed / (dist_sq + soft_sq)
    return lap.astype(jnp.bfloat16)

def first_pass(center, beside_all, kappa):
    delta_x, delta_y, dist_sq, cubed = geometry(center, beside_all)
    lap = kappa * 40.0 * beside_all[4][:, None, :] * dist_sq * cubed / (dist_sq + soft_sq)
    coef = lap.astype(jnp.bfloat16)
    den = shift_term + lax.optimization_barrier(jnp.sum(coef.astype(jnp.float32), axis=-1))
    grad_w = 20.0 * cubed * beside_all[4][:, None, :]
    flow = (beside_all[2][:, None, :] - center[2][:, :, None]) * delta_x + (beside_all[3][:, None, :] - center[3][:, :, None]) * delta_y
    source = kappa * lax.optimization_barrier(jnp.sum(grad_w * flow, axis=-1))
    return (coef, source, den)

def push_row(center, beside_all, center_p, around_p, kappa):
    delta_x, delta_y, dist_sq, cubed = geometry(center, beside_all)
    weight = 20.0 * cubed * beside_all[4][:, None, :]
    diff = around_p.astype(jnp.float32)[:, None, :] - center_p.astype(jnp.float32)[:, :, None]
    grad_x = -lax.optimization_barrier(jnp.sum(weight * diff * delta_x, axis=-1))
    grad_y = -lax.optimization_barrier(jnp.sum(weight * diff * delta_y, axis=-1))
    alive = (center[4] > 0.0).astype(jnp.float32)
    return jnp.stack([(center[2] - kappa * grad_x) * alive, (center[3] - kappa * grad_y) * alive])

def reference(position, velocity, volume, pressure_prev, fill, drift_from):
    slots = jnp.arange(P_SIZE, dtype=jnp.int32)
    live = (slots[None, None, :] < fill[:, :, None]).astype(jnp.float32)
    held = volume * live
    top = jnp.max(jnp.abs(velocity) * live[None])
    step = cfl_number / (top + speed_eps)
    old = jnp.concatenate([position, velocity, held[None], pressure_prev[None]], axis=0)
    padded = jnp.pad(old, ((0, 0), (1, 1), (1, 1), (0, 0)))
    fresh = drift_bins(padded, drift_from + 1, step)
    ext = jnp.pad(fresh, ((0, 0), (1, 1), (1, 1), (0, 0)))
    kappa = 1.0 / P_SIZE
    row_ids = jnp.arange(GX, dtype=jnp.int32)

    def setup(row):
        center, beside_all = gather_row(ext, row, GY)
        coef, source, den = first_pass(center, beside_all, kappa)
        return (source, den)
    source, den = lax.map(setup, row_ids)
    press = fresh[5]
    for sweep in range(SWEEPS):
        rounded = press.astype(jnp.bfloat16)
        pext = jnp.pad(rounded, ((1, 1), (1, 1), (0, 0)))

        def relax(row):
            center, beside_all = gather_row(ext, row, GY)
            coef = coefficients(center, beside_all, kappa)
            center_p, around_p = gather_row(pext, row, GY)
            return jnp.einsum('yij,yj->yi', coef.astype(jnp.float32), around_p.astype(jnp.float32), precision=lax.Precision.HIGHEST)
        totals = lax.map(relax, row_ids)
        press = (source + totals) / den
    alive = (fresh[4] > 0.0).astype(jnp.float32)
    pressure = press * alive
    rounded = press.astype(jnp.bfloat16)
    pext = jnp.pad(rounded, ((1, 1), (1, 1), (0, 0)))

    def update(row):
        center, beside_all = gather_row(ext, row, GY)
        center_p, around_p = gather_row(pext, row, GY)
        return push_row(center, beside_all, center_p, around_p, kappa)
    moved = lax.map(update, row_ids)
    velocity_new = jnp.transpose(moved, (1, 0, 2, 3))
    return (pressure, velocity_new)
```

```python
import jax
import jax.numpy as jnp
import numpy as np
from jax import lax
from jax.sharding import PartitionSpec as P

SWEEPS = 4


cfl_number = 0.25
speed_eps = 1e-06
soft_sq = 0.01
shift_term = 1.0


def with_halo(shard, dims, width):
    dim_x, dim_y = dims
    size_x, size_y = lax.axis_size("gx"), lax.axis_size("gy")

    def part(dim, toward, array):
        if toward == 0:
            return array
        length = array.shape[dim]
        low = length - width if toward > 0 else 0
        return lax.slice_in_dim(array, low, low + width, axis=dim)

    def received(move_x, move_y):
        if move_x == 0 and move_y == 0:
            return shard
        pairs = [
            (x * size_y + y, (x + move_x) * size_y + y + move_y)
            for x in range(size_x)
            for y in range(size_y)
            if 0 <= x + move_x < size_x and 0 <= y + move_y < size_y
        ]
        return lax.ppermute(part(dim_y, move_y, part(dim_x, move_x, shard)), ("gx", "gy"), pairs)

    rows = [
        jnp.concatenate([received(move_x, move_y) for move_y in (1, 0, -1)], axis=dim_y)
        for move_x in (1, 0, -1)
    ]
    return jnp.concatenate(rows, axis=dim_x)


def drift_bins(extended, codes, step):
    rows = codes.shape[0]
    cols = codes.shape[1]
    result = jnp.zeros((extended.shape[0], rows, cols, extended.shape[3]), extended.dtype)
    for offset in range(9):
        shift_x = offset // 3
        shift_y = offset % 3
        source = extended[:, shift_x : shift_x + rows, shift_y : shift_y + cols, :]
        moved_x = source[0] + float(shift_x - 1) + step * source[2]
        moved_y = source[1] + float(shift_y - 1) + step * source[3]
        moved = jnp.concatenate([moved_x[None], moved_y[None], source[2:]], axis=0)
        chosen = (codes == offset + 1)[None, :, :, None]
        result = result + jnp.where(chosen, moved, 0.0)
    return result


def gather_row(extended, row, cols):
    axis_pos = extended.ndim - 3
    block = lax.dynamic_slice_in_dim(extended, row, 3, axis=axis_pos)
    center = block[..., 1, 1 : 1 + cols, :]
    pieces = [block[..., code // 3, code % 3 : code % 3 + cols, :] for code in range(9)]
    beside_all = jnp.stack(pieces, axis=-2)
    beside_all = beside_all.reshape(beside_all.shape[:-2] + (9 * beside_all.shape[-1],))
    return (center, beside_all)


def geometry(center, beside_all):
    width = center.shape[-1]
    off_x = jnp.asarray(np.repeat(np.arange(9) // 3 - 1, width).astype(np.float32))
    off_y = jnp.asarray(np.repeat(np.arange(9) % 3 - 1, width).astype(np.float32))
    delta_x = center[0][:, :, None] - (beside_all[0][:, None, :] + off_x)
    delta_y = center[1][:, :, None] - (beside_all[1][:, None, :] + off_y)
    dist_sq = delta_x * delta_x + delta_y * delta_y
    remain = jnp.maximum(1.0 - jnp.sqrt(dist_sq), 0.0)
    cubed = remain * remain * remain
    return (delta_x, delta_y, dist_sq, cubed)


def first_pass(center, beside_all, kappa):
    delta_x, delta_y, dist_sq, cubed = geometry(center, beside_all)
    lap = kappa * 40.0 * beside_all[4][:, None, :] * dist_sq * cubed / (dist_sq + soft_sq)
    coef = lap.astype(jnp.bfloat16)
    den = shift_term + jnp.sum(coef.astype(jnp.float32), axis=-1)
    grad_w = 20.0 * cubed * beside_all[4][:, None, :]
    flow = (beside_all[2][:, None, :] - center[2][:, :, None]) * delta_x + (
        beside_all[3][:, None, :] - center[3][:, :, None]
    ) * delta_y
    source = kappa * jnp.sum(grad_w * flow, axis=-1)
    return (coef, source, den)


def push_row(center, beside_all, center_p, around_p, kappa):
    delta_x, delta_y, dist_sq, cubed = geometry(center, beside_all)
    weight = 20.0 * cubed * beside_all[4][:, None, :]
    diff = around_p.astype(jnp.float32)[:, None, :] - center_p.astype(jnp.float32)[:, :, None]
    grad_x = -jnp.sum(weight * diff * delta_x, axis=-1)
    grad_y = -jnp.sum(weight * diff * delta_y, axis=-1)
    alive = (center[4] > 0.0).astype(jnp.float32)
    return jnp.stack([(center[2] - kappa * grad_x) * alive, (center[3] - kappa * grad_y) * alive])


def pressure_cycle(values):
    return with_halo(values, (0, 1), 1)


def local(position, velocity, volume, pressure_prev, fill, drift_from):
    width = position.shape[3]
    rows = position.shape[1]
    cols = position.shape[2]
    slots = jnp.arange(width, dtype=jnp.int32)
    live = (slots[None, None, :] < fill[:, :, None]).astype(jnp.float32)
    held = volume * live
    local_top = jnp.max(jnp.abs(velocity) * live[None])
    top = jnp.max(lax.all_gather(jnp.broadcast_to(local_top, (8, 128)), ("gx", "gy"), tiled=True))
    step = cfl_number / (top + speed_eps)
    old = jnp.concatenate([position, velocity, held[None], pressure_prev[None]], axis=0)
    codes = drift_from + 1
    code_channel = jnp.broadcast_to(codes.astype(jnp.float32)[None, :, :, None], (1, rows, cols, width))
    around_old = with_halo(jnp.concatenate([old, code_channel], axis=0), (1, 2), 2)
    around_codes = around_old[6, 1:-1, 1:-1, 0].astype(jnp.int32)
    ext = drift_bins(around_old[:6], around_codes, step)
    fresh_center = ext[:, 1:-1, 1:-1, :]
    kappa = 1.0 / width
    row_ids = jnp.arange(rows, dtype=jnp.int32)

    def setup(row):
        center, beside_all = gather_row(ext, row, cols)
        return first_pass(center, beside_all, kappa)

    coef_all, source, den = lax.map(setup, row_ids)
    press = fresh_center[5]
    for sweep in range(SWEEPS):
        if sweep == 0:
            pext = ext[5].astype(jnp.bfloat16)
        else:
            pext = pressure_cycle(press.astype(jnp.bfloat16))

        def relax_kept(items):
            row, coef = items
            center_p, around_p = gather_row(pext, row, cols)
            return jnp.einsum("yij,yj->yi", coef, around_p, preferred_element_type=jnp.float32)

        totals = lax.map(relax_kept, (row_ids, coef_all))
        press = (source + totals) / den
    alive = (fresh_center[4] > 0.0).astype(jnp.float32)
    pressure = press * alive
    final_ext = pressure_cycle(press.astype(jnp.bfloat16))

    def update(row):
        center, beside_all = gather_row(ext, row, cols)
        center_p, around_p = gather_row(final_ext, row, cols)
        return push_row(center, beside_all, center_p, around_p, kappa)

    moved = lax.map(update, row_ids)
    velocity_new = jnp.transpose(moved, (1, 0, 2, 3))
    return (pressure, velocity_new)


def solution(mesh):
    return jax.shard_map(
        local,
        mesh=mesh,
        in_specs=(
            P(None, "gx", "gy", None),
            P(None, "gx", "gy", None),
            P("gx", "gy", None),
            P("gx", "gy", None),
            P("gx", "gy"),
            P("gx", "gy"),
        ),
        out_specs=(P("gx", "gy", None), P(None, "gx", "gy", None)),
        check_vma=False,
    )
```

```python
import functools

import jax
import jax.numpy as jnp
from jax import lax
from jax.experimental import pallas as pl
from jax.experimental.pallas import tpu as pltpu
from jax.sharding import PartitionSpec as P

SWEEPS = 4
CFL = 0.25
SPEED_EPS = 1e-06
SOFT = 0.01
CHUNK = 32
VMEM_LIMIT = 56 * 1024 * 1024

X, Y, U, V, VOL, PRES, CODE = range(7)
S_0, S_X, S_Y, S_SOURCE, S_RDEN, S_VOL = range(6)


def call(kernel, **kwargs):
    return pl.pallas_call(
        kernel, compiler_params=pltpu.CompilerParams(vmem_limit_bytes=VMEM_LIMIT), **kwargs
    )


def row_index(width):
    return lax.broadcasted_iota(jnp.int32, (8, width), 0)


def split(value):
    high = value.astype(jnp.bfloat16).astype(jnp.float32)
    return jnp.concatenate([high, value - high], axis=0).astype(jnp.bfloat16)


def dot(left, right):
    return jnp.dot(left, right, preferred_element_type=jnp.float32)


def prepare_kernel(position, velocity, volume, pressure, fill, code, old, top):
    rows, cols, width = volume.shape
    slots = lax.broadcasted_iota(jnp.int32, (cols, width), 1)
    most = jnp.zeros((cols, width), jnp.float32)
    for row in range(rows):
        live = (slots < fill[row]).astype(jnp.float32)
        most = jnp.maximum(most, jnp.abs(velocity[0, row]) * live)
        most = jnp.maximum(most, jnp.abs(velocity[1, row]) * live)
        channels = [
            position[0, row],
            position[1, row],
            velocity[0, row],
            velocity[1, row],
            volume[row] * live,
            pressure[row],
            jnp.broadcast_to((code[row] + 1).astype(jnp.float32), (cols, width)),
            jnp.zeros((cols, width), jnp.float32),
        ]
        for channel, value in enumerate(channels):
            old[row, :, channel, :] = value
    top[...] = jnp.broadcast_to(jnp.max(most), top.shape)


def prepare(position, velocity, volume, pressure, fill, code):
    rows, cols, width = volume.shape
    return call(
        prepare_kernel,
        out_shape=(
            jax.ShapeDtypeStruct((rows, cols, 8, width), jnp.float32),
            jax.ShapeDtypeStruct((8, width), jnp.float32),
        ),
        name="prepare",
    )(position, velocity, volume, pressure, fill[:, :, None], code[:, :, None])


def neighbours(axis, low_side, high_side):
    devices = lax.axis_size(axis)
    up = [(i, i + 1) for i in range(devices - 1)]
    down = [(i + 1, i) for i in range(devices - 1)]
    return lax.ppermute(high_side, axis, up), lax.ppermute(low_side, axis, down)


def exchange(shard, depth):
    above, below = neighbours("gx", shard[:depth], shard[-depth:])
    low = jnp.concatenate([above[:, :depth], shard[:, :depth], below[:, :depth]], axis=0)
    high = jnp.concatenate([above[:, -depth:], shard[:, -depth:], below[:, -depth:]], axis=0)
    left, right = neighbours("gy", low, high)
    return above, below, left, right


def assemble(out, center, above, below, left, right, depth):
    rows, cols = center.shape[:2]
    out[:depth, depth : depth + cols] = above[...]
    out[depth : depth + rows, depth : depth + cols] = center[...]
    out[depth + rows :, depth : depth + cols] = below[...]
    out[:, :depth] = left[...]
    out[:, depth + cols :] = right[...]


def drift_kernel(top, center, above, below, left, right, fresh, old):
    rows, cols, _, width = fresh.shape
    assemble(old, center, above, below, left, right, 2)
    step = CFL / (jnp.max(top[...]) + SPEED_EPS)
    index = row_index(width)

    def one_row(row, carry):
        for col in range(cols):
            code = old[row + 1, col + 1, CODE : CODE + 1, :]
            tile = jnp.zeros((8, width), jnp.float32)
            for k in range(9):
                off_x, off_y = k // 3, k % 3
                offset = jnp.where(index == X, off_x - 1.0, jnp.where(index == Y, off_y - 1.0, 0.0))
                source = old[row + off_x, col + off_y] + offset
                tile = jnp.where(code == k + 1.0, source, tile)
            moved = tile + step * pltpu.roll(tile, 6, 0)
            fresh[row, col] = jnp.where(index <= Y, moved, tile)
        return carry

    lax.fori_loop(0, rows, one_row, 0)


def drift(top, center, above, below, left, right):
    rows, cols, _, width = center.shape
    return call(
        drift_kernel,
        out_shape=jax.ShapeDtypeStruct((rows + 2, cols + 2, 8, width), jnp.float32),
        scratch_shapes=[pltpu.VMEM((rows + 4, cols + 4, 8, width), jnp.float32)],
        name="drift",
    )(top, center, above, below, left, right)


def setup_kernel(kappa, fresh, coef, weight, sums, pv, xs, ys, feat):
    cols = coef.shape[0]
    width = coef.shape[2]
    wide = fresh.shape[1]
    row = pl.program_id(0)

    def columns(source_row):
        slot = lax.rem(source_row, 3)

        def one(col, carry):
            tile = fresh[source_row, col]
            xs[slot, col] = jnp.broadcast_to(tile[X : X + 1], (width, width)).T
            ys[slot, col] = jnp.broadcast_to(tile[Y : Y + 1], (width, width)).T
            x, y, u, v = (tile[i : i + 1] for i in range(4))
            vol = tile[VOL : VOL + 1]
            zero = jnp.zeros_like(vol)
            flow = vol * (u * x + v * y)
            base = [vol, vol * x, vol * y, vol * u, vol * v, flow, vol * tile[PRES : PRES + 1], zero]
            feat[slot, col, 0] = jnp.concatenate(base, axis=0)
            feat[slot, col, 1] = jnp.concatenate([zero, vol, zero, zero, zero, vol * u, zero, zero], axis=0)
            feat[slot, col, 2] = jnp.concatenate([zero, zero, vol, zero, zero, vol * v, zero, zero], axis=0)
            return carry

        lax.fori_loop(0, wide, one, 0)

    @pl.when(row == 0)
    def _():
        columns(0)
        columns(1)

    columns(row + 2)

    def one_bin(col, carry):
        tile = fresh[row + 1, col + 1]
        x, y, u, v = (tile[i : i + 1] for i in range(4))
        vol = tile[VOL : VOL + 1]
        total_w = jnp.zeros((16, width), jnp.float32)
        total_c = jnp.zeros((16, width), jnp.float32)
        for k in range(9):
            off_x, off_y = k // 3 - 1, k % 3 - 1
            slot = lax.rem(row + k // 3, 3)
            xi, yi = x - off_x, y - off_y
            for part in range(width // CHUNK):
                span = pl.ds(part * CHUNK, CHUNK)
                dx = xi - xs[slot, col + k % 3, span]
                dy = yi - ys[slot, col + k % 3, span]
                square = jnp.maximum(dx * dx + dy * dy, 1e-14)
                remain = jnp.maximum(1.0 - square * lax.rsqrt(square), 0.0)
                cubed = remain * remain * remain
                ratio = square * pl.reciprocal(square + SOFT, approx=True)
                place = pl.ds(k * width + part * CHUNK, CHUNK)
                weight[col, place] = cubed.astype(jnp.bfloat16)
                coef[col, place] = (cubed * ratio).astype(jnp.bfloat16)
            features = feat[slot, col + k % 3, 0]
            if off_x:
                features = features + float(off_x) * feat[slot, col + k % 3, 1]
            if off_y:
                features = features + float(off_y) * feat[slot, col + k % 3, 2]
            features = split(features)
            place = pl.ds(k * width, width)
            total_w += dot(features, weight[col, place])
            total_c += dot(features, coef[col, place])
        total_w = total_w[:8] + total_w[8:]
        total_c = total_c[:8] + total_c[8:]
        w_0, w_x, w_y, w_u, w_v, w_flow = (total_w[i : i + 1] for i in range(6))
        source = x * w_u + y * w_v - w_flow - (u * x + v * y) * w_0 + u * w_x + v * w_y
        source = kappa * 20.0 * source
        rden = 1.0 / (1.0 + kappa * 40.0 * total_c[0:1])
        first = (source + kappa * 40.0 * total_c[6:7]) * rden
        sums[col] = jnp.concatenate([w_0, w_x, w_y, source, rden, vol, first, vol], axis=0)
        pv[pl.ds(col, 1), :] = first * vol
        return carry

    lax.fori_loop(0, cols, one_bin, 0)


def setup(fresh, kappa):
    rows, cols, _, width = fresh.shape
    rows, cols = rows - 2, cols - 2
    matrix = jax.ShapeDtypeStruct((rows, cols, 9 * width, width), jnp.bfloat16)
    matrix_spec = pl.BlockSpec((None, cols, 9 * width, width), lambda row: (row, 0, 0, 0))
    return call(
        functools.partial(setup_kernel, kappa),
        grid=(rows,),
        in_specs=[pl.BlockSpec(memory_space=pltpu.VMEM)],
        out_specs=(
            matrix_spec,
            matrix_spec,
            pl.BlockSpec((None, cols, 8, width), lambda row: (row, 0, 0, 0)),
            pl.BlockSpec((None, cols, width), lambda row: (row, 0, 0)),
        ),
        out_shape=(
            matrix,
            matrix,
            jax.ShapeDtypeStruct((rows, cols, 8, width), jnp.float32),
            jax.ShapeDtypeStruct((rows, cols, width), jnp.float32),
        ),
        scratch_shapes=[
            pltpu.VMEM((3, cols + 2, width, width), jnp.float32),
            pltpu.VMEM((3, cols + 2, width, width), jnp.float32),
            pltpu.VMEM((3, cols + 2, 3, 8, width), jnp.float32),
        ],
        name="setup",
    )(fresh)


def sweep_kernel(kappa, last, center, above, below, left, right, coef, sums, pv, *rest):
    pressure = rest[0] if last else None
    ext, tiles = rest[-2:]
    row = pl.program_id(0)
    cols, _, width = coef.shape

    @pl.when(row == 0)
    def _():
        assemble(ext, center, above, below, left, right, 1)

        def one_row(r, carry):
            for col in range(cols + 2):
                value = ext[r, col : col + 1, :]
                high = value.astype(jnp.bfloat16).astype(jnp.float32)
                both = jnp.concatenate([high, value - high, jnp.zeros((14, width), jnp.float32)], axis=0)
                tiles[r, col] = both.astype(jnp.bfloat16)
            return carry

        lax.fori_loop(0, ext.shape[0], one_row, 0)

    def one_bin(col, carry):
        around = [tiles[row + k // 3, col + k % 3] for k in range(9)]
        total = dot(jnp.concatenate(around, axis=1), coef[col])
        total = total[0:1] + total[1:2]
        tile = sums[col]
        value = (tile[S_SOURCE : S_SOURCE + 1] + kappa * 40.0 * total) * tile[S_RDEN : S_RDEN + 1]
        vol = tile[S_VOL : S_VOL + 1]
        pv[pl.ds(col, 1), :] = value * vol
        if last:
            pressure[pl.ds(col, 1), :] = jnp.where(vol > 0.0, value, 0.0)
        return carry

    lax.fori_loop(0, cols, one_bin, 0)


def sweep(kappa, last, pv, halo, coef, sums):
    rows, cols, deep, width = coef.shape
    whole = pl.BlockSpec(memory_space=pltpu.VMEM)
    out = jax.ShapeDtypeStruct((rows, cols, width), jnp.float32)
    out_spec = pl.BlockSpec((None, cols, width), lambda row: (row, 0, 0))
    count = 2 if last else 1
    return call(
        functools.partial(sweep_kernel, kappa, last),
        grid=(rows,),
        in_specs=[whole] * 5
        + [
            pl.BlockSpec((None, cols, deep, width), lambda row: (row, 0, 0, 0)),
            pl.BlockSpec((None, cols, 8, width), lambda row: (row, 0, 0, 0)),
        ],
        out_specs=[out_spec] * count,
        out_shape=[out] * count,
        scratch_shapes=[
            pltpu.VMEM((rows + 2, cols + 2, width), jnp.float32),
            pltpu.VMEM((rows + 2, cols + 2, 16, width), jnp.bfloat16),
        ],
        name="sweep",
    )(pv, *halo, coef, sums)


def push_kernel(kappa, center, above, below, left, right, fresh, weight, sums, pressure, out, ext, feat):
    row = pl.program_id(0)
    cols, _, width = weight.shape

    @pl.when(row == 0)
    def _():
        assemble(ext, center, above, below, left, right, 1)

        def one_row(r, carry):
            for col in range(cols + 2):
                value = ext[r, col : col + 1, :]
                tile = fresh[r, col]
                parts = [value, value * tile[X : X + 1], value * tile[Y : Y + 1], jnp.zeros((5, width), jnp.float32)]
                feat[r, col] = jnp.concatenate(parts, axis=0)
            return carry

        lax.fori_loop(0, ext.shape[0], one_row, 0)

    index = row_index(width)

    def one_bin(col, carry):
        around = []
        for k in range(9):
            tile = feat[row + k // 3, col + k % 3]
            off_x, off_y = k // 3 - 1.0, k % 3 - 1.0
            scale = jnp.where(index == 1, off_x, jnp.where(index == 2, off_y, 0.0))
            around.append(split(tile + scale * tile[0:1]))
        total = dot(jnp.concatenate(around, axis=1), weight[col])
        total = total[:8] + total[8:]
        tile = fresh[row + 1, col + 1]
        summed = sums[col]
        x, y, u, v = (tile[i : i + 1] for i in range(4))
        alive = tile[VOL : VOL + 1] > 0.0
        own = pressure[pl.ds(col, 1), :]
        grad_x = x * total[0:1] - total[1:2] - own * (x * summed[S_0 : S_0 + 1] - summed[S_X : S_X + 1])
        grad_y = y * total[0:1] - total[2:3] - own * (y * summed[S_0 : S_0 + 1] - summed[S_Y : S_Y + 1])
        out[0, pl.ds(col, 1), :] = jnp.where(alive, u + kappa * 20.0 * grad_x, 0.0)
        out[1, pl.ds(col, 1), :] = jnp.where(alive, v + kappa * 20.0 * grad_y, 0.0)
        return carry

    lax.fori_loop(0, cols, one_bin, 0)


def push(kappa, pv, halo, fresh, weight, sums, pressure):
    rows, cols, deep, width = weight.shape
    whole = pl.BlockSpec(memory_space=pltpu.VMEM)
    return call(
        functools.partial(push_kernel, kappa),
        grid=(rows,),
        in_specs=[whole] * 6
        + [
            pl.BlockSpec((None, cols, deep, width), lambda row: (row, 0, 0, 0)),
            pl.BlockSpec((None, cols, 8, width), lambda row: (row, 0, 0, 0)),
            pl.BlockSpec((None, cols, width), lambda row: (row, 0, 0)),
        ],
        out_specs=pl.BlockSpec((2, None, cols, width), lambda row: (0, row, 0, 0)),
        out_shape=jax.ShapeDtypeStruct((2, rows, cols, width), jnp.float32),
        scratch_shapes=[
            pltpu.VMEM((rows + 2, cols + 2, width), jnp.float32),
            pltpu.VMEM((rows + 2, cols + 2, 8, width), jnp.float32),
        ],
        name="push",
    )(pv, *halo, fresh, weight, sums, pressure)


def local(position, velocity, volume, pressure_prev, fill, drift_from):
    kappa = 1.0 / volume.shape[2]
    old, top = prepare(position, velocity, volume, pressure_prev, fill, drift_from)
    top = lax.pmax(top[0, 0], ("gx", "gy")).reshape(1, 1)
    fresh = drift(top, old, *exchange(old, 2))
    coef, weight, sums, pv = setup(fresh, kappa)
    for step in range(1, SWEEPS):
        last = step == SWEEPS - 1
        pv, *pressure = sweep(kappa, last, pv, exchange(pv, 1), coef, sums)
    velocity_new = push(kappa, pv, exchange(pv, 1), fresh, weight, sums, pressure[0])
    return (pressure[0], velocity_new)


def solution(mesh):
    return jax.shard_map(
        local,
        mesh=mesh,
        in_specs=(
            P(None, "gx", "gy", None),
            P(None, "gx", "gy", None),
            P("gx", "gy", None),
            P("gx", "gy", None),
            P("gx", "gy"),
            P("gx", "gy"),
        ),
        out_specs=(P("gx", "gy", None), P(None, "gx", "gy", None)),
        check_vma=False,
    )
```

```python
import functools

import jax
import jax.numpy as jnp
from jax import lax
from jax.experimental import pallas as pl
from jax.experimental.pallas import tpu as pltpu
from jax.sharding import PartitionSpec as P

SWEEPS = 4
CFL = 0.25
SPEED_EPS = 1e-06
SOFT = 0.01
CHUNK = 32
GROUP = 4
VMEM_LIMIT = 20 * 1024 * 1024

X, Y, U, V, VOL, PRES, CODE = range(7)
S_0, S_X, S_Y, S_SOURCE, S_RDEN, S_VOL = range(6)


def call(kernel, **kwargs):
    return pl.pallas_call(
        kernel, compiler_params=pltpu.CompilerParams(vmem_limit_bytes=VMEM_LIMIT), **kwargs
    )


def row_index(width):
    return lax.broadcasted_iota(jnp.int32, (8, width), 0)


def split(value):
    high = value.astype(jnp.bfloat16).astype(jnp.float32)
    return jnp.concatenate([high, value - high], axis=0).astype(jnp.bfloat16)


def dot(left, right):
    return jnp.dot(left, right, preferred_element_type=jnp.float32)


def prepare_kernel(position, velocity, volume, pressure, fill, code, old, top):
    rows, cols, width = volume.shape
    slots = lax.broadcasted_iota(jnp.int32, (cols, width), 1)
    most = jnp.zeros((cols, width), jnp.float32)
    for row in range(rows):
        live = (slots < fill[row]).astype(jnp.float32)
        most = jnp.maximum(most, jnp.abs(velocity[0, row]) * live)
        most = jnp.maximum(most, jnp.abs(velocity[1, row]) * live)
        channels = [
            position[0, row],
            position[1, row],
            velocity[0, row],
            velocity[1, row],
            volume[row] * live,
            pressure[row],
            jnp.broadcast_to((code[row] + 1).astype(jnp.float32), (cols, width)),
            jnp.zeros((cols, width), jnp.float32),
        ]
        for channel, value in enumerate(channels):
            old[row, :, channel, :] = value
    top[...] = jnp.broadcast_to(jnp.max(most), top.shape)


def prepare(position, velocity, volume, pressure, fill, code):
    rows, cols, width = volume.shape
    return call(
        prepare_kernel,
        out_shape=(
            jax.ShapeDtypeStruct((rows, cols, 8, width), jnp.float32),
            jax.ShapeDtypeStruct((8, width), jnp.float32),
        ),
        name="prepare",
    )(position, velocity, volume, pressure, fill[:, :, None], code[:, :, None])


def neighbours(axis, low_side, high_side):
    devices = lax.axis_size(axis)
    up = [(i, i + 1) for i in range(devices - 1)]
    down = [(i + 1, i) for i in range(devices - 1)]
    return lax.ppermute(high_side, axis, up), lax.ppermute(low_side, axis, down)


def exchange(shard, depth):
    above, below = neighbours("gx", shard[:depth], shard[-depth:])
    low = jnp.concatenate([above[:, :depth], shard[:, :depth], below[:, :depth]], axis=0)
    high = jnp.concatenate([above[:, -depth:], shard[:, -depth:], below[:, -depth:]], axis=0)
    left, right = neighbours("gy", low, high)
    return above, below, left, right


def assemble(out, center, above, below, left, right, depth):
    rows, cols = center.shape[:2]
    out[:depth, depth : depth + cols] = above[...]
    out[depth : depth + rows, depth : depth + cols] = center[...]
    out[depth + rows :, depth : depth + cols] = below[...]
    out[:, :depth] = left[...]
    out[:, depth + cols :] = right[...]


def drift_kernel(top, center, above, below, left, right, fresh, old):
    rows, cols, _, width = fresh.shape
    assemble(old, center, above, below, left, right, 2)
    step = CFL / (jnp.max(top[...]) + SPEED_EPS)
    index = row_index(width)

    def one_row(row, carry):
        for col in range(cols):
            code = old[row + 1, col + 1, CODE : CODE + 1, :]
            tile = jnp.zeros((8, width), jnp.float32)
            for k in range(9):
                off_x, off_y = k // 3, k % 3
                offset = jnp.where(index == X, off_x - 1.0, jnp.where(index == Y, off_y - 1.0, 0.0))
                source = old[row + off_x, col + off_y] + offset
                tile = jnp.where(code == k + 1.0, source, tile)
            moved = tile + step * pltpu.roll(tile, 6, 0)
            fresh[row, col] = jnp.where(index <= Y, moved, tile)
        return carry

    lax.fori_loop(0, rows, one_row, 0)


def drift(top, center, above, below, left, right):
    rows, cols, _, width = center.shape
    return call(
        drift_kernel,
        out_shape=jax.ShapeDtypeStruct((rows + 2, cols + 2, 8, width), jnp.float32),
        scratch_shapes=[pltpu.VMEM((rows + 4, cols + 4, 8, width), jnp.float32)],
        name="drift",
    )(top, center, above, below, left, right)


def dot_nt(left, right):
    return lax.dot_general(left, right, (((1,), (1,)), ((), ())), preferred_element_type=jnp.float32)


def setup_kernel(kappa, fresh, coef, weight, sums, pv, xcol, ycol, feat, both_a, both_b, sem):
    rows, cols, width, deep = coef.shape
    wide = cols + 2

    def features_of(place, carry):
        row, col = place // wide, lax.rem(place, wide)
        tile = fresh[row, col]
        x, y, u, v = (tile[i : i + 1] for i in range(4))
        vol = tile[VOL : VOL + 1]
        zero = jnp.zeros_like(vol)
        vol_u, vol_v = vol * u, vol * v
        base = [vol, vol * x, vol * y, vol_u, vol_v, vol_u * x + vol_v * y, vol * tile[PRES : PRES + 1], zero]
        feat[row, col, 0] = jnp.concatenate(base, axis=0)
        feat[row, col, 1] = jnp.concatenate([zero, vol, zero, zero, zero, vol_u, zero, zero], axis=0)
        feat[row, col, 2] = jnp.concatenate([zero, zero, vol, zero, zero, vol_v, zero, zero], axis=0)
        return carry

    lax.fori_loop(0, (rows + 2) * wide, features_of, 0)

    def columns(bin_id, slot):
        tile = fresh[bin_id // cols + 1, lax.rem(bin_id, cols) + 1]
        xcol[slot] = jnp.broadcast_to(tile[X : X + 1], (width, width)).T
        ycol[slot] = jnp.broadcast_to(tile[Y : Y + 1], (width, width)).T

    def blocks(bin_id, slot, both):
        row, col = bin_id // cols, lax.rem(bin_id, cols)
        for k in range(9):
            tile = fresh[row + k // 3, col + k % 3]
            xj = tile[X : X + 1] + (k // 3 - 1.0)
            yj = tile[Y : Y + 1] + (k % 3 - 1.0)
            lanes = pl.ds(k * width, width)
            for part in range(width // CHUNK):
                span = pl.ds(part * CHUNK, CHUNK)
                dx = xcol[slot, span] - xj
                dy = ycol[slot, span] - yj
                square = jnp.maximum(dx * dx + dy * dy, 1e-14)
                remain = jnp.maximum(1.0 - square * lax.rsqrt(square), 0.0)
                cubed = remain * remain * remain
                ratio = square * pl.reciprocal(square + SOFT, approx=True)
                value = (cubed * ratio).astype(jnp.bfloat16)
                both[span, lanes] = cubed.astype(jnp.bfloat16)
                both[pl.ds(width + part * CHUNK, CHUNK), lanes] = value
                coef[row, col, span, lanes] = value

    def finish(bin_id, both):
        row, col = bin_id // cols, lax.rem(bin_id, cols)
        around = []
        for k in range(9):
            off_x, off_y = k // 3 - 1, k % 3 - 1
            features = feat[row + k // 3, col + k % 3, 0]
            if off_x:
                features = features + float(off_x) * feat[row + k // 3, col + k % 3, 1]
            if off_y:
                features = features + float(off_y) * feat[row + k // 3, col + k % 3, 2]
            around.append(split(features))
        total = dot_nt(both[...], jnp.concatenate(around, axis=1))
        total = total[:, :8] + total[:, 8:]
        total_w, total_c = total[:width].T, total[width:].T
        tile = fresh[row + 1, col + 1]
        x, y, u, v = (tile[i : i + 1] for i in range(4))
        vol = tile[VOL : VOL + 1]
        w_0, w_x, w_y, w_u, w_v, w_flow = (total_w[i : i + 1] for i in range(6))
        source = x * w_u + y * w_v - w_flow - (u * x + v * y) * w_0 + u * w_x + v * w_y
        source = kappa * 20.0 * source
        rden = 1.0 / (1.0 + kappa * 40.0 * total_c[0:1])
        first = (source + kappa * 40.0 * total_c[6:7]) * rden
        sums[row, col] = jnp.concatenate([w_0, w_x, w_y, source, rden, vol, first, vol], axis=0)
        pv[row, pl.ds(col, 1), :] = first * vol

    def copy_out(bin_id, both, slot):
        target = weight.at[bin_id // cols, lax.rem(bin_id, cols)]
        return pltpu.make_async_copy(both.at[pl.ds(0, width)], target, sem.at[slot])

    count = rows * cols
    columns(0, 0)
    columns(1, 1)

    def two_bins(step, carry):
        even = 2 * step

        @pl.when(step > 0)
        def _():
            copy_out(even - 2, both_a, 0).wait()

        blocks(even, 0, both_a)
        columns(jnp.minimum(even + 2, count - 1), 0)

        @pl.when(step > 0)
        def _():
            copy_out(even - 1, both_b, 1).wait()

        copy_out(even, both_a, 0).start()
        finish(even, both_a)
        blocks(even + 1, 1, both_b)
        columns(jnp.minimum(even + 3, count - 1), 1)
        copy_out(even + 1, both_b, 1).start()
        finish(even + 1, both_b)
        return carry

    lax.fori_loop(0, count // 2, two_bins, 0)
    copy_out(count - 2, both_a, 0).wait()
    copy_out(count - 1, both_b, 1).wait()


def setup(fresh, kappa):
    rows, cols, _, width = fresh.shape
    rows, cols = rows - 2, cols - 2
    vmem = pl.BlockSpec(memory_space=pltpu.VMEM)
    return call(
        functools.partial(setup_kernel, kappa),
        in_specs=[vmem],
        out_specs=(vmem, pl.BlockSpec(memory_space=pltpu.HBM), vmem, vmem),
        out_shape=(
            pltpu.VMEM((rows, cols, width, 9 * width), jnp.bfloat16),
            jax.ShapeDtypeStruct((rows, cols, width, 9 * width), jnp.bfloat16),
            jax.ShapeDtypeStruct((rows, cols, 8, width), jnp.float32),
            jax.ShapeDtypeStruct((rows, cols, width), jnp.float32),
        ),
        scratch_shapes=[
            pltpu.VMEM((2, width, width), jnp.float32),
            pltpu.VMEM((2, width, width), jnp.float32),
            pltpu.VMEM((rows + 2, cols + 2, 3, 8, width), jnp.float32),
            pltpu.VMEM((2 * width, 9 * width), jnp.bfloat16),
            pltpu.VMEM((2 * width, 9 * width), jnp.bfloat16),
            pltpu.SemaphoreType.DMA((2,)),
        ],
        name="setup",
    )(fresh)


def sweep_kernel(kappa, last, center, above, below, left, right, coef, sums, pv, *rest):
    pressure = rest[0] if last else None
    ext, tiles = rest[-2:]
    rows, cols, width, _ = coef.shape
    assemble(ext, center, above, below, left, right, 1)

    def spread(row, carry):
        for col in range(cols + 2):
            tiles[row, col] = jnp.broadcast_to(ext[row, col : col + 1, :], (16, width)).astype(jnp.bfloat16)
        return carry

    lax.fori_loop(0, rows + 2, spread, 0)
    ones = jnp.ones((16, width), jnp.bfloat16)

    def some_bins(step, carry):
        row, first = step // (cols // GROUP), lax.rem(step, cols // GROUP) * GROUP
        for col in range(GROUP):
            col = first + col
            parts = []
            for part in range(width // 16):
                total = None
                for k in range(9):
                    term = coef[row, col, pl.ds(part * 16, 16), pl.ds(k * width, width)] * tiles[row + k // 3, col + k % 3]
                    total = term if total is None else total + term
                parts.append(total)
            total = dot_nt(ones, jnp.concatenate(parts, axis=0))[0:1]
            tile = sums[row, col]
            value = (tile[S_SOURCE : S_SOURCE + 1] + kappa * 40.0 * total) * tile[S_RDEN : S_RDEN + 1]
            vol = tile[S_VOL : S_VOL + 1]
            pv[row, pl.ds(col, 1), :] = value * vol
            if last:
                pressure[row, pl.ds(col, 1), :] = jnp.where(vol > 0.0, value, 0.0)
        return carry

    lax.fori_loop(0, rows * cols // GROUP, some_bins, 0)


def sweep(kappa, last, pv, halo, coef, sums):
    rows, cols, width, _ = coef.shape
    vmem = pl.BlockSpec(memory_space=pltpu.VMEM)
    out = jax.ShapeDtypeStruct((rows, cols, width), jnp.float32)
    count = 2 if last else 1
    return call(
        functools.partial(sweep_kernel, kappa, last),
        in_specs=[vmem] * 7,
        out_specs=[vmem] * count,
        out_shape=[out] * count,
        scratch_shapes=[
            pltpu.VMEM((rows + 2, cols + 2, width), jnp.float32),
            pltpu.VMEM((rows + 2, cols + 2, 16, width), jnp.bfloat16),
        ],
        name="sweep",
    )(pv, *halo, pltpu.with_memory_space_constraint(coef, pltpu.VMEM), sums)


def push_kernel(kappa, center, above, below, left, right, fresh, weight, sums, pressure, out, ext, feat):
    row, half = pl.program_id(0), pl.program_id(1)
    cols, width, _ = weight.shape

    @pl.when((row == 0) & (half == 0))
    def _():
        assemble(ext, center, above, below, left, right, 1)

        def one_row(r, carry):
            for col in range(ext.shape[1]):
                value = ext[r, col : col + 1, :]
                tile = fresh[r, col]
                parts = [value, value * tile[X : X + 1], value * tile[Y : Y + 1], jnp.zeros((5, width), jnp.float32)]
                feat[r, col] = jnp.concatenate(parts, axis=0)
            return carry

        lax.fori_loop(0, ext.shape[0], one_row, 0)

    index = row_index(width)

    def some_bins(step, carry):
        for col in range(4):
            col = step * 4 + col
            place = half * cols + col
            around = []
            for k in range(9):
                tile = feat[row + k // 3, place + k % 3]
                off_x, off_y = k // 3 - 1.0, k % 3 - 1.0
                scale = jnp.where(index == 1, off_x, jnp.where(index == 2, off_y, 0.0))
                around.append(split(tile + scale * tile[0:1]))
            total = dot_nt(weight[col], jnp.concatenate(around, axis=1))
            total = (total[:, :8] + total[:, 8:]).T
            tile = fresh[row + 1, place + 1]
            summed = sums[col]
            x, y, u, v = (tile[i : i + 1] for i in range(4))
            alive = tile[VOL : VOL + 1] > 0.0
            own = pressure[pl.ds(col, 1), :]
            grad_x = x * total[0:1] - total[1:2] - own * (x * summed[S_0 : S_0 + 1] - summed[S_X : S_X + 1])
            grad_y = y * total[0:1] - total[2:3] - own * (y * summed[S_0 : S_0 + 1] - summed[S_Y : S_Y + 1])
            out[0, pl.ds(col, 1), :] = jnp.where(alive, u + kappa * 20.0 * grad_x, 0.0)
            out[1, pl.ds(col, 1), :] = jnp.where(alive, v + kappa * 20.0 * grad_y, 0.0)
        return carry

    lax.fori_loop(0, cols // 4, some_bins, 0)


def push(kappa, pv, halo, fresh, weight, sums, pressure):
    rows, cols, width, deep = weight.shape
    half = cols // 2
    whole = pl.BlockSpec(memory_space=pltpu.VMEM)
    return call(
        functools.partial(push_kernel, kappa),
        grid=(rows, 2),
        in_specs=[whole] * 6
        + [
            pl.BlockSpec((None, half, width, deep), lambda row, part: (row, part, 0, 0)),
            pl.BlockSpec((None, half, 8, width), lambda row, part: (row, part, 0, 0)),
            pl.BlockSpec((None, half, width), lambda row, part: (row, part, 0)),
        ],
        out_specs=pl.BlockSpec((2, None, half, width), lambda row, part: (0, row, part, 0)),
        out_shape=jax.ShapeDtypeStruct((2, rows, cols, width), jnp.float32),
        scratch_shapes=[
            pltpu.VMEM((rows + 2, cols + 2, width), jnp.float32),
            pltpu.VMEM((rows + 2, cols + 2, 8, width), jnp.float32),
        ],
        name="push",
    )(pv, *halo, fresh, weight, sums, pressure)


def local(position, velocity, volume, pressure_prev, fill, drift_from):
    kappa = 1.0 / volume.shape[2]
    old, top = prepare(position, velocity, volume, pressure_prev, fill, drift_from)
    top = lax.pmax(top[0, 0], ("gx", "gy")).reshape(1, 1)
    fresh = drift(top, old, *exchange(old, 2))
    coef, weight, sums, pv = setup(fresh, kappa)
    for step in range(1, SWEEPS):
        last = step == SWEEPS - 1
        pv, *pressure = sweep(kappa, last, pv, exchange(pv, 1), coef, sums)
    velocity_new = push(kappa, pv, exchange(pv, 1), fresh, weight, sums, pressure[0])
    return (pressure[0], velocity_new)


def solution(mesh):
    return jax.shard_map(
        local,
        mesh=mesh,
        in_specs=(
            P(None, "gx", "gy", None),
            P(None, "gx", "gy", None),
            P("gx", "gy", None),
            P("gx", "gy", None),
            P("gx", "gy"),
            P("gx", "gy"),
        ),
        out_specs=(P("gx", "gy", None), P(None, "gx", "gy", None)),
        check_vma=False,
    )
```

```python
import functools

import jax
import jax.numpy as jnp
from jax import lax
from jax.experimental import pallas as pl
from jax.experimental.pallas import tpu as pltpu
from jax.sharding import PartitionSpec as P

SWEEPS = 4
CFL = 0.25
SPEED_EPS = 1e-06
SOFT = 0.01
CHUNK = 32
GROUP = 4
VMEM_LIMIT = 20 * 1024 * 1024

X, Y, U, V, VOL, PRES, CODE = range(7)
S_0, S_X, S_Y, S_SOURCE, S_RDEN, S_VOL = range(6)


def call(kernel, **kwargs):
    return pl.pallas_call(
        kernel, compiler_params=pltpu.CompilerParams(vmem_limit_bytes=VMEM_LIMIT), **kwargs
    )


def row_index(width):
    return lax.broadcasted_iota(jnp.int32, (8, width), 0)


def split(value):
    high = value.astype(jnp.bfloat16).astype(jnp.float32)
    return jnp.concatenate([high, value - high], axis=0).astype(jnp.bfloat16)


def dot(left, right):
    return jnp.dot(left, right, preferred_element_type=jnp.float32)


def prepare_kernel(position, velocity, volume, pressure, fill, code, old, top):
    rows, cols, width = volume.shape
    slots = lax.broadcasted_iota(jnp.int32, (cols, width), 1)
    most = jnp.zeros((cols, width), jnp.float32)
    for row in range(rows):
        live = (slots < fill[row]).astype(jnp.float32)
        most = jnp.maximum(most, jnp.abs(velocity[0, row]) * live)
        most = jnp.maximum(most, jnp.abs(velocity[1, row]) * live)
        channels = [
            position[0, row],
            position[1, row],
            velocity[0, row],
            velocity[1, row],
            volume[row] * live,
            pressure[row],
            jnp.broadcast_to((code[row] + 1).astype(jnp.float32), (cols, width)),
            jnp.zeros((cols, width), jnp.float32),
        ]
        for channel, value in enumerate(channels):
            old[row, :, channel, :] = value
    top[...] = jnp.broadcast_to(jnp.max(most), top.shape)


def prepare(position, velocity, volume, pressure, fill, code):
    rows, cols, width = volume.shape
    return call(
        prepare_kernel,
        out_shape=(
            jax.ShapeDtypeStruct((rows, cols, 8, width), jnp.float32),
            jax.ShapeDtypeStruct((8, width), jnp.float32),
        ),
        name="prepare",
    )(position, velocity, volume, pressure, fill[:, :, None], code[:, :, None])


def neighbours(axis, low_side, high_side):
    devices = lax.axis_size(axis)
    up = [(i, i + 1) for i in range(devices - 1)]
    down = [(i + 1, i) for i in range(devices - 1)]
    return lax.ppermute(high_side, axis, up), lax.ppermute(low_side, axis, down)


def exchange(shard, depth):
    above, below = neighbours("gx", shard[:depth], shard[-depth:])
    low = jnp.concatenate([above[:, :depth], shard[:, :depth], below[:, :depth]], axis=0)
    high = jnp.concatenate([above[:, -depth:], shard[:, -depth:], below[:, -depth:]], axis=0)
    left, right = neighbours("gy", low, high)
    return above, below, left, right


def assemble(out, center, above, below, left, right, depth):
    rows, cols = center.shape[:2]
    out[:depth, depth : depth + cols] = above[...]
    out[depth : depth + rows, depth : depth + cols] = center[...]
    out[depth + rows :, depth : depth + cols] = below[...]
    out[:, :depth] = left[...]
    out[:, depth + cols :] = right[...]


def drift_kernel(top, center, above, below, left, right, fresh, old):
    rows, cols, _, width = fresh.shape
    assemble(old, center, above, below, left, right, 2)
    step = CFL / (jnp.max(top[...]) + SPEED_EPS)
    index = row_index(width)

    def one_row(row, carry):
        for col in range(cols):
            code = old[row + 1, col + 1, CODE : CODE + 1, :]
            tile = jnp.zeros((8, width), jnp.float32)
            for k in range(9):
                off_x, off_y = k // 3, k % 3
                offset = jnp.where(index == X, off_x - 1.0, jnp.where(index == Y, off_y - 1.0, 0.0))
                source = old[row + off_x, col + off_y] + offset
                tile = jnp.where(code == k + 1.0, source, tile)
            moved = tile + step * pltpu.roll(tile, 6, 0)
            fresh[row, col] = jnp.where(index <= Y, moved, tile)
        return carry

    lax.fori_loop(0, rows, one_row, 0)


def drift(top, center, above, below, left, right):
    rows, cols, _, width = center.shape
    return call(
        drift_kernel,
        out_shape=jax.ShapeDtypeStruct((rows + 2, cols + 2, 8, width), jnp.float32),
        scratch_shapes=[pltpu.VMEM((rows + 4, cols + 4, 8, width), jnp.float32)],
        name="drift",
    )(top, center, above, below, left, right)


def dot_nt(left, right):
    return lax.dot_general(left, right, (((1,), (1,)), ((), ())), preferred_element_type=jnp.float32)


def setup_kernel(kappa, fresh, coef, weight, sums, pv, xcol, ycol, feat, both_a, both_b, sem):
    rows, cols, width, deep = coef.shape
    wide = cols + 2

    def features_of(place, carry):
        row, col = place // wide, lax.rem(place, wide)
        tile = fresh[row, col]
        x, y, u, v = (tile[i : i + 1] for i in range(4))
        vol = tile[VOL : VOL + 1]
        zero = jnp.zeros_like(vol)
        vol_u, vol_v = vol * u, vol * v
        base = [vol, vol * x, vol * y, vol_u, vol_v, vol_u * x + vol_v * y, vol * tile[PRES : PRES + 1], zero]
        feat[row, col, 0] = jnp.concatenate(base, axis=0)
        feat[row, col, 1] = jnp.concatenate([zero, vol, zero, zero, zero, vol_u, zero, zero], axis=0)
        feat[row, col, 2] = jnp.concatenate([zero, zero, vol, zero, zero, vol_v, zero, zero], axis=0)
        return carry

    lax.fori_loop(0, (rows + 2) * wide, features_of, 0)

    def columns(bin_id, slot):
        tile = fresh[bin_id // cols + 1, lax.rem(bin_id, cols) + 1]
        xcol[slot] = jnp.broadcast_to(tile[X : X + 1], (width, width)).T
        ycol[slot] = jnp.broadcast_to(tile[Y : Y + 1], (width, width)).T

    def blocks(bin_id, slot, both):
        row, col = bin_id // cols, lax.rem(bin_id, cols)
        for k in range(9):
            tile = fresh[row + k // 3, col + k % 3]
            xj = tile[X : X + 1] + (k // 3 - 1.0)
            yj = tile[Y : Y + 1] + (k % 3 - 1.0)
            lanes = pl.ds(k * width, width)
            for part in range(width // CHUNK):
                span = pl.ds(part * CHUNK, CHUNK)
                dx = xcol[slot, span] - xj
                dy = ycol[slot, span] - yj
                square = jnp.maximum(dx * dx + dy * dy, 1e-14)
                remain = jnp.maximum(1.0 - square * lax.rsqrt(square), 0.0)
                cubed = remain * remain * remain
                ratio = square * pl.reciprocal(square + SOFT, approx=True)
                value = (cubed * ratio).astype(jnp.bfloat16)
                both[span, lanes] = cubed.astype(jnp.bfloat16)
                both[pl.ds(width + part * CHUNK, CHUNK), lanes] = value
                coef[row, col, span, lanes] = value

    def finish(bin_id, both):
        row, col = bin_id // cols, lax.rem(bin_id, cols)
        around = []
        for k in range(9):
            off_x, off_y = k // 3 - 1, k % 3 - 1
            features = feat[row + k // 3, col + k % 3, 0]
            if off_x:
                features = features + float(off_x) * feat[row + k // 3, col + k % 3, 1]
            if off_y:
                features = features + float(off_y) * feat[row + k // 3, col + k % 3, 2]
            around.append(split(features))
        total = dot_nt(both[...], jnp.concatenate(around, axis=1))
        total = total[:, :8] + total[:, 8:]
        total_w, total_c = total[:width].T, total[width:].T
        tile = fresh[row + 1, col + 1]
        x, y, u, v = (tile[i : i + 1] for i in range(4))
        vol = tile[VOL : VOL + 1]
        w_0, w_x, w_y, w_u, w_v, w_flow = (total_w[i : i + 1] for i in range(6))
        source = x * w_u + y * w_v - w_flow - (u * x + v * y) * w_0 + u * w_x + v * w_y
        source = kappa * 20.0 * source
        rden = 1.0 / (1.0 + kappa * 40.0 * total_c[0:1])
        first = (source + kappa * 40.0 * total_c[6:7]) * rden
        sums[row, col] = jnp.concatenate([w_0, w_x, w_y, source, rden, vol, first, vol], axis=0)
        pv[row, pl.ds(col, 1), :] = first * vol

    def copy_out(bin_id, both, slot):
        target = weight.at[bin_id // cols, lax.rem(bin_id, cols)]
        return pltpu.make_async_copy(both.at[pl.ds(0, width)], target, sem.at[slot])

    count = rows * cols
    columns(0, 0)
    columns(1, 1)

    def two_bins(step, carry):
        even = 2 * step

        @pl.when(step > 0)
        def _():
            copy_out(even - 2, both_a, 0).wait()

        blocks(even, 0, both_a)
        columns(jnp.minimum(even + 2, count - 1), 0)

        @pl.when(step > 0)
        def _():
            copy_out(even - 1, both_b, 1).wait()

        copy_out(even, both_a, 0).start()
        finish(even, both_a)
        blocks(even + 1, 1, both_b)
        columns(jnp.minimum(even + 3, count - 1), 1)
        copy_out(even + 1, both_b, 1).start()
        finish(even + 1, both_b)
        return carry

    lax.fori_loop(0, count // 2, two_bins, 0)
    copy_out(count - 2, both_a, 0).wait()
    copy_out(count - 1, both_b, 1).wait()


def setup(fresh, kappa):
    rows, cols, _, width = fresh.shape
    rows, cols = rows - 2, cols - 2
    vmem = pl.BlockSpec(memory_space=pltpu.VMEM)
    return call(
        functools.partial(setup_kernel, kappa),
        in_specs=[vmem],
        out_specs=(vmem, pl.BlockSpec(memory_space=pltpu.HBM), vmem, vmem),
        out_shape=(
            pltpu.VMEM((rows, cols, width, 9 * width), jnp.bfloat16),
            jax.ShapeDtypeStruct((rows, cols, width, 9 * width), jnp.bfloat16),
            jax.ShapeDtypeStruct((rows, cols, 8, width), jnp.float32),
            jax.ShapeDtypeStruct((rows, cols, width), jnp.float32),
        ),
        scratch_shapes=[
            pltpu.VMEM((2, width, width), jnp.float32),
            pltpu.VMEM((2, width, width), jnp.float32),
            pltpu.VMEM((rows + 2, cols + 2, 3, 8, width), jnp.float32),
            pltpu.VMEM((2 * width, 9 * width), jnp.bfloat16),
            pltpu.VMEM((2 * width, 9 * width), jnp.bfloat16),
            pltpu.SemaphoreType.DMA((2,)),
        ],
        name="setup",
    )(fresh)


def sweep_kernel(kappa, last, center, above, below, left, right, coef, sums, pv, *rest):
    pressure = rest[0] if last else None
    ext, tiles = rest[-2:]
    rows, cols, width, _ = coef.shape
    assemble(ext, center, above, below, left, right, 1)

    def spread(row, carry):
        for col in range(cols + 2):
            tiles[row, col] = jnp.broadcast_to(ext[row, col : col + 1, :], (16, width)).astype(jnp.bfloat16)
        return carry

    lax.fori_loop(0, rows + 2, spread, 0)
    ones = jnp.ones((16, width), jnp.bfloat16)

    def some_bins(step, carry):
        row, first = step // (cols // GROUP), lax.rem(step, cols // GROUP) * GROUP
        for col in range(GROUP):
            col = first + col
            around = [tiles[row + k // 3, col + k % 3] for k in range(9)]
            parts = []
            for part in range(width // 16):
                total = None
                for k in range(9):
                    term = coef[row, col, pl.ds(part * 16, 16), pl.ds(k * width, width)] * around[k]
                    total = term if total is None else total + term
                parts.append(total)
            total = dot_nt(ones, jnp.concatenate(parts, axis=0))[0:1]
            tile = sums[row, col]
            value = (tile[S_SOURCE : S_SOURCE + 1] + kappa * 40.0 * total) * tile[S_RDEN : S_RDEN + 1]
            vol = tile[S_VOL : S_VOL + 1]
            pv[row, pl.ds(col, 1), :] = value * vol
            if last:
                pressure[row, pl.ds(col, 1), :] = jnp.where(vol > 0.0, value, 0.0)
        return carry

    lax.fori_loop(0, rows * cols // GROUP, some_bins, 0)


def sweep(kappa, last, pv, halo, coef, sums):
    rows, cols, width, _ = coef.shape
    vmem = pl.BlockSpec(memory_space=pltpu.VMEM)
    out = jax.ShapeDtypeStruct((rows, cols, width), jnp.float32)
    count = 2 if last else 1
    return call(
        functools.partial(sweep_kernel, kappa, last),
        in_specs=[vmem] * 7,
        out_specs=[vmem] * count,
        out_shape=[out] * count,
        scratch_shapes=[
            pltpu.VMEM((rows + 2, cols + 2, width), jnp.float32),
            pltpu.VMEM((rows + 2, cols + 2, 16, width), jnp.bfloat16),
        ],
        name="sweep",
    )(pv, *halo, pltpu.with_memory_space_constraint(coef, pltpu.VMEM), sums)


def push_kernel(kappa, center, above, below, left, right, fresh, weight, sums, pressure, out, ext, feat):
    row, half = pl.program_id(0), pl.program_id(1)
    cols, width, _ = weight.shape

    @pl.when((row == 0) & (half == 0))
    def _():
        assemble(ext, center, above, below, left, right, 1)

        def one_row(r, carry):
            for col in range(ext.shape[1]):
                value = ext[r, col : col + 1, :]
                tile = fresh[r, col]
                parts = [value, value * tile[X : X + 1], value * tile[Y : Y + 1], jnp.zeros((5, width), jnp.float32)]
                feat[r, col] = jnp.concatenate(parts, axis=0)
            return carry

        lax.fori_loop(0, ext.shape[0], one_row, 0)

    index = row_index(width)

    def some_bins(step, carry):
        for col in range(4):
            col = step * 4 + col
            place = half * cols + col
            around = []
            for k in range(9):
                tile = feat[row + k // 3, place + k % 3]
                off_x, off_y = k // 3 - 1.0, k % 3 - 1.0
                scale = jnp.where(index == 1, off_x, jnp.where(index == 2, off_y, 0.0))
                around.append(split(tile + scale * tile[0:1]))
            total = dot_nt(weight[col], jnp.concatenate(around, axis=1))
            total = (total[:, :8] + total[:, 8:]).T
            tile = fresh[row + 1, place + 1]
            summed = sums[col]
            x, y, u, v = (tile[i : i + 1] for i in range(4))
            alive = tile[VOL : VOL + 1] > 0.0
            own = pressure[pl.ds(col, 1), :]
            grad_x = x * total[0:1] - total[1:2] - own * (x * summed[S_0 : S_0 + 1] - summed[S_X : S_X + 1])
            grad_y = y * total[0:1] - total[2:3] - own * (y * summed[S_0 : S_0 + 1] - summed[S_Y : S_Y + 1])
            out[0, pl.ds(col, 1), :] = jnp.where(alive, u + kappa * 20.0 * grad_x, 0.0)
            out[1, pl.ds(col, 1), :] = jnp.where(alive, v + kappa * 20.0 * grad_y, 0.0)
        return carry

    lax.fori_loop(0, cols // 4, some_bins, 0)


def push(kappa, pv, halo, fresh, weight, sums, pressure):
    rows, cols, width, deep = weight.shape
    half = cols // 2
    whole = pl.BlockSpec(memory_space=pltpu.VMEM)
    return call(
        functools.partial(push_kernel, kappa),
        grid=(rows, 2),
        in_specs=[whole] * 6
        + [
            pl.BlockSpec((None, half, width, deep), lambda row, part: (row, part, 0, 0)),
            pl.BlockSpec((None, half, 8, width), lambda row, part: (row, part, 0, 0)),
            pl.BlockSpec((None, half, width), lambda row, part: (row, part, 0)),
        ],
        out_specs=pl.BlockSpec((2, None, half, width), lambda row, part: (0, row, part, 0)),
        out_shape=jax.ShapeDtypeStruct((2, rows, cols, width), jnp.float32),
        scratch_shapes=[
            pltpu.VMEM((rows + 2, cols + 2, width), jnp.float32),
            pltpu.VMEM((rows + 2, cols + 2, 8, width), jnp.float32),
        ],
        name="push",
    )(pv, *halo, fresh, weight, sums, pressure)


def local(position, velocity, volume, pressure_prev, fill, drift_from):
    kappa = 1.0 / volume.shape[2]
    old, top = prepare(position, velocity, volume, pressure_prev, fill, drift_from)
    top = lax.all_gather(top, ("gx", "gy"), tiled=True)
    fresh = drift(top, old, *exchange(old, 2))
    coef, weight, sums, pv = setup(fresh, kappa)
    for step in range(1, SWEEPS):
        last = step == SWEEPS - 1
        pv, *pressure = sweep(kappa, last, pv, exchange(pv, 1), coef, sums)
    velocity_new = push(kappa, pv, exchange(pv, 1), fresh, weight, sums, pressure[0])
    return (pressure[0], velocity_new)


def solution(mesh):
    return jax.shard_map(
        local,
        mesh=mesh,
        in_specs=(
            P(None, "gx", "gy", None),
            P(None, "gx", "gy", None),
            P("gx", "gy", None),
            P("gx", "gy", None),
            P("gx", "gy"),
            P("gx", "gy"),
        ),
        out_specs=(P("gx", "gy", None), P(None, "gx", "gy", None)),
        check_vma=False,
    )
```

```python
import functools

import jax
import jax.numpy as jnp
from jax import lax
from jax.experimental import pallas as pl
from jax.experimental.pallas import tpu as pltpu
from jax.sharding import PartitionSpec as P

SWEEPS = 4
CFL = 0.25
SPEED_EPS = 1e-06
SOFT = 0.01
CHUNK = 32
VMEM_LIMIT = 20 * 1024 * 1024

X, Y, U, V, VOL, PRES, CODE = range(7)


def call(kernel, **kwargs):
    return pl.pallas_call(
        kernel, compiler_params=pltpu.CompilerParams(vmem_limit_bytes=VMEM_LIMIT), **kwargs
    )


def row_index(width):
    return lax.broadcasted_iota(jnp.int32, (8, width), 0)


def split(value):
    high = value.astype(jnp.bfloat16).astype(jnp.float32)
    return jnp.concatenate([high, value - high], axis=0).astype(jnp.bfloat16)


def dot(left, right):
    return jnp.dot(left, right, preferred_element_type=jnp.float32)


def prepare_kernel(position, velocity, volume, pressure, fill, code, old, top):
    rows, cols, width = volume.shape
    slots = lax.broadcasted_iota(jnp.int32, (cols, width), 1)
    most = jnp.zeros((cols, width), jnp.float32)
    for row in range(rows):
        live = (slots < fill[row]).astype(jnp.float32)
        most = jnp.maximum(most, jnp.abs(velocity[0, row]) * live)
        most = jnp.maximum(most, jnp.abs(velocity[1, row]) * live)
        channels = [
            position[0, row],
            position[1, row],
            velocity[0, row],
            velocity[1, row],
            volume[row] * live,
            pressure[row],
            jnp.broadcast_to((code[row] + 1).astype(jnp.float32), (cols, width)),
            jnp.zeros((cols, width), jnp.float32),
        ]
        for channel, value in enumerate(channels):
            old[row, :, channel, :] = value
    top[...] = jnp.broadcast_to(jnp.max(most), top.shape)


def prepare(position, velocity, volume, pressure, fill, code):
    rows, cols, width = volume.shape
    return call(
        prepare_kernel,
        out_shape=(
            jax.ShapeDtypeStruct((rows, cols, 8, width), jnp.float32),
            jax.ShapeDtypeStruct((8, width), jnp.float32),
        ),
        name="prepare",
    )(position, velocity, volume, pressure, fill[:, :, None], code[:, :, None])


def neighbours(axis, low_side, high_side):
    devices = lax.axis_size(axis)
    up = [(i, i + 1) for i in range(devices - 1)]
    down = [(i + 1, i) for i in range(devices - 1)]
    return lax.ppermute(high_side, axis, up), lax.ppermute(low_side, axis, down)


def exchange(shard, depth):
    above, below = neighbours("gx", shard[:depth], shard[-depth:])
    low = jnp.concatenate([above[:, :depth], shard[:, :depth], below[:, :depth]], axis=0)
    high = jnp.concatenate([above[:, -depth:], shard[:, -depth:], below[:, -depth:]], axis=0)
    left, right = neighbours("gy", low, high)
    return above, below, left, right


def largest(value):
    for axis in ("gy", "gx"):
        devices = lax.axis_size(axis)
        if devices & (devices - 1):
            value = lax.pmax(value, axis)
            continue
        for bit in range(devices.bit_length() - 1):
            pairs = [(i, i ^ (1 << bit)) for i in range(devices)]
            value = jnp.maximum(value, lax.ppermute(value, axis, pairs))
    return value


def assemble(out, center, above, below, left, right, depth):
    rows, cols = center.shape[:2]
    out[:depth, depth : depth + cols] = above[...]
    out[depth : depth + rows, depth : depth + cols] = center[...]
    out[depth + rows :, depth : depth + cols] = below[...]
    out[:, :depth] = left[...]
    out[:, depth + cols :] = right[...]


def drift_kernel(top, center, above, below, left, right, fresh, old):
    rows, cols, _, width = fresh.shape
    assemble(old, center, above, below, left, right, 2)
    step = CFL / (jnp.max(top[...]) + SPEED_EPS)
    index = row_index(width)

    def one_row(row, carry):
        for col in range(cols):
            code = old[row + 1, col + 1, CODE : CODE + 1, :]
            tile = jnp.zeros((8, width), jnp.float32)
            for k in range(9):
                off_x, off_y = k // 3, k % 3
                offset = jnp.where(index == X, off_x - 1.0, jnp.where(index == Y, off_y - 1.0, 0.0))
                source = old[row + off_x, col + off_y] + offset
                tile = jnp.where(code == k + 1.0, source, tile)
            moved = tile + step * pltpu.roll(tile, 6, 0)
            fresh[row, col] = jnp.where(index <= Y, moved, tile)
        return carry

    lax.fori_loop(0, rows, one_row, 0)


def drift(top, center, above, below, left, right):
    rows, cols, _, width = center.shape
    return call(
        drift_kernel,
        out_shape=jax.ShapeDtypeStruct((rows + 2, cols + 2, 8, width), jnp.float32),
        scratch_shapes=[pltpu.VMEM((rows + 4, cols + 4, 8, width), jnp.float32)],
        name="drift",
    )(top, center, above, below, left, right)


def dot_nt(left, right):
    return lax.dot_general(left, right, (((1,), (1,)), ((), ())), preferred_element_type=jnp.float32)


def setup_kernel(kappa, fresh, coef, weight, sums, pv, xcol, ycol, feat, both_a, both_b, sem):
    rows, cols, width, deep = coef.shape
    wide = cols + 2

    def features_of(place, carry):
        row, col = place // wide, lax.rem(place, wide)
        tile = fresh[row, col]
        x, y, u, v = (tile[i : i + 1] for i in range(4))
        vol = tile[VOL : VOL + 1]
        zero = jnp.zeros_like(vol)
        vol_u, vol_v = vol * u, vol * v
        base = [vol, vol * x, vol * y, vol_u, vol_v, vol_u * x + vol_v * y, vol * tile[PRES : PRES + 1], zero]
        feat[row, col, 0] = jnp.concatenate(base, axis=0)
        feat[row, col, 1] = jnp.concatenate([zero, vol, zero, zero, zero, vol_u, zero, zero], axis=0)
        feat[row, col, 2] = jnp.concatenate([zero, zero, vol, zero, zero, vol_v, zero, zero], axis=0)
        return carry

    lax.fori_loop(0, (rows + 2) * wide, features_of, 0)

    def columns(bin_id, slot):
        tile = fresh[bin_id // cols + 1, lax.rem(bin_id, cols) + 1]
        xcol[slot] = jnp.broadcast_to(tile[X : X + 1], (width, width)).T
        ycol[slot] = jnp.broadcast_to(tile[Y : Y + 1], (width, width)).T

    def blocks(bin_id, slot, both):
        row, col = bin_id // cols, lax.rem(bin_id, cols)
        around = [fresh[row + k // 3, col + k % 3] for k in range(9)]
        xj = [jnp.broadcast_to(around[k][X : X + 1] + (k // 3 - 1.0), (8, width)) for k in range(9)]
        yj = [jnp.broadcast_to(around[k][Y : Y + 1] + (k % 3 - 1.0), (8, width)) for k in range(9)]
        for part in range(width // CHUNK):
            spans = [pl.ds(part * CHUNK + 8 * i, 8) for i in range(CHUNK // 8)]
            xi = [xcol[slot, span] for span in spans]
            yi = [ycol[slot, span] for span in spans]
            for k in range(9):
                lanes = pl.ds(k * width, width)
                weights, values = [], []
                for x, y in zip(xi, yi):
                    dx = x - xj[k]
                    dy = y - yj[k]
                    square = jnp.maximum(dx * dx + dy * dy, 1e-14)
                    remain = jnp.maximum(1.0 - square * lax.rsqrt(square), 0.0)
                    cubed = remain * remain * remain
                    weights.append(cubed)
                    values.append(cubed * (square * pltpu.reciprocal(square + SOFT, approx=True)))
                weights = jnp.concatenate(weights, axis=0).astype(jnp.bfloat16)
                values = jnp.concatenate(values, axis=0).astype(jnp.bfloat16)
                both[pl.ds(part * CHUNK, CHUNK), lanes] = weights
                both[pl.ds(width + part * CHUNK, CHUNK), lanes] = values
                coef[row, col, pl.ds(part * CHUNK, CHUNK), lanes] = values

    def finish(bin_id, both):
        row, col = bin_id // cols, lax.rem(bin_id, cols)
        around = []
        for k in range(9):
            off_x, off_y = k // 3 - 1, k % 3 - 1
            features = feat[row + k // 3, col + k % 3, 0]
            if off_x:
                features = features + float(off_x) * feat[row + k // 3, col + k % 3, 1]
            if off_y:
                features = features + float(off_y) * feat[row + k // 3, col + k % 3, 2]
            around.append(split(features))
        total = dot_nt(both[...], jnp.concatenate(around, axis=1))
        total = total[:, :8] + total[:, 8:]
        total_w, total_c = total[:width].T, total[width:].T
        tile = fresh[row + 1, col + 1]
        x, y, u, v = (tile[i : i + 1] for i in range(4))
        vol = tile[VOL : VOL + 1]
        w_0, w_x, w_y, w_u, w_v, w_flow = (total_w[i : i + 1] for i in range(6))
        source = x * w_u + y * w_v - w_flow - (u * x + v * y) * w_0 + u * w_x + v * w_y
        source = kappa * 20.0 * source
        rden = 1.0 / (1.0 + kappa * 40.0 * total_c[0:1])
        first = (source + kappa * 40.0 * total_c[6:7]) * rden
        for place, value in enumerate((source, rden, vol)):
            sums[place, row, pl.ds(col, 1), :] = value
        pv[row, pl.ds(col, 1), :] = first * vol

    def copy_out(bin_id, both, slot):
        target = weight.at[bin_id // cols, lax.rem(bin_id, cols)]
        return pltpu.make_async_copy(both.at[pl.ds(0, width)], target, sem.at[slot])

    count = rows * cols
    columns(0, 0)
    columns(1, 1)

    def two_bins(step, carry):
        even = 2 * step

        @pl.when(step > 0)
        def _():
            copy_out(even - 2, both_a, 0).wait()

        blocks(even, 0, both_a)
        columns(jnp.minimum(even + 2, count - 1), 0)

        @pl.when(step > 0)
        def _():
            copy_out(even - 1, both_b, 1).wait()

        copy_out(even, both_a, 0).start()
        finish(even, both_a)
        blocks(even + 1, 1, both_b)
        columns(jnp.minimum(even + 3, count - 1), 1)
        copy_out(even + 1, both_b, 1).start()
        finish(even + 1, both_b)
        return carry

    lax.fori_loop(0, count // 2, two_bins, 0)
    copy_out(count - 2, both_a, 0).wait()
    copy_out(count - 1, both_b, 1).wait()


def setup(fresh, kappa):
    rows, cols, _, width = fresh.shape
    rows, cols = rows - 2, cols - 2
    vmem = pl.BlockSpec(memory_space=pltpu.VMEM)
    return call(
        functools.partial(setup_kernel, kappa),
        in_specs=[vmem],
        out_specs=(vmem, pl.BlockSpec(memory_space=pltpu.HBM), vmem, vmem),
        out_shape=(
            pltpu.VMEM((rows, cols, width, 9 * width), jnp.bfloat16),
            jax.ShapeDtypeStruct((rows, cols, width, 9 * width), jnp.bfloat16),
            jax.ShapeDtypeStruct((3, rows, cols, width), jnp.float32),
            jax.ShapeDtypeStruct((rows, cols, width), jnp.float32),
        ),
        scratch_shapes=[
            pltpu.VMEM((2, width, width), jnp.float32),
            pltpu.VMEM((2, width, width), jnp.float32),
            pltpu.VMEM((rows + 2, cols + 2, 3, 8, width), jnp.float32),
            pltpu.VMEM((2 * width, 9 * width), jnp.bfloat16),
            pltpu.VMEM((2 * width, 9 * width), jnp.bfloat16),
            pltpu.SemaphoreType.DMA((2,)),
        ],
        name="setup",
    )(fresh)


def sweep_kernel(kappa, last, center, above, below, left, right, coef, sums, pv, *rest):
    pressure = rest[0] if last else None
    ext, tiles = rest[-2:]
    rows, cols, width, _ = coef.shape
    assemble(ext, center, above, below, left, right, 1)

    def spread(row, carry):
        for col in range(cols + 2):
            tiles[row, col] = jnp.broadcast_to(ext[row, col : col + 1, :], (16, width)).astype(jnp.bfloat16)
        return carry

    lax.fori_loop(0, rows + 2, spread, 0)
    ones = jnp.ones((16, width), jnp.bfloat16)

    def one_row(row, carry):
        totals = []
        for col in range(cols):
            around = [tiles[row + k // 3, col + k % 3] for k in range(9)]
            parts = []
            for part in range(width // 16):
                total = None
                for k in range(9):
                    term = coef[row, col, pl.ds(part * 16, 16), pl.ds(k * width, width)] * around[k]
                    total = term if total is None else total + term
                parts.append(total)
            totals.append(dot_nt(ones, jnp.concatenate(parts, axis=0))[0:1])
        total = jnp.concatenate(totals, axis=0)
        value = (sums[0, row] + kappa * 40.0 * total) * sums[1, row]
        vol = sums[2, row]
        pv[row] = value * vol
        if last:
            pressure[row] = jnp.where(vol > 0.0, value, 0.0)
        return carry

    lax.fori_loop(0, rows, one_row, 0)


def sweep(kappa, last, pv, halo, coef, sums):
    rows, cols, width, _ = coef.shape
    vmem = pl.BlockSpec(memory_space=pltpu.VMEM)
    out = jax.ShapeDtypeStruct((rows, cols, width), jnp.float32)
    count = 2 if last else 1
    return call(
        functools.partial(sweep_kernel, kappa, last),
        in_specs=[vmem] * 7,
        out_specs=[vmem] * count,
        out_shape=[out] * count,
        scratch_shapes=[
            pltpu.VMEM((rows + 2, cols + 2, width), jnp.float32),
            pltpu.VMEM((rows + 2, cols + 2, 16, width), jnp.bfloat16),
        ],
        name="sweep",
    )(pv, *halo, pltpu.with_memory_space_constraint(coef, pltpu.VMEM), sums)


def push_kernel(kappa, center, above, below, left, right, fresh, weight, pressure, out, ext, feat):
    row = pl.program_id(0)
    cols, width, _ = weight.shape

    @pl.when(row == 0)
    def _():
        assemble(ext, center, above, below, left, right, 1)

        def one_row(r, carry):
            tiles = []
            for col in range(ext.shape[1]):
                value = ext[r, col : col + 1, :]
                tile = fresh[r, col]
                x, y, vol = tile[X : X + 1], tile[Y : Y + 1], tile[VOL : VOL + 1]
                zero = jnp.zeros_like(x)
                tiles.append(jnp.concatenate([value, value * x, value * y, zero, vol, vol * x, vol * y, zero], axis=0))
            for col in range(ext.shape[1]):
                feat[r, col] = tiles[col]
            return carry

        lax.fori_loop(0, ext.shape[0], one_row, 0)

    index = row_index(width)
    news = ([], [])
    for col in range(cols):
        around = []
        for k in range(9):
            tile = feat[row + k // 3, col + k % 3]
            off_x, off_y = k // 3 - 1.0, k % 3 - 1.0
            pv, vol = tile[0:1], tile[4:5]
            if off_x:
                tile = tile + jnp.where(index == 1, off_x * pv, jnp.where(index == 5, off_x * vol, 0.0))
            if off_y:
                tile = tile + jnp.where(index == 2, off_y * pv, jnp.where(index == 6, off_y * vol, 0.0))
            around.append(split(tile))
        total = dot_nt(weight[col], jnp.concatenate(around, axis=1))
        total = (total[:, :8] + total[:, 8:]).T
        tile = fresh[row + 1, col + 1]
        own = pressure[col : col + 1, :]
        alive = tile[VOL : VOL + 1] > 0.0
        for axis in (0, 1):
            at = tile[axis : axis + 1]
            grad = at * total[0:1] - total[1 + axis : 2 + axis] - own * (at * total[4:5] - total[5 + axis : 6 + axis])
            news[axis].append(jnp.where(alive, tile[2 + axis : 3 + axis] + kappa * 20.0 * grad, 0.0))
    out[0] = jnp.concatenate(news[0], axis=0)
    out[1] = jnp.concatenate(news[1], axis=0)


def push(kappa, pv, halo, fresh, weight, pressure):
    rows, cols, width, deep = weight.shape
    whole = pl.BlockSpec(memory_space=pltpu.VMEM)
    return call(
        functools.partial(push_kernel, kappa),
        grid=(rows,),
        in_specs=[whole] * 6
        + [
            pl.BlockSpec((None, cols, width, deep), lambda row: (row, 0, 0, 0)),
            pl.BlockSpec((None, cols, width), lambda row: (row, 0, 0)),
        ],
        out_specs=pl.BlockSpec((2, None, cols, width), lambda row: (0, row, 0, 0)),
        out_shape=jax.ShapeDtypeStruct((2, rows, cols, width), jnp.float32),
        scratch_shapes=[
            pltpu.VMEM((rows + 2, cols + 2, width), jnp.float32),
            pltpu.VMEM((rows + 2, cols + 2, 8, width), jnp.float32),
        ],
        name="push",
    )(pv, *halo, fresh, weight, pressure)


def local(position, velocity, volume, pressure_prev, fill, drift_from):
    kappa = 1.0 / volume.shape[2]
    old, top = prepare(position, velocity, volume, pressure_prev, fill, drift_from)
    top = largest(top)
    fresh = drift(top, old, *exchange(old, 2))
    coef, weight, sums, pv = setup(fresh, kappa)
    for step in range(1, SWEEPS):
        last = step == SWEEPS - 1
        pv, *pressure = sweep(kappa, last, pv, exchange(pv, 1), coef, sums)
    velocity_new = push(kappa, pv, exchange(pv, 1), fresh, weight, pressure[0])
    return (pressure[0], velocity_new)


def solution(mesh):
    return jax.shard_map(
        local,
        mesh=mesh,
        in_specs=(
            P(None, "gx", "gy", None),
            P(None, "gx", "gy", None),
            P("gx", "gy", None),
            P("gx", "gy", None),
            P("gx", "gy"),
            P("gx", "gy"),
        ),
        out_specs=(P("gx", "gy", None), P(None, "gx", "gy", None)),
        check_vma=False,
    )
```

```python
import functools

import jax
import jax.numpy as jnp
from jax import lax
from jax.experimental import pallas as pl
from jax.experimental.pallas import tpu as pltpu
from jax.sharding import PartitionSpec as P

SWEEPS = 4
CFL = 0.25
SPEED_EPS = 1e-06
SOFT = 0.01
CHUNK = 32
VMEM_LIMIT = 20 * 1024 * 1024

X, Y, U, V, VOL, PRES, CODE = range(7)


def call(kernel, **kwargs):
    return pl.pallas_call(
        kernel, compiler_params=pltpu.CompilerParams(vmem_limit_bytes=VMEM_LIMIT), **kwargs
    )


def row_index(width):
    return lax.broadcasted_iota(jnp.int32, (8, width), 0)


def split(value):
    high = value.astype(jnp.bfloat16).astype(jnp.float32)
    return jnp.concatenate([high, value - high], axis=0).astype(jnp.bfloat16)


def dot(left, right):
    return jnp.dot(left, right, preferred_element_type=jnp.float32)


def prepare_kernel(position, velocity, volume, pressure, fill, code, old, top):
    rows, cols, width = volume.shape
    slots = lax.broadcasted_iota(jnp.int32, (cols, width), 1)
    most = jnp.zeros((cols, width), jnp.float32)
    for row in range(rows):
        live = (slots < fill[row]).astype(jnp.float32)
        most = jnp.maximum(most, jnp.abs(velocity[0, row]) * live)
        most = jnp.maximum(most, jnp.abs(velocity[1, row]) * live)
        channels = [
            position[0, row],
            position[1, row],
            velocity[0, row],
            velocity[1, row],
            volume[row] * live,
            pressure[row],
            jnp.broadcast_to((code[row] + 1).astype(jnp.float32), (cols, width)),
            jnp.zeros((cols, width), jnp.float32),
        ]
        for channel, value in enumerate(channels):
            old[row, :, channel, :] = value
    top[...] = jnp.broadcast_to(jnp.max(most), top.shape)


def prepare(position, velocity, volume, pressure, fill, code):
    rows, cols, width = volume.shape
    return call(
        prepare_kernel,
        out_shape=(
            pltpu.VMEM((rows, cols, 8, width), jnp.float32),
            pltpu.VMEM((8, width), jnp.float32),
        ),
        name="prepare",
    )(position, velocity, volume, pressure, fill[:, :, None], code[:, :, None])


def neighbours(axis, low, high):
    devices = lax.axis_size(axis)
    even = lax.axis_index(axis) % 2 == 0

    def swap(value, first):
        pairs = [(i, i + 1) for i in range(first, devices - 1, 2)]
        return lax.ppermute(value, axis, pairs + [(j, i) for i, j in pairs])

    one = swap(jnp.where(even, high, low), 0)
    two = swap(jnp.where(even, low, high), 1)
    return jnp.where(even, two, one), jnp.where(even, one, two)


def exchange(shard, depth):
    above, below = neighbours("gx", shard[:depth], shard[-depth:])
    low = jnp.concatenate([above[:, :depth], shard[:, :depth], below[:, :depth]], axis=0)
    high = jnp.concatenate([above[:, -depth:], shard[:, -depth:], below[:, -depth:]], axis=0)
    left, right = neighbours("gy", low, high)
    return above, below, left, right


def largest(value):
    for axis in ("gy", "gx"):
        devices = lax.axis_size(axis)
        if devices & (devices - 1):
            value = lax.pmax(value, axis)
            continue
        for bit in range(devices.bit_length() - 1):
            pairs = [(i, i ^ (1 << bit)) for i in range(devices)]
            value = jnp.maximum(value, lax.ppermute(value, axis, pairs))
    return value


def assemble(out, center, above, below, left, right, depth):
    rows, cols = center.shape[:2]
    out[:depth, depth : depth + cols] = above[...]
    out[depth : depth + rows, depth : depth + cols] = center[...]
    out[depth + rows :, depth : depth + cols] = below[...]
    out[:, :depth] = left[...]
    out[:, depth + cols :] = right[...]


def drift_kernel(top, center, above, below, left, right, fresh, old):
    rows, cols, _, width = fresh.shape
    assemble(old, center, above, below, left, right, 2)
    step = CFL / (jnp.max(top[...]) + SPEED_EPS)
    index = row_index(width)

    def one_row(row, carry):
        for col in range(cols):
            code = old[row + 1, col + 1, CODE : CODE + 1, :]
            tile = jnp.zeros((8, width), jnp.float32)
            for k in range(9):
                off_x, off_y = k // 3, k % 3
                offset = jnp.where(index == X, off_x - 1.0, jnp.where(index == Y, off_y - 1.0, 0.0))
                source = old[row + off_x, col + off_y] + offset
                tile = jnp.where(code == k + 1.0, source, tile)
            moved = tile + step * pltpu.roll(tile, 6, 0)
            fresh[row, col] = jnp.where(index <= Y, moved, tile)
        return carry

    lax.fori_loop(0, rows, one_row, 0)


def drift(top, center, above, below, left, right):
    rows, cols, _, width = center.shape
    return call(
        drift_kernel,
        out_shape=pltpu.VMEM((rows + 2, cols + 2, 8, width), jnp.float32),
        scratch_shapes=[pltpu.VMEM((rows + 4, cols + 4, 8, width), jnp.float32)],
        name="drift",
    )(top, center, above, below, left, right)


def dot_nt(left, right):
    return lax.dot_general(left, right, (((1,), (1,)), ((), ())), preferred_element_type=jnp.float32)


def setup_kernel(fresh, coef, weight, xcol, ycol, out_a, out_b, sem):
    rows, cols, width, _ = coef.shape

    def columns(bin_id, slot):
        tile = fresh[bin_id // cols + 1, lax.rem(bin_id, cols) + 1]
        xcol[slot] = jnp.broadcast_to(tile[X : X + 1], (width, width)).T
        ycol[slot] = jnp.broadcast_to(tile[Y : Y + 1], (width, width)).T

    def blocks(bin_id, slot, out):
        row, col = bin_id // cols, lax.rem(bin_id, cols)
        around = [fresh[row + k // 3, col + k % 3] for k in range(9)]
        xj = [jnp.broadcast_to(around[k][X : X + 1] + (k // 3 - 1.0), (8, width)) for k in range(9)]
        yj = [jnp.broadcast_to(around[k][Y : Y + 1] + (k % 3 - 1.0), (8, width)) for k in range(9)]
        for part in range(width // CHUNK):
            span = pl.ds(part * CHUNK, CHUNK)
            spans = [pl.ds(part * CHUNK + 8 * i, 8) for i in range(CHUNK // 8)]
            xi = [xcol[slot, piece] for piece in spans]
            yi = [ycol[slot, piece] for piece in spans]
            for k in range(9):
                lanes = pl.ds(k * width, width)
                squares, weights = [], []
                for x, y in zip(xi, yi):
                    dx = x - xj[k]
                    dy = y - yj[k]
                    square = jnp.maximum(dx * dx + dy * dy, 1e-14)
                    remain = jnp.maximum(1.0 - square * lax.rsqrt(square), 0.0)
                    squares.append(square)
                    weights.append(remain * remain * remain)
                squares = jnp.concatenate(squares, axis=0).astype(jnp.bfloat16)
                weights = jnp.concatenate(weights, axis=0).astype(jnp.bfloat16)
                ratio = squares * pltpu.reciprocal(squares + jnp.bfloat16(SOFT), approx=True)
                out[span, lanes] = weights
                coef[row, col, span, lanes] = weights * ratio

    def copy_out(bin_id, out, slot):
        target = weight.at[bin_id // cols, lax.rem(bin_id, cols)]
        return pltpu.make_async_copy(out, target, sem.at[slot])

    count = rows * cols
    columns(0, 0)
    columns(1, 1)

    def two_bins(step, carry):
        even = 2 * step

        @pl.when(step > 0)
        def _():
            copy_out(even - 2, out_a, 0).wait()

        blocks(even, 0, out_a)
        columns(jnp.minimum(even + 2, count - 1), 0)
        copy_out(even, out_a, 0).start()

        @pl.when(step > 0)
        def _():
            copy_out(even - 1, out_b, 1).wait()

        blocks(even + 1, 1, out_b)
        columns(jnp.minimum(even + 3, count - 1), 1)
        copy_out(even + 1, out_b, 1).start()
        return carry

    lax.fori_loop(0, count // 2, two_bins, 0)
    copy_out(count - 2, out_a, 0).wait()
    copy_out(count - 1, out_b, 1).wait()


def setup(fresh):
    rows, cols, _, width = fresh.shape
    rows, cols = rows - 2, cols - 2
    vmem = pl.BlockSpec(memory_space=pltpu.VMEM)
    return call(
        setup_kernel,
        in_specs=[vmem],
        out_specs=(vmem, pl.BlockSpec(memory_space=pltpu.HBM)),
        out_shape=(
            pltpu.VMEM((rows, cols, width, 9 * width), jnp.bfloat16),
            jax.ShapeDtypeStruct((rows, cols, width, 9 * width), jnp.bfloat16),
        ),
        scratch_shapes=[
            pltpu.VMEM((2, width, width), jnp.float32),
            pltpu.VMEM((2, width, width), jnp.float32),
            pltpu.VMEM((width, 9 * width), jnp.bfloat16),
            pltpu.VMEM((width, 9 * width), jnp.bfloat16),
            pltpu.SemaphoreType.DMA((2,)),
        ],
        name="setup",
    )(fresh)


def first_kernel(kappa, fresh, coef, weight, sums, pv, feat):
    row = pl.program_id(0)
    cols, width, _ = weight.shape

    @pl.when(row == 0)
    def _():
        def one_row(r, carry):
            tiles = []
            for col in range(fresh.shape[1]):
                tile = fresh[r, col]
                x, y, u, v = (tile[i : i + 1] for i in range(4))
                vol = tile[VOL : VOL + 1]
                zero = jnp.zeros_like(vol)
                vol_u, vol_v = vol * u, vol * v
                base = [vol, vol * x, vol * y, vol_u, vol_v, vol_u * x + vol_v * y, vol * tile[PRES : PRES + 1], zero]
                along_x = [zero, vol, zero, zero, zero, vol_u, zero, zero]
                along_y = [zero, zero, vol, zero, zero, vol_v, zero, zero]
                tiles.append([jnp.concatenate(rows, axis=0) for rows in (base, along_x, along_y)])
            for col in range(fresh.shape[1]):
                for i in range(3):
                    feat[r, col, i] = tiles[col][i]
            return carry

        lax.fori_loop(0, fresh.shape[0], one_row, 0)

    outs = ([], [], [], [])
    for col in range(cols):
        around = []
        for k in range(9):
            off_x, off_y = k // 3 - 1, k % 3 - 1
            features = feat[row + k // 3, col + k % 3, 0]
            if off_x:
                features = features + float(off_x) * feat[row + k // 3, col + k % 3, 1]
            if off_y:
                features = features + float(off_y) * feat[row + k // 3, col + k % 3, 2]
            around.append(split(features))
        around = jnp.concatenate(around, axis=1)
        total_w = dot_nt(weight[col], around)
        total_c = dot_nt(coef[row, col], around)
        total_w = (total_w[:, :8] + total_w[:, 8:]).T
        total_c = (total_c[:, :8] + total_c[:, 8:]).T
        tile = fresh[row + 1, col + 1]
        x, y, u, v = (tile[i : i + 1] for i in range(4))
        vol = tile[VOL : VOL + 1]
        w_0, w_x, w_y, w_u, w_v, w_flow = (total_w[i : i + 1] for i in range(6))
        source = x * w_u + y * w_v - w_flow - (u * x + v * y) * w_0 + u * w_x + v * w_y
        source = kappa * 20.0 * source
        rden = 1.0 / (1.0 + kappa * 40.0 * total_c[0:1])
        first = (source + kappa * 40.0 * total_c[6:7]) * rden
        for out, value in zip(outs, (source, rden, vol, first * vol)):
            out.append(value)
    for place in range(3):
        sums[place, row] = jnp.concatenate(outs[place], axis=0)
    pv[row] = jnp.concatenate(outs[3], axis=0)


def first_sweep(kappa, fresh, coef, weight):
    rows, cols, width, deep = weight.shape
    vmem = pl.BlockSpec(memory_space=pltpu.VMEM)
    return call(
        functools.partial(first_kernel, kappa),
        grid=(rows,),
        in_specs=[vmem, vmem, pl.BlockSpec((None, cols, width, deep), lambda row: (row, 0, 0, 0))],
        out_specs=(vmem, vmem),
        out_shape=(
            pltpu.VMEM((3, rows, cols, width), jnp.float32),
            pltpu.VMEM((rows, cols, width), jnp.float32),
        ),
        scratch_shapes=[pltpu.VMEM((rows + 2, cols + 2, 3, 8, width), jnp.float32)],
        name="first_sweep",
    )(fresh, pltpu.with_memory_space_constraint(coef, pltpu.VMEM), weight)


def sweep_kernel(kappa, last, center, above, below, left, right, coef, sums, pv, *rest):
    pressure = rest[0] if last else None
    ext, tiles = rest[-2:]
    rows, cols, width, _ = coef.shape
    assemble(ext, center, above, below, left, right, 1)

    def spread(row, carry):
        for col in range(cols + 2):
            tiles[row, col] = jnp.broadcast_to(ext[row, col : col + 1, :], (16, width)).astype(jnp.bfloat16)
        return carry

    lax.fori_loop(0, rows + 2, spread, 0)
    ones = jnp.ones((16, width), jnp.bfloat16)

    def one_row(row, carry):
        totals = []
        for col in range(cols):
            around = [tiles[row + k // 3, col + k % 3] for k in range(9)]
            parts = []
            for part in range(width // 16):
                total = None
                for k in range(9):
                    term = coef[row, col, pl.ds(part * 16, 16), pl.ds(k * width, width)] * around[k]
                    total = term if total is None else total + term
                parts.append(total)
            totals.append(dot_nt(ones, jnp.concatenate(parts, axis=0))[0:1])
        total = jnp.concatenate(totals, axis=0)
        value = (sums[0, row] + kappa * 40.0 * total) * sums[1, row]
        vol = sums[2, row]
        pv[row] = value * vol
        if last:
            pressure[row] = jnp.where(vol > 0.0, value, 0.0)
        return carry

    lax.fori_loop(0, rows, one_row, 0)


def sweep(kappa, last, pv, halo, coef, sums):
    rows, cols, width, _ = coef.shape
    vmem = pl.BlockSpec(memory_space=pltpu.VMEM)
    out = pltpu.VMEM((rows, cols, width), jnp.float32)
    count = 2 if last else 1
    return call(
        functools.partial(sweep_kernel, kappa, last),
        in_specs=[vmem] * 7,
        out_specs=[vmem] * count,
        out_shape=[out] * count,
        scratch_shapes=[
            pltpu.VMEM((rows + 2, cols + 2, width), jnp.float32),
            pltpu.VMEM((rows + 2, cols + 2, 16, width), jnp.bfloat16),
        ],
        name="sweep",
    )(pv, *halo, pltpu.with_memory_space_constraint(coef, pltpu.VMEM), sums)


def push_kernel(kappa, center, above, below, left, right, fresh, weight, pressure, out, ext, feat):
    row = pl.program_id(0)
    cols, width, _ = weight.shape

    @pl.when(row == 0)
    def _():
        assemble(ext, center, above, below, left, right, 1)

        def one_row(r, carry):
            tiles = []
            for col in range(ext.shape[1]):
                value = ext[r, col : col + 1, :]
                tile = fresh[r, col]
                x, y, vol = tile[X : X + 1], tile[Y : Y + 1], tile[VOL : VOL + 1]
                zero = jnp.zeros_like(x)
                tiles.append(jnp.concatenate([value, value * x, value * y, zero, vol, vol * x, vol * y, zero], axis=0))
            for col in range(ext.shape[1]):
                feat[r, col] = tiles[col]
            return carry

        lax.fori_loop(0, ext.shape[0], one_row, 0)

    index = row_index(width)
    news = ([], [])
    for col in range(cols):
        around = []
        for k in range(9):
            tile = feat[row + k // 3, col + k % 3]
            off_x, off_y = k // 3 - 1.0, k % 3 - 1.0
            pv, vol = tile[0:1], tile[4:5]
            if off_x:
                tile = tile + jnp.where(index == 1, off_x * pv, jnp.where(index == 5, off_x * vol, 0.0))
            if off_y:
                tile = tile + jnp.where(index == 2, off_y * pv, jnp.where(index == 6, off_y * vol, 0.0))
            around.append(split(tile))
        total = dot_nt(weight[col], jnp.concatenate(around, axis=1))
        total = (total[:, :8] + total[:, 8:]).T
        tile = fresh[row + 1, col + 1]
        own = pressure[col : col + 1, :]
        alive = tile[VOL : VOL + 1] > 0.0
        for axis in (0, 1):
            at = tile[axis : axis + 1]
            grad = at * total[0:1] - total[1 + axis : 2 + axis] - own * (at * total[4:5] - total[5 + axis : 6 + axis])
            news[axis].append(jnp.where(alive, tile[2 + axis : 3 + axis] + kappa * 20.0 * grad, 0.0))
    out[0] = jnp.concatenate(news[0], axis=0)
    out[1] = jnp.concatenate(news[1], axis=0)


def push(kappa, pv, halo, fresh, weight, pressure):
    rows, cols, width, deep = weight.shape
    whole = pl.BlockSpec(memory_space=pltpu.VMEM)
    return call(
        functools.partial(push_kernel, kappa),
        grid=(rows,),
        in_specs=[whole] * 6
        + [
            pl.BlockSpec((None, cols, width, deep), lambda row: (row, 0, 0, 0)),
            pl.BlockSpec((None, cols, width), lambda row: (row, 0, 0)),
        ],
        out_specs=pl.BlockSpec((2, None, cols, width), lambda row: (0, row, 0, 0)),
        out_shape=jax.ShapeDtypeStruct((2, rows, cols, width), jnp.float32),
        scratch_shapes=[
            pltpu.VMEM((rows + 2, cols + 2, width), jnp.float32),
            pltpu.VMEM((rows + 2, cols + 2, 8, width), jnp.float32),
        ],
        name="push",
    )(pv, *halo, fresh, weight, pressure)


def local(position, velocity, volume, pressure_prev, fill, drift_from):
    kappa = 1.0 / volume.shape[2]
    old, top = prepare(position, velocity, volume, pressure_prev, fill, drift_from)
    top = largest(top)
    fresh = drift(top, old, *exchange(old, 2))
    coef, weight = setup(fresh)
    sums, pv = first_sweep(kappa, fresh, coef, weight)
    for step in range(1, SWEEPS):
        last = step == SWEEPS - 1
        pv, *pressure = sweep(kappa, last, pv, exchange(pv, 1), coef, sums)
    velocity_new = push(kappa, pv, exchange(pv, 1), fresh, weight, pressure[0])
    return (pressure[0], velocity_new)


def solution(mesh):
    return jax.shard_map(
        local,
        mesh=mesh,
        in_specs=(
            P(None, "gx", "gy", None),
            P(None, "gx", "gy", None),
            P("gx", "gy", None),
            P("gx", "gy", None),
            P("gx", "gy"),
            P("gx", "gy"),
        ),
        out_specs=(P("gx", "gy", None), P(None, "gx", "gy", None)),
        check_vma=False,
    )
```

```python
import functools

import jax
import jax.numpy as jnp
from jax import lax
from jax.experimental import pallas as pl
from jax.experimental.pallas import tpu as pltpu
from jax.sharding import PartitionSpec as P

SWEEPS = 4
CFL = 0.25
SPEED_EPS = 1e-06
SOFT = 0.01
CHUNK = 64
VMEM_LIMIT = 20 * 1024 * 1024

X, Y, U, V, VOL, PRES, CODE = range(7)


def call(kernel, **kwargs):
    return pl.pallas_call(
        kernel, compiler_params=pltpu.CompilerParams(vmem_limit_bytes=VMEM_LIMIT), **kwargs
    )


def row_index(width):
    return lax.broadcasted_iota(jnp.int32, (8, width), 0)


def split(value):
    high = value.astype(jnp.bfloat16).astype(jnp.float32)
    return jnp.concatenate([high, value - high], axis=0).astype(jnp.bfloat16)


def dot(left, right):
    return jnp.dot(left, right, preferred_element_type=jnp.float32)


def prepare_kernel(position, velocity, volume, pressure, fill, code, old, top):
    rows, cols, width = volume.shape
    slots = lax.broadcasted_iota(jnp.int32, (cols, width), 1)
    most = jnp.zeros((cols, width), jnp.float32)
    for row in range(rows):
        live = (slots < fill[row]).astype(jnp.float32)
        most = jnp.maximum(most, jnp.abs(velocity[0, row]) * live)
        most = jnp.maximum(most, jnp.abs(velocity[1, row]) * live)
        channels = [
            position[0, row],
            position[1, row],
            velocity[0, row],
            velocity[1, row],
            volume[row] * live,
            pressure[row],
            jnp.broadcast_to((code[row] + 1).astype(jnp.float32), (cols, width)),
            jnp.zeros((cols, width), jnp.float32),
        ]
        for channel, value in enumerate(channels):
            old[row, :, channel, :] = value
    top[...] = jnp.broadcast_to(jnp.max(most), top.shape)


def prepare(position, velocity, volume, pressure, fill, code):
    rows, cols, width = volume.shape
    return call(
        prepare_kernel,
        out_shape=(
            pltpu.VMEM((rows, cols, 8, width), jnp.float32),
            pltpu.VMEM((8, width), jnp.float32),
        ),
        name="prepare",
    )(position, velocity, volume, pressure, fill[:, :, None], code[:, :, None])


def neighbours(axis, low, high):
    devices = lax.axis_size(axis)
    even = lax.axis_index(axis) % 2 == 0

    def swap(value, first):
        pairs = [(i, i + 1) for i in range(first, devices - 1, 2)]
        return lax.ppermute(value, axis, pairs + [(j, i) for i, j in pairs])

    one = swap(jnp.where(even, high, low), 0)
    two = swap(jnp.where(even, low, high), 1)
    return jnp.where(even, two, one), jnp.where(even, one, two)


def exchange_old(shard, depth):
    above, below = neighbours("gx", shard[:depth], shard[-depth:])
    low = jnp.concatenate([above[:, :depth], shard[:, :depth], below[:, :depth]], axis=0)
    high = jnp.concatenate([above[:, -depth:], shard[:, -depth:], below[:, -depth:]], axis=0)
    left, right = neighbours("gy", low, high)
    return above, below, left, right


def exchange_edges(edge, rows):
    above, below = neighbours("gx", edge[0], edge[1])
    half = edge.shape[1] // 2
    low = jnp.concatenate([above[:1], edge[0, :1], edge[2, : rows - 2], edge[1, :1], below[:1]], axis=0)
    high = jnp.concatenate([above[-1:], edge[0, -1:], edge[2, half : half + rows - 2], edge[1, -1:], below[-1:]], axis=0)
    left, right = neighbours("gy", low, high)
    return above, below, left, right


def groups_of(edge, rows, cols):
    return (3, cols) if edge else (rows - 2, cols - 2)


def place_of(edge, group, index, rows, cols):
    if not edge:
        return group + 1, index + 1
    half = cols // 2
    left = index < half
    side_row = jnp.minimum(jnp.where(left, index, index - half) + 1, rows - 2)
    side_col = jnp.where(left, 0, cols - 1)
    row = jnp.where(group == 0, 0, jnp.where(group == 1, rows - 1, side_row))
    return row, jnp.where(group == 2, side_col, index)


def join(out, at, edge, inner, rows, cols):
    half = cols // 2
    out[at, at : at + cols] = edge[0]
    out[at + rows - 1, at : at + cols] = edge[1]
    for row in range(1, rows - 1):
        out[at + row, at : at + 1] = edge[2, row - 1 : row]
        out[at + row, at + cols - 1 : at + cols] = edge[2, half + row - 1 : half + row]
        out[at + row, at + 1 : at + cols - 1] = inner[row - 1]


def frame(out, above, below, left, right, rows, cols):
    out[0, 1 : cols + 1] = above[...]
    out[rows + 1, 1 : cols + 1] = below[...]
    for row in range(rows + 2):
        out[row, 0:1] = left[row : row + 1]
        out[row, cols + 1 : cols + 2] = right[row : row + 1]


def largest(value):
    for axis in ("gy", "gx"):
        devices = lax.axis_size(axis)
        if devices & (devices - 1):
            value = lax.pmax(value, axis)
            continue
        for bit in range(devices.bit_length() - 1):
            pairs = [(i, i ^ (1 << bit)) for i in range(devices)]
            value = jnp.maximum(value, lax.ppermute(value, axis, pairs))
    return value


def assemble(out, center, above, below, left, right, depth):
    rows, cols = center.shape[:2]
    out[:depth, depth : depth + cols] = above[...]
    out[depth : depth + rows, depth : depth + cols] = center[...]
    out[depth + rows :, depth : depth + cols] = below[...]
    out[:, :depth] = left[...]
    out[:, depth + cols :] = right[...]


def drift_kernel(top, center, above, below, left, right, fresh, old):
    rows, cols, _, width = fresh.shape
    assemble(old, center, above, below, left, right, 2)
    step = CFL / (jnp.max(top[...]) + SPEED_EPS)
    index = row_index(width)

    def one_row(row, carry):
        for col in range(cols):
            code = old[row + 1, col + 1, CODE : CODE + 1, :]
            tile = jnp.zeros((8, width), jnp.float32)
            for k in range(9):
                off_x, off_y = k // 3, k % 3
                offset = jnp.where(index == X, off_x - 1.0, jnp.where(index == Y, off_y - 1.0, 0.0))
                source = old[row + off_x, col + off_y] + offset
                tile = jnp.where(code == k + 1.0, source, tile)
            moved = tile + step * pltpu.roll(tile, 6, 0)
            fresh[row, col] = jnp.where(index <= Y, moved, tile)
        return carry

    lax.fori_loop(0, rows, one_row, 0)


def drift(top, center, above, below, left, right):
    rows, cols, _, width = center.shape
    return call(
        drift_kernel,
        out_shape=pltpu.VMEM((rows + 2, cols + 2, 8, width), jnp.float32),
        scratch_shapes=[pltpu.VMEM((rows + 4, cols + 4, 8, width), jnp.float32)],
        name="drift",
    )(top, center, above, below, left, right)


def dot_nt(left, right):
    return lax.dot_general(left, right, (((1,), (1,)), ((), ())), preferred_element_type=jnp.float32)


def setup_kernel(edge, fresh, coef, weight, xcol, ycol, out_a, out_b, sem):
    groups, size, width, _ = coef.shape
    rows, cols = fresh.shape[0] - 2, fresh.shape[1] - 2

    def place(bin_id):
        return place_of(edge, bin_id // size, lax.rem(bin_id, size), rows, cols)

    def columns(bin_id, slot):
        row, col = place(bin_id)
        tile = fresh[row + 1, col + 1]
        xcol[slot] = jnp.broadcast_to(tile[X : X + 1], (width, width)).T
        ycol[slot] = jnp.broadcast_to(tile[Y : Y + 1], (width, width)).T

    def blocks(bin_id, slot, out):
        row, col = place(bin_id)
        values = coef.at[bin_id // size, lax.rem(bin_id, size)]
        around = [fresh[row + k // 3, col + k % 3] for k in range(9)]
        xj = [jnp.broadcast_to(around[k][X : X + 1] + (k // 3 - 1.0), (8, width)) for k in range(9)]
        yj = [jnp.broadcast_to(around[k][Y : Y + 1] + (k % 3 - 1.0), (8, width)) for k in range(9)]
        for part in range(width // CHUNK):
            span = pl.ds(part * CHUNK, CHUNK)
            spans = [pl.ds(part * CHUNK + 8 * i, 8) for i in range(CHUNK // 8)]
            xi = [xcol[slot, piece] for piece in spans]
            yi = [ycol[slot, piece] for piece in spans]
            for k in range(9):
                lanes = pl.ds(k * width, width)
                squares, weights = [], []
                for x, y in zip(xi, yi):
                    dx = x - xj[k]
                    dy = y - yj[k]
                    square = jnp.maximum(dx * dx + dy * dy, 1e-14)
                    remain = jnp.maximum(1.0 - square * lax.rsqrt(square), 0.0)
                    squares.append(square)
                    weights.append(remain * remain * remain)
                squares = jnp.concatenate(squares, axis=0).astype(jnp.bfloat16)
                weights = jnp.concatenate(weights, axis=0).astype(jnp.bfloat16)
                ratio = squares * pltpu.reciprocal(squares + jnp.bfloat16(SOFT), approx=True)
                out[span, lanes] = weights
                values[span, lanes] = weights * ratio

    def copy_out(bin_id, out, slot):
        target = weight.at[bin_id // size, lax.rem(bin_id, size)]
        return pltpu.make_async_copy(out, target, sem.at[slot])

    count = groups * size
    columns(0, 0)
    columns(1, 1)

    def two_bins(step, carry):
        even = 2 * step

        @pl.when(step > 0)
        def _():
            copy_out(even - 2, out_a, 0).wait()

        blocks(even, 0, out_a)
        columns(jnp.minimum(even + 2, count - 1), 0)
        copy_out(even, out_a, 0).start()

        @pl.when(step > 0)
        def _():
            copy_out(even - 1, out_b, 1).wait()

        blocks(even + 1, 1, out_b)
        columns(jnp.minimum(even + 3, count - 1), 1)
        copy_out(even + 1, out_b, 1).start()
        return carry

    lax.fori_loop(0, count // 2, two_bins, 0)
    copy_out(count - 2, out_a, 0).wait()
    copy_out(count - 1, out_b, 1).wait()


def setup(edge, fresh):
    rows, cols, _, width = fresh.shape
    groups, size = groups_of(edge, rows - 2, cols - 2)
    vmem = pl.BlockSpec(memory_space=pltpu.VMEM)
    return call(
        functools.partial(setup_kernel, edge),
        in_specs=[vmem],
        out_specs=(vmem, pl.BlockSpec(memory_space=pltpu.HBM)),
        out_shape=(
            pltpu.VMEM((groups, size, width, 9 * width), jnp.bfloat16),
            jax.ShapeDtypeStruct((groups, size, width, 9 * width), jnp.bfloat16),
        ),
        scratch_shapes=[
            pltpu.VMEM((2, width, width), jnp.float32),
            pltpu.VMEM((2, width, width), jnp.float32),
            pltpu.VMEM((width, 9 * width), jnp.bfloat16),
            pltpu.VMEM((width, 9 * width), jnp.bfloat16),
            pltpu.SemaphoreType.DMA((2,)),
        ],
        name="setup",
    )(fresh)


def first_kernel(kappa, edge, fresh, coef, weight, sums, pv, feat):
    group = pl.program_id(0)
    size, width, _ = weight.shape

    @pl.when(group == 0)
    def _():
        def one_row(r, carry):
            tiles = []
            for col in range(fresh.shape[1]):
                tile = fresh[r, col]
                x, y, u, v = (tile[i : i + 1] for i in range(4))
                vol = tile[VOL : VOL + 1]
                zero = jnp.zeros_like(vol)
                vol_u, vol_v = vol * u, vol * v
                base = [vol, vol * x, vol * y, vol_u, vol_v, vol_u * x + vol_v * y, vol * tile[PRES : PRES + 1], zero]
                along_x = [zero, vol, zero, zero, zero, vol_u, zero, zero]
                along_y = [zero, zero, vol, zero, zero, vol_v, zero, zero]
                tiles.append([jnp.concatenate(rows, axis=0) for rows in (base, along_x, along_y)])
            for col in range(fresh.shape[1]):
                for i in range(3):
                    feat[r, col, i] = tiles[col][i]
            return carry

        lax.fori_loop(0, fresh.shape[0], one_row, 0)

    outs = ([], [], [], [])
    for index in range(size):
        row, col = place_of(edge, group, index, fresh.shape[0] - 2, fresh.shape[1] - 2)
        around = []
        for k in range(9):
            off_x, off_y = k // 3 - 1, k % 3 - 1
            features = feat[row + k // 3, col + k % 3, 0]
            if off_x:
                features = features + float(off_x) * feat[row + k // 3, col + k % 3, 1]
            if off_y:
                features = features + float(off_y) * feat[row + k // 3, col + k % 3, 2]
            around.append(split(features))
        around = jnp.concatenate(around, axis=1)
        total_w = dot_nt(weight[index], around)
        total_c = dot_nt(coef[group, index], around)
        total_w = (total_w[:, :8] + total_w[:, 8:]).T
        total_c = (total_c[:, :8] + total_c[:, 8:]).T
        tile = fresh[row + 1, col + 1]
        x, y, u, v = (tile[i : i + 1] for i in range(4))
        vol = tile[VOL : VOL + 1]
        w_0, w_x, w_y, w_u, w_v, w_flow = (total_w[i : i + 1] for i in range(6))
        source = x * w_u + y * w_v - w_flow - (u * x + v * y) * w_0 + u * w_x + v * w_y
        source = kappa * 20.0 * source
        rden = 1.0 / (1.0 + kappa * 40.0 * total_c[0:1])
        first = (source + kappa * 40.0 * total_c[6:7]) * rden
        for out, value in zip(outs, (source, rden, vol, first * vol)):
            out.append(value)
    for place in range(3):
        sums[place, group] = jnp.concatenate(outs[place], axis=0)
    pv[group] = jnp.concatenate(outs[3], axis=0)


def first_sweep(kappa, edge, fresh, coef, weight):
    groups, size, width, deep = weight.shape
    rows, cols = fresh.shape[:2]
    vmem = pl.BlockSpec(memory_space=pltpu.VMEM)
    return call(
        functools.partial(first_kernel, kappa, edge),
        grid=(groups,),
        in_specs=[vmem, vmem, pl.BlockSpec((None, size, width, deep), lambda group: (group, 0, 0, 0))],
        out_specs=(vmem, vmem),
        out_shape=(
            pltpu.VMEM((3, groups, size, width), jnp.float32),
            pltpu.VMEM((groups, size, width), jnp.float32),
        ),
        scratch_shapes=[pltpu.VMEM((rows, cols, 3, 8, width), jnp.float32)],
        name="first_sweep",
    )(fresh, pltpu.with_memory_space_constraint(coef, pltpu.VMEM), weight)


def sweep_kernel(kappa, last, edge, rows, cols, count, *refs):
    before_edge, before_inner, *halo = refs[: count - 2]
    coef, sums = refs[count - 2 : count]
    pv, *pressure = refs[count:-2]
    ext, tiles = refs[-2:]
    groups, size, width, _ = coef.shape
    join(ext, 1, before_edge, before_inner, rows, cols)
    if edge:
        frame(ext, *halo, rows, cols)

    def spread(row, carry):
        for col in range(cols + 2):
            tiles[row, col] = jnp.broadcast_to(ext[row, col : col + 1, :], (16, width)).astype(jnp.bfloat16)
        return carry

    if edge:
        lax.fori_loop(0, rows + 2, spread, 0)
    else:
        lax.fori_loop(1, rows + 1, spread, 0)
    ones = jnp.ones((16, width), jnp.bfloat16)

    def one_group(group, carry):
        totals = []
        for index in range(size):
            row, col = place_of(edge, group, index, rows, cols)
            around = [tiles[row + k // 3, col + k % 3] for k in range(9)]
            parts = []
            for part in range(width // 16):
                total = None
                for k in range(9):
                    term = coef[group, index, pl.ds(part * 16, 16), pl.ds(k * width, width)] * around[k]
                    total = term if total is None else total + term
                parts.append(total)
            totals.append(dot_nt(ones, jnp.concatenate(parts, axis=0))[0:1])
        total = jnp.concatenate(totals, axis=0)
        value = (sums[0, group] + kappa * 40.0 * total) * sums[1, group]
        vol = sums[2, group]
        pv[group] = value * vol
        if last:
            pressure[0][group] = jnp.where(vol > 0.0, value, 0.0)
        return carry

    lax.fori_loop(0, groups, one_group, 0)


def sweep(kappa, last, edge, shape, pv, halo, coef, sums):
    rows, cols, width = shape
    groups, size = coef.shape[:2]
    vmem = pl.BlockSpec(memory_space=pltpu.VMEM)
    out = pltpu.VMEM((groups, size, width), jnp.float32)
    outs = 2 if last else 1
    args = (*pv, *(halo if edge else ()), pltpu.with_memory_space_constraint(coef, pltpu.VMEM), sums)
    return call(
        functools.partial(sweep_kernel, kappa, last, edge, rows, cols, len(args)),
        in_specs=[vmem] * len(args),
        out_specs=[vmem] * outs,
        out_shape=[out] * outs,
        scratch_shapes=[
            pltpu.VMEM((rows + 2, cols + 2, width), jnp.float32),
            pltpu.VMEM((rows + 2, cols + 2, 16, width), jnp.bfloat16),
        ],
        name="sweep",
    )(*args)


def push_kernel(kappa, edge, count, *refs):
    before_edge, before_inner, *halo = refs[: count - (5 if edge else 3)]
    fresh, weight, pressure = refs[count - (5 if edge else 3) : count][:3]
    ext, feat = refs[-2:]
    group = pl.program_id(0)
    size, width, _ = weight.shape
    rows, cols = fresh.shape[0] - 2, fresh.shape[1] - 2

    @pl.when(group == 0)
    def _():
        join(ext, 1, before_edge, before_inner, rows, cols)
        if edge:
            frame(ext, *halo, rows, cols)

        def one_row(r, carry):
            tiles = []
            for col in range(ext.shape[1]):
                value = ext[r, col : col + 1, :]
                tile = fresh[r, col]
                x, y, vol = tile[X : X + 1], tile[Y : Y + 1], tile[VOL : VOL + 1]
                zero = jnp.zeros_like(x)
                tiles.append(jnp.concatenate([value, value * x, value * y, zero, vol, vol * x, vol * y, zero], axis=0))
            for col in range(ext.shape[1]):
                feat[r, col] = tiles[col]
            return carry

        lax.fori_loop(0, rows + 2, one_row, 0)

    feature = row_index(width)
    news = ([], [])
    for index in range(size):
        row, col = place_of(edge, group, index, rows, cols)
        around = []
        for k in range(9):
            tile = feat[row + k // 3, col + k % 3]
            off_x, off_y = k // 3 - 1.0, k % 3 - 1.0
            pv, vol = tile[0:1], tile[4:5]
            if off_x:
                tile = tile + jnp.where(feature == 1, off_x * pv, jnp.where(feature == 5, off_x * vol, 0.0))
            if off_y:
                tile = tile + jnp.where(feature == 2, off_y * pv, jnp.where(feature == 6, off_y * vol, 0.0))
            around.append(split(tile))
        total = dot_nt(weight[index], jnp.concatenate(around, axis=1))
        total = (total[:, :8] + total[:, 8:]).T
        tile = fresh[row + 1, col + 1]
        own = pressure[group, index : index + 1, :]
        alive = tile[VOL : VOL + 1] > 0.0
        for axis in (0, 1):
            at = tile[axis : axis + 1]
            grad = at * total[0:1] - total[1 + axis : 2 + axis] - own * (at * total[4:5] - total[5 + axis : 6 + axis])
            news[axis].append(jnp.where(alive, tile[2 + axis : 3 + axis] + kappa * 20.0 * grad, 0.0))
    if not edge:
        out = refs[count]
        for axis in (0, 1):
            out[axis, group] = jnp.concatenate(news[axis], axis=0)
        return
    inner_pressure, inner_new = refs[count - 2 : count]
    out_pressure, out_new, new = refs[count:-2]
    for axis in (0, 1):
        new[axis, group] = jnp.concatenate(news[axis], axis=0)

    @pl.when(group == 2)
    def _():
        join(out_pressure, 0, pressure, inner_pressure, rows, cols)
        for axis in (0, 1):
            join(out_new.at[axis], 0, new.at[axis], inner_new.at[axis], rows, cols)


def push(kappa, edge, pv, halo, fresh, weight, pressure, inner):
    groups, size, width, deep = weight.shape
    rows, cols = fresh.shape[:2]
    vmem = pl.BlockSpec(memory_space=pltpu.VMEM)
    args = (*pv, *(halo if edge else ()), fresh, weight, pressure, *(inner if edge else ()))
    specs = [vmem] * len(args)
    specs[len(pv) + (len(halo) if edge else 0) + 1] = pl.BlockSpec(
        (None, size, width, deep), lambda group: (group, 0, 0, 0)
    )
    if edge:
        outs = [
            jax.ShapeDtypeStruct((rows - 2, cols - 2, width), jnp.float32),
            jax.ShapeDtypeStruct((2, rows - 2, cols - 2, width), jnp.float32),
        ]
    else:
        outs = [pltpu.VMEM((2, groups, size, width), jnp.float32)]
    return call(
        functools.partial(push_kernel, kappa, edge, len(args)),
        grid=(groups,),
        in_specs=specs,
        out_specs=[vmem] * len(outs),
        out_shape=outs,
        scratch_shapes=([pltpu.VMEM((2, groups, size, width), jnp.float32)] if edge else [])
        + [
            pltpu.VMEM((rows, cols, width), jnp.float32),
            pltpu.VMEM((rows, cols, 8, width), jnp.float32),
        ],
        name="push",
    )(*args)


def local(position, velocity, volume, pressure_prev, fill, drift_from):
    shape = volume.shape
    kappa = 1.0 / shape[2]
    old, top = prepare(position, velocity, volume, pressure_prev, fill, drift_from)
    top = largest(top)
    fresh = drift(top, old, *exchange_old(old, 2))
    edge_coef, edge_weight = setup(True, fresh)
    edge_sums, edge_pv = first_sweep(kappa, True, fresh, edge_coef, edge_weight)
    inner_coef, inner_weight = setup(False, fresh)
    inner_sums, inner_pv = first_sweep(kappa, False, fresh, inner_coef, inner_weight)
    for step in range(1, SWEEPS):
        last = step == SWEEPS - 1
        before = (edge_pv, inner_pv)
        halo = exchange_edges(edge_pv, shape[0])
        inner_pv, *inner_pressure = sweep(kappa, last, False, shape, before, halo, inner_coef, inner_sums)
        edge_pv, *edge_pressure = sweep(kappa, last, True, shape, before, halo, edge_coef, edge_sums)
    pv = (edge_pv, inner_pv)
    halo = exchange_edges(edge_pv, shape[0])
    (inner_new,) = push(kappa, False, pv, halo, fresh, inner_weight, inner_pressure[0], ())
    inner = (inner_pressure[0], inner_new)
    pressure, velocity_new = push(kappa, True, pv, halo, fresh, edge_weight, edge_pressure[0], inner)
    return (pressure, velocity_new)


def solution(mesh):
    return jax.shard_map(
        local,
        mesh=mesh,
        in_specs=(
            P(None, "gx", "gy", None),
            P(None, "gx", "gy", None),
            P("gx", "gy", None),
            P("gx", "gy", None),
            P("gx", "gy"),
            P("gx", "gy"),
        ),
        out_specs=(P("gx", "gy", None), P(None, "gx", "gy", None)),
        check_vma=False,
    )
```

```python
import functools

import jax
import jax.numpy as jnp
from jax import lax
from jax.experimental import pallas as pl
from jax.experimental.pallas import tpu as pltpu
from jax.sharding import PartitionSpec as P

SWEEPS = 4
CFL = 0.25
SPEED_EPS = 1e-06
SOFT = 0.01
CHUNK = 128
VMEM_LIMIT = 16 * 1024 * 1024

X, Y, U, V, VOL, PRES, CODE = range(7)


def call(kernel, **kwargs):
    return pl.pallas_call(
        kernel, compiler_params=pltpu.CompilerParams(vmem_limit_bytes=VMEM_LIMIT), **kwargs
    )


def in_hbm(array):
    return pltpu.with_memory_space_constraint(array, pltpu.HBM)


def once(array):
    return pl.BlockSpec(array.shape, lambda group: (0,) * array.ndim)


def row_index(width):
    return lax.broadcasted_iota(jnp.int32, (8, width), 0)


def split(value):
    high = value.astype(jnp.bfloat16).astype(jnp.float32)
    return jnp.concatenate([high, value - high], axis=0).astype(jnp.bfloat16)


def dot(left, right):
    return jnp.dot(left, right, preferred_element_type=jnp.float32)


def prepare_kernel(position, velocity, volume, pressure, fill, code, old, top):
    rows, cols, width = volume.shape
    slots = lax.broadcasted_iota(jnp.int32, (cols, width), 1)
    most = jnp.zeros((cols, width), jnp.float32)
    for row in range(rows):
        live = (slots < fill[row]).astype(jnp.float32)
        most = jnp.maximum(most, jnp.abs(velocity[0, row]) * live)
        most = jnp.maximum(most, jnp.abs(velocity[1, row]) * live)
        channels = [
            position[0, row],
            position[1, row],
            velocity[0, row],
            velocity[1, row],
            volume[row] * live,
            pressure[row],
            jnp.broadcast_to((code[row] + 1).astype(jnp.float32), (cols, width)),
            jnp.zeros((cols, width), jnp.float32),
        ]
        for channel, value in enumerate(channels):
            old[row, :, channel, :] = value
    top[...] = jnp.broadcast_to(jnp.max(most), top.shape)


def prepare(position, velocity, volume, pressure, fill, code):
    rows, cols, width = volume.shape
    return call(
        prepare_kernel,
        out_shape=(
            pltpu.VMEM((rows, cols, 8, width), jnp.float32),
            pltpu.VMEM((8, width), jnp.float32),
        ),
        name="prepare",
    )(position, velocity, volume, pressure, fill[:, :, None], code[:, :, None])


def neighbours(axis, even, low, high):
    devices = lax.axis_size(axis)

    def swap(value, first):
        pairs = [(i, i + 1) for i in range(first, devices - 1, 2)]
        return lax.ppermute(value, axis, pairs + [(j, i) for i, j in pairs])

    one = swap(jnp.where(even, high, low), 0)
    two = swap(jnp.where(even, low, high), 1)
    return jnp.where(even, two, one), jnp.where(even, one, two)


def exchange_old(even, shard, depth):
    above, below = neighbours("gx", even[0], shard[:depth], shard[-depth:])
    low = jnp.concatenate([above[:, :depth], shard[:, :depth], below[:, :depth]], axis=0)
    high = jnp.concatenate([above[:, -depth:], shard[:, -depth:], below[:, -depth:]], axis=0)
    left, right = neighbours("gy", even[1], low, high)
    return above, below, left, right


def exchange_edges(even, edge, left, right):
    above, below = neighbours("gx", even[0], edge[0][None], edge[1][None])
    low = jnp.concatenate([above[:, :1], left, below[:, :1]], axis=0)
    high = jnp.concatenate([above[:, -1:], right, below[:, -1:]], axis=0)
    return above, below, *neighbours("gy", even[1], low, high)


def groups_of(edge, rows, cols):
    return (3, cols) if edge else (rows - 2, cols - 2)


def first_of(edge, rows, cols):
    return 0 if edge else 3 * cols


def place_of(edge, group, index, rows, cols):
    if not edge:
        return group + 1, index + 1
    half = cols // 2
    left = index < half
    side_row = jnp.minimum(jnp.where(left, index, index - half) + 1, rows - 2)
    side_col = jnp.where(left, 0, cols - 1)
    row = jnp.where(group == 0, 0, jnp.where(group == 1, rows - 1, side_row))
    return row, jnp.where(group == 2, side_col, index)


def join(out, at, edge, inner, rows, cols):
    half = cols // 2
    out[at, at : at + cols] = edge[0]
    out[at + rows - 1, at : at + cols] = edge[1]
    for row in range(1, rows - 1):
        out[at + row, at : at + 1] = edge[2, row - 1 : row]
        out[at + row, at + cols - 1 : at + cols] = edge[2, half + row - 1 : half + row]
        out[at + row, at + 1 : at + cols - 1] = inner[row - 1]


def write_sides(left, right, edge):
    rows, half = left.shape[0], edge.shape[1] // 2
    for out, corner, first in ((left, 0, 0), (right, 2 * half - 1, half)):
        out[0] = edge[0, corner : corner + 1]
        out[rows - 1] = edge[1, corner : corner + 1]
        for row in range(1, rows - 1):
            out[row] = edge[2, first + row - 1 : first + row]


def frame(out, above, below, left, right, rows, cols):
    out[0, 1 : cols + 1] = above[0]
    out[rows + 1, 1 : cols + 1] = below[0]
    for row in range(rows + 2):
        out[row, 0:1] = left[row]
        out[row, cols + 1 : cols + 2] = right[row]


def largest(value):
    for axis in ("gy", "gx"):
        devices = lax.axis_size(axis)
        if devices & (devices - 1):
            value = lax.pmax(value, axis)
            continue
        for bit in range(devices.bit_length() - 1):
            pairs = [(i, i ^ (1 << bit)) for i in range(devices)]
            value = jnp.maximum(value, lax.ppermute(value, axis, pairs))
    return value


def assemble(out, center, above, below, left, right, depth):
    rows, cols = center.shape[:2]
    out[:depth, depth : depth + cols] = above[...]
    out[depth : depth + rows, depth : depth + cols] = center[...]
    out[depth + rows :, depth : depth + cols] = below[...]
    out[:, :depth] = left[...]
    out[:, depth + cols :] = right[...]


def drift_kernel(top, center, above, below, left, right, out, fresh, old):
    rows, cols, _, width = fresh.shape
    assemble(old, center, above, below, left, right, 2)
    step = CFL / (jnp.max(top[...]) + SPEED_EPS)
    index = row_index(width)

    def one_row(row, carry):
        for col in range(cols):
            code = old[row + 1, col + 1, CODE : CODE + 1, :]
            tile = jnp.zeros((8, width), jnp.float32)
            for k in range(9):
                off_x, off_y = k // 3, k % 3
                offset = jnp.where(index == X, off_x - 1.0, jnp.where(index == Y, off_y - 1.0, 0.0))
                source = old[row + off_x, col + off_y] + offset
                tile = jnp.where(code == k + 1.0, source, tile)
            moved = tile + step * pltpu.roll(tile, 6, 0)
            fresh[row, col] = jnp.where(index <= Y, moved, tile)
        return carry

    lax.fori_loop(0, rows, one_row, 0)
    pltpu.sync_copy(fresh, out)


def drift(top, center, above, below, left, right):
    rows, cols, _, width = center.shape
    return call(
        drift_kernel,
        out_specs=pl.BlockSpec(memory_space=pltpu.HBM),
        out_shape=pltpu.HBM((rows + 2, cols + 2, 8, width), jnp.float32),
        scratch_shapes=[pltpu.VMEM((rows + 2, cols + 2, 8, width), jnp.float32), pltpu.VMEM((rows + 4, cols + 4, 8, width), jnp.float32)],
        name="drift",
    )(top, center, above, below, left, right)


def dot_nt(left, right):
    return lax.dot_general(left, right, (((1,), (1,)), ((), ())), preferred_element_type=jnp.float32)


def setup_kernel(source, coef, edge_weight, inner_weight, fresh, xcol, ycol, out_a, out_b, sem):
    pltpu.sync_copy(source, fresh)
    for edge, weight in ((True, edge_weight), (False, inner_weight)):
        setup_list(edge, fresh, coef, weight, xcol, ycol, out_a, out_b, sem)


def setup_list(edge, fresh, coef, weight, xcol, ycol, out_a, out_b, sem):
    groups, size, width, _ = weight.shape
    rows, cols = fresh.shape[0] - 2, fresh.shape[1] - 2
    base = first_of(edge, rows, cols)

    def place(bin_id):
        return place_of(edge, bin_id // size, lax.rem(bin_id, size), rows, cols)

    def columns(bin_id, slot):
        row, col = place(bin_id)
        tile = fresh[row + 1, col + 1]
        xcol[slot] = jnp.broadcast_to(tile[X : X + 1], (width, width)).T
        ycol[slot] = jnp.broadcast_to(tile[Y : Y + 1], (width, width)).T

    def blocks(bin_id, slot, out):
        row, col = place(bin_id)
        values = coef.at[base + bin_id]
        around = [fresh[row + k // 3, col + k % 3] for k in range(9)]
        xj = [jnp.broadcast_to(around[k][X : X + 1] + (k // 3 - 1.0), (8, width)) for k in range(9)]
        yj = [jnp.broadcast_to(around[k][Y : Y + 1] + (k % 3 - 1.0), (8, width)) for k in range(9)]
        for part in range(width // CHUNK):
            span = pl.ds(part * CHUNK, CHUNK)
            spans = [pl.ds(part * CHUNK + 8 * i, 8) for i in range(CHUNK // 8)]
            xi = [xcol[slot, piece] for piece in spans]
            yi = [ycol[slot, piece] for piece in spans]
            for k in range(9):
                lanes = pl.ds(k * width, width)
                squares, weights = [], []
                for x, y in zip(xi, yi):
                    dx = x - xj[k]
                    dy = y - yj[k]
                    square = jnp.maximum(dx * dx + dy * dy, 1e-14)
                    remain = jnp.maximum(1.0 - square * lax.rsqrt(square), 0.0)
                    squares.append(square)
                    weights.append(remain * remain * remain)
                squares = jnp.concatenate(squares, axis=0).astype(jnp.bfloat16)
                weights = jnp.concatenate(weights, axis=0).astype(jnp.bfloat16)
                ratio = squares * pltpu.reciprocal(squares + jnp.bfloat16(SOFT), approx=True)
                out[span, lanes] = weights
                values[span, lanes] = weights * ratio

    def copy_out(bin_id, out, slot):
        target = weight.at[bin_id // size, lax.rem(bin_id, size)]
        return pltpu.make_async_copy(out, target, sem.at[slot])

    count = groups * size
    columns(0, 0)
    columns(1, 1)

    def two_bins(step, carry):
        even = 2 * step

        @pl.when(step > 0)
        def _():
            copy_out(even - 2, out_a, 0).wait()

        blocks(even, 0, out_a)
        columns(jnp.minimum(even + 2, count - 1), 0)
        copy_out(even, out_a, 0).start()

        @pl.when(step > 0)
        def _():
            copy_out(even - 1, out_b, 1).wait()

        blocks(even + 1, 1, out_b)
        columns(jnp.minimum(even + 3, count - 1), 1)
        copy_out(even + 1, out_b, 1).start()
        return carry

    lax.fori_loop(0, count // 2, two_bins, 0)
    copy_out(count - 2, out_a, 0).wait()
    copy_out(count - 1, out_b, 1).wait()


def setup(fresh):
    rows, cols, _, width = fresh.shape
    edge, inner = (groups_of(kind, rows - 2, cols - 2) for kind in (True, False))
    vmem, hbm = pl.BlockSpec(memory_space=pltpu.VMEM), pl.BlockSpec(memory_space=pltpu.HBM)
    return call(
        setup_kernel,
        in_specs=[hbm],
        out_specs=(vmem, hbm, hbm),
        out_shape=(
            pltpu.VMEM((edge[0] * edge[1] + inner[0] * inner[1], width, 9 * width), jnp.bfloat16),
            pltpu.HBM((*edge, width, 9 * width), jnp.bfloat16),
            pltpu.HBM((*inner, width, 9 * width), jnp.bfloat16),
        ),
        scratch_shapes=[
            pltpu.VMEM(fresh.shape, jnp.float32),
            pltpu.VMEM((2, width, width), jnp.float32),
            pltpu.VMEM((2, width, width), jnp.float32),
            pltpu.VMEM((width, 9 * width), jnp.bfloat16),
            pltpu.VMEM((width, 9 * width), jnp.bfloat16),
            pltpu.SemaphoreType.DMA((2,)),
        ],
        name="setup",
    )(in_hbm(fresh))


def first_kernel(kappa, edge, fresh, coef, weight, sums, pv, *rest):
    feat = rest[-1]
    group = pl.program_id(0)
    size, width, _ = weight.shape

    @pl.when(group == 0)
    def _():
        def one_row(r, carry):
            tiles = []
            for col in range(fresh.shape[1]):
                tile = fresh[r, col]
                x, y, u, v = (tile[i : i + 1] for i in range(4))
                vol = tile[VOL : VOL + 1]
                zero = jnp.zeros_like(vol)
                vol_u, vol_v = vol * u, vol * v
                base = [vol, vol * x, vol * y, vol_u, vol_v, vol_u * x + vol_v * y, vol * tile[PRES : PRES + 1], zero]
                along_x = [zero, vol, zero, zero, zero, vol_u, zero, zero]
                along_y = [zero, zero, vol, zero, zero, vol_v, zero, zero]
                tiles.append([jnp.concatenate(rows, axis=0) for rows in (base, along_x, along_y)])
            for col in range(fresh.shape[1]):
                for i in range(3):
                    feat[r, col, i] = tiles[col][i]
            return carry

        lax.fori_loop(0, fresh.shape[0], one_row, 0)

    base = first_of(edge, fresh.shape[0] - 2, fresh.shape[1] - 2)
    outs = ([], [], [], [])
    for index in range(size):
        row, col = place_of(edge, group, index, fresh.shape[0] - 2, fresh.shape[1] - 2)
        around = []
        for k in range(9):
            off_x, off_y = k // 3 - 1, k % 3 - 1
            features = feat[row + k // 3, col + k % 3, 0]
            if off_x:
                features = features + float(off_x) * feat[row + k // 3, col + k % 3, 1]
            if off_y:
                features = features + float(off_y) * feat[row + k // 3, col + k % 3, 2]
            around.append(split(features))
        around = jnp.concatenate(around, axis=1)
        total_w = dot_nt(weight[index], around)
        total_c = dot_nt(coef[base + group * size + index], around)
        total_w = (total_w[:, :8] + total_w[:, 8:]).T
        total_c = (total_c[:, :8] + total_c[:, 8:]).T
        tile = fresh[row + 1, col + 1]
        x, y, u, v = (tile[i : i + 1] for i in range(4))
        vol = tile[VOL : VOL + 1]
        w_0, w_x, w_y, w_u, w_v, w_flow = (total_w[i : i + 1] for i in range(6))
        source = x * w_u + y * w_v - w_flow - (u * x + v * y) * w_0 + u * w_x + v * w_y
        source = kappa * 20.0 * source
        rden = 1.0 / (1.0 + kappa * 40.0 * total_c[0:1])
        first = (source + kappa * 40.0 * total_c[6:7]) * rden
        for out, value in zip(outs, (source, rden, vol, first * vol)):
            out.append(value)
    for place in range(3):
        sums[place, group] = jnp.concatenate(outs[place], axis=0)
    pv[group] = jnp.concatenate(outs[3], axis=0)
    if edge:

        @pl.when(group == 2)
        def _():
            write_sides(*rest[:2], pv)


def first_sweep(kappa, edge, fresh, coef, weight):
    groups, size, width, deep = weight.shape
    rows, cols = fresh.shape[:2]
    vmem = pl.BlockSpec(memory_space=pltpu.VMEM)
    return call(
        functools.partial(first_kernel, kappa, edge),
        grid=(groups,),
        in_specs=[once(fresh), vmem, pl.BlockSpec((None, size, width, deep), lambda group: (group, 0, 0, 0))],
        out_specs=[vmem] * (4 if edge else 2),
        out_shape=[
            pltpu.VMEM((3, groups, size, width), jnp.float32),
            pltpu.VMEM((groups, size, width), jnp.float32),
        ]
        + [pltpu.VMEM((rows - 2, 1, width), jnp.float32)] * (2 if edge else 0),
        scratch_shapes=[pltpu.VMEM((rows, cols, 3, 8, width), jnp.float32)],
        name="first_sweep",
    )(in_hbm(fresh), pltpu.with_memory_space_constraint(coef, pltpu.VMEM), in_hbm(weight))


def sweep_kernel(kappa, last, edge, rows, cols, count, *refs):
    before_edge, before_inner, *halo = refs[: count - 2]
    coef, sums = refs[count - 2 : count]
    pv, *rest = refs[count:-2]
    pressure = rest[-1] if last else None
    ext, tiles = refs[-2:]
    groups, size, width = pv.shape
    base = first_of(edge, rows, cols)
    join(ext, 1, before_edge, before_inner, rows, cols)
    if edge:
        frame(ext, *halo, rows, cols)

    def spread(row, carry):
        for col in range(cols + 2):
            tiles[row, col] = jnp.broadcast_to(ext[row, col : col + 1, :], (16, width)).astype(jnp.bfloat16)
        return carry

    if edge:
        lax.fori_loop(0, rows + 2, spread, 0)
    else:
        lax.fori_loop(1, rows + 1, spread, 0)
    ones = jnp.ones((16, width), jnp.bfloat16)

    def one_group(group, carry):
        totals = []
        for index in range(size):
            row, col = place_of(edge, group, index, rows, cols)
            around = [tiles[row + k // 3, col + k % 3] for k in range(9)]
            parts = []
            for part in range(width // 16):
                total = None
                for k in range(9):
                    term = coef[base + group * size + index, pl.ds(part * 16, 16), pl.ds(k * width, width)] * around[k]
                    total = term if total is None else total + term
                parts.append(total)
            totals.append(dot_nt(ones, jnp.concatenate(parts, axis=0))[0:1])
        total = jnp.concatenate(totals, axis=0)
        value = (sums[0, group] + kappa * 40.0 * total) * sums[1, group]
        vol = sums[2, group]
        pv[group] = value * vol
        if last:
            pressure[group] = jnp.where(vol > 0.0, value, 0.0)
        return carry

    lax.fori_loop(0, groups, one_group, 0)
    if edge:
        write_sides(*rest[:2], pv)


def sweep(kappa, last, edge, shape, pv, halo, coef, sums):
    rows, cols, width = shape
    groups, size = groups_of(edge, rows, cols)
    vmem = pl.BlockSpec(memory_space=pltpu.VMEM)
    out = pltpu.VMEM((groups, size, width), jnp.float32)
    side = pltpu.VMEM((rows, 1, width), jnp.float32)
    outs = [out] + [side] * (2 if edge else 0) + [out] * (1 if last else 0)
    args = (*pv, *(halo if edge else ()), pltpu.with_memory_space_constraint(coef, pltpu.VMEM), sums)
    return call(
        functools.partial(sweep_kernel, kappa, last, edge, rows, cols, len(args)),
        in_specs=[vmem] * len(args),
        out_specs=[vmem] * len(outs),
        out_shape=outs,
        scratch_shapes=[
            pltpu.VMEM((rows + 2, cols + 2, width), jnp.float32),
            pltpu.VMEM((rows + 2, cols + 2, 16, width), jnp.bfloat16),
        ],
        name="sweep",
    )(*args)


def push_kernel(kappa, edge, count, *refs):
    before_edge, before_inner, *halo = refs[: count - (5 if edge else 3)]
    fresh, weight, pressure = refs[count - (5 if edge else 3) : count][:3]
    ext, feat = refs[-2:]
    group = pl.program_id(0)
    size, width, _ = weight.shape
    rows, cols = fresh.shape[0] - 2, fresh.shape[1] - 2

    @pl.when(group == 0)
    def _():
        join(ext, 1, before_edge, before_inner, rows, cols)
        if edge:
            frame(ext, *halo, rows, cols)

        def one_row(r, carry):
            tiles = []
            for col in range(ext.shape[1]):
                value = ext[r, col : col + 1, :]
                tile = fresh[r, col]
                x, y, vol = tile[X : X + 1], tile[Y : Y + 1], tile[VOL : VOL + 1]
                zero = jnp.zeros_like(x)
                tiles.append(jnp.concatenate([value, value * x, value * y, zero, vol, vol * x, vol * y, zero], axis=0))
            for col in range(ext.shape[1]):
                feat[r, col] = tiles[col]
            return carry

        lax.fori_loop(0, rows + 2, one_row, 0)

    feature = row_index(width)
    news = ([], [])
    for index in range(size):
        row, col = place_of(edge, group, index, rows, cols)
        around = []
        for k in range(9):
            tile = feat[row + k // 3, col + k % 3]
            off_x, off_y = k // 3 - 1.0, k % 3 - 1.0
            pv, vol = tile[0:1], tile[4:5]
            if off_x:
                tile = tile + jnp.where(feature == 1, off_x * pv, jnp.where(feature == 5, off_x * vol, 0.0))
            if off_y:
                tile = tile + jnp.where(feature == 2, off_y * pv, jnp.where(feature == 6, off_y * vol, 0.0))
            around.append(split(tile))
        total = dot_nt(weight[index], jnp.concatenate(around, axis=1))
        total = (total[:, :8] + total[:, 8:]).T
        tile = fresh[row + 1, col + 1]
        own = pressure[group, index : index + 1, :]
        alive = tile[VOL : VOL + 1] > 0.0
        for axis in (0, 1):
            at = tile[axis : axis + 1]
            grad = at * total[0:1] - total[1 + axis : 2 + axis] - own * (at * total[4:5] - total[5 + axis : 6 + axis])
            news[axis].append(jnp.where(alive, tile[2 + axis : 3 + axis] + kappa * 20.0 * grad, 0.0))
    if not edge:
        out = refs[count]
        for axis in (0, 1):
            out[axis, group] = jnp.concatenate(news[axis], axis=0)
        return
    inner_pressure, inner_new = refs[count - 2 : count]
    out_pressure, out_new, new = refs[count:-2]
    for axis in (0, 1):
        new[axis, group] = jnp.concatenate(news[axis], axis=0)

    @pl.when(group == 2)
    def _():
        join(out_pressure, 0, pressure, inner_pressure, rows, cols)
        for axis in (0, 1):
            join(out_new.at[axis], 0, new.at[axis], inner_new.at[axis], rows, cols)


def push(kappa, edge, pv, halo, fresh, weight, pressure, inner):
    groups, size, width, deep = weight.shape
    rows, cols = fresh.shape[:2]
    vmem = pl.BlockSpec(memory_space=pltpu.VMEM)
    weight = in_hbm(weight)
    args = (*pv, *(halo if edge else ()), in_hbm(fresh), weight, pressure, *(inner if edge else ()))
    specs = [vmem] * len(args)
    specs[len(pv) + (len(halo) if edge else 0)] = once(fresh)
    specs[len(pv) + (len(halo) if edge else 0) + 1] = pl.BlockSpec(
        (None, size, width, deep), lambda group: (group, 0, 0, 0)
    )
    if edge:
        outs = [
            jax.ShapeDtypeStruct((rows - 2, cols - 2, width), jnp.float32),
            jax.ShapeDtypeStruct((2, rows - 2, cols - 2, width), jnp.float32),
        ]
    else:
        outs = [pltpu.VMEM((2, groups, size, width), jnp.float32)]
    return call(
        functools.partial(push_kernel, kappa, edge, len(args)),
        grid=(groups,),
        in_specs=specs,
        out_specs=[vmem] * len(outs),
        out_shape=outs,
        scratch_shapes=([pltpu.VMEM((2, groups, size, width), jnp.float32)] if edge else [])
        + [
            pltpu.VMEM((rows, cols, width), jnp.float32),
            pltpu.VMEM((rows, cols, 8, width), jnp.float32),
        ],
        name="push",
    )(*args)


def local(position, velocity, volume, pressure_prev, fill, drift_from):
    shape = volume.shape
    kappa = 1.0 / shape[2]
    even = [lax.axis_index(axis) % 2 == 0 for axis in ("gx", "gy")]
    position, even = lax.optimization_barrier((position, even))
    old, top = prepare(position, velocity, volume, pressure_prev, fill, drift_from)
    top = largest(top)
    fresh = drift(top, old, *exchange_old(even, old, 2))
    coef, edge_weight, inner_weight = setup(fresh)
    edge_sums, edge_pv, *sides = first_sweep(kappa, True, fresh, coef, edge_weight)
    inner_sums, inner_pv = first_sweep(kappa, False, fresh, coef, inner_weight)
    for step in range(1, SWEEPS):
        last = step == SWEEPS - 1
        before = (edge_pv, inner_pv)
        halo = exchange_edges(even, edge_pv, *sides)
        inner_pv, *inner_pressure = sweep(kappa, last, False, shape, before, halo, coef, inner_sums)
        edge_pv, *rest = sweep(kappa, last, True, shape, before, halo, coef, edge_sums)
        sides, edge_pressure = rest[:2], rest[2:]
    pv = (edge_pv, inner_pv)
    halo = exchange_edges(even, edge_pv, *sides)
    (inner_new,) = push(kappa, False, pv, halo, fresh, inner_weight, inner_pressure[0], ())
    inner = (inner_pressure[0], inner_new)
    pressure, velocity_new = push(kappa, True, pv, halo, fresh, edge_weight, edge_pressure[0], inner)
    return (pressure, velocity_new)


def solution(mesh):
    return jax.shard_map(
        local,
        mesh=mesh,
        in_specs=(
            P(None, "gx", "gy", None),
            P(None, "gx", "gy", None),
            P("gx", "gy", None),
            P("gx", "gy", None),
            P("gx", "gy"),
            P("gx", "gy"),
        ),
        out_specs=(P("gx", "gy", None), P(None, "gx", "gy", None)),
        check_vma=False,
    )
```

```python
import functools

import jax
import jax.numpy as jnp
from jax import lax
from jax.experimental import pallas as pl
from jax.experimental.pallas import tpu as pltpu
from jax.sharding import PartitionSpec as P

SWEEPS = 4
CFL = 0.25
SPEED_EPS = 1e-06
SOFT = 0.01
CHUNK = 64
VMEM_LIMIT = 16 * 1024 * 1024

X, Y, U, V, VOL, PRES, CODE = range(7)


def call(kernel, **kwargs):
    return pl.pallas_call(
        kernel, compiler_params=pltpu.CompilerParams(vmem_limit_bytes=VMEM_LIMIT), **kwargs
    )


def in_hbm(array):
    return pltpu.with_memory_space_constraint(array, pltpu.HBM)


def once(array):
    return pl.BlockSpec(array.shape, lambda group: (0,) * array.ndim)


def row_index(width):
    return lax.broadcasted_iota(jnp.int32, (8, width), 0)


def split(value):
    high = value.astype(jnp.bfloat16).astype(jnp.float32)
    return jnp.concatenate([high, value - high], axis=0).astype(jnp.bfloat16)


def dot(left, right):
    return jnp.dot(left, right, preferred_element_type=jnp.float32)


def prepare_kernel(position, velocity, volume, pressure, fill, code, old, top):
    rows, cols, width = volume.shape
    slots = lax.broadcasted_iota(jnp.int32, (cols, width), 1)
    most = jnp.zeros((cols, width), jnp.float32)
    for row in range(rows):
        live = (slots < fill[row]).astype(jnp.float32)
        most = jnp.maximum(most, jnp.abs(velocity[0, row]) * live)
        most = jnp.maximum(most, jnp.abs(velocity[1, row]) * live)
        channels = [
            position[0, row],
            position[1, row],
            velocity[0, row],
            velocity[1, row],
            volume[row] * live,
            pressure[row],
            jnp.broadcast_to((code[row] + 1).astype(jnp.float32), (cols, width)),
            jnp.zeros((cols, width), jnp.float32),
        ]
        for channel, value in enumerate(channels):
            old[row, :, channel, :] = value
    top[...] = jnp.broadcast_to(jnp.max(most), top.shape)


def prepare(position, velocity, volume, pressure, fill, code):
    rows, cols, width = volume.shape
    return call(
        prepare_kernel,
        out_shape=(
            pltpu.VMEM((rows, cols, 8, width), jnp.float32),
            pltpu.VMEM((8, width), jnp.float32),
        ),
        name="prepare",
    )(position, velocity, volume, pressure, fill[:, :, None], code[:, :, None])


def neighbours(axis, even, low, high):
    devices = lax.axis_size(axis)

    def swap(value, first):
        pairs = [(i, i + 1) for i in range(first, devices - 1, 2)]
        return lax.ppermute(value, axis, pairs + [(j, i) for i, j in pairs])

    one = swap(jnp.where(even, high, low), 0)
    two = swap(jnp.where(even, low, high), 1)
    return jnp.where(even, two, one), jnp.where(even, one, two)


def exchange_old(even, shard, depth):
    above, below = neighbours("gx", even[0], shard[:depth], shard[-depth:])
    low = jnp.concatenate([above[:, :depth], shard[:, :depth], below[:, :depth]], axis=0)
    high = jnp.concatenate([above[:, -depth:], shard[:, -depth:], below[:, -depth:]], axis=0)
    left, right = neighbours("gy", even[1], low, high)
    return above, below, left, right


def exchange_edges(even, edge, left, right):
    above, below = neighbours("gx", even[0], edge[0][None], edge[1][None])
    low = jnp.concatenate([above[:, :1], left, below[:, :1]], axis=0)
    high = jnp.concatenate([above[:, -1:], right, below[:, -1:]], axis=0)
    return above, below, *neighbours("gy", even[1], low, high)


def groups_of(edge, rows, cols):
    return (3, cols) if edge else (rows - 2, cols - 2)


def first_of(edge, rows, cols):
    return 0 if edge else 3 * cols


def place_of(edge, group, index, rows, cols):
    if not edge:
        return group + 1, index + 1
    half = cols // 2
    left = index < half
    side_row = jnp.minimum(jnp.where(left, index, index - half) + 1, rows - 2)
    side_col = jnp.where(left, 0, cols - 1)
    row = jnp.where(group == 0, 0, jnp.where(group == 1, rows - 1, side_row))
    return row, jnp.where(group == 2, side_col, index)


def join(out, at, edge, inner, rows, cols):
    half = cols // 2
    out[at, at : at + cols] = edge[0]
    out[at + rows - 1, at : at + cols] = edge[1]
    for row in range(1, rows - 1):
        out[at + row, at : at + 1] = edge[2, row - 1 : row]
        out[at + row, at + cols - 1 : at + cols] = edge[2, half + row - 1 : half + row]
        out[at + row, at + 1 : at + cols - 1] = inner[row - 1]


def write_sides(left, right, edge):
    rows, half = left.shape[0], edge.shape[1] // 2
    for out, corner, first in ((left, 0, 0), (right, 2 * half - 1, half)):
        out[0] = edge[0, corner : corner + 1]
        out[rows - 1] = edge[1, corner : corner + 1]
        for row in range(1, rows - 1):
            out[row] = edge[2, first + row - 1 : first + row]


def frame(out, above, below, left, right, rows, cols):
    out[0, 1 : cols + 1] = above[0]
    out[rows + 1, 1 : cols + 1] = below[0]
    for row in range(rows + 2):
        out[row, 0:1] = left[row]
        out[row, cols + 1 : cols + 2] = right[row]


def largest(value):
    for axis in ("gy", "gx"):
        devices = lax.axis_size(axis)
        if devices & (devices - 1):
            value = lax.pmax(value, axis)
            continue
        for bit in range(devices.bit_length() - 1):
            pairs = [(i, i ^ (1 << bit)) for i in range(devices)]
            value = jnp.maximum(value, lax.ppermute(value, axis, pairs))
    return value


def assemble(out, center, above, below, left, right, depth):
    rows, cols = center.shape[:2]
    out[:depth, depth : depth + cols] = above[...]
    out[depth : depth + rows, depth : depth + cols] = center[...]
    out[depth + rows :, depth : depth + cols] = below[...]
    out[:, :depth] = left[...]
    out[:, depth + cols :] = right[...]


def drift_kernel(top, center, above, below, left, right, out, fresh, old):
    rows, cols, _, width = fresh.shape
    assemble(old, center, above, below, left, right, 2)
    step = CFL / (jnp.max(top[...]) + SPEED_EPS)
    index = row_index(width)

    def one_row(row, carry):
        for col in range(cols):
            code = old[row + 1, col + 1, CODE : CODE + 1, :]
            tile = jnp.zeros((8, width), jnp.float32)
            for k in range(9):
                off_x, off_y = k // 3, k % 3
                offset = jnp.where(index == X, off_x - 1.0, jnp.where(index == Y, off_y - 1.0, 0.0))
                source = old[row + off_x, col + off_y] + offset
                tile = jnp.where(code == k + 1.0, source, tile)
            moved = tile + step * pltpu.roll(tile, 6, 0)
            fresh[row, col] = jnp.where(index <= Y, moved, tile)
        return carry

    lax.fori_loop(0, rows, one_row, 0)
    pltpu.sync_copy(fresh, out)


def drift(top, center, above, below, left, right):
    rows, cols, _, width = center.shape
    return call(
        drift_kernel,
        out_specs=pl.BlockSpec(memory_space=pltpu.HBM),
        out_shape=pltpu.HBM((rows + 2, cols + 2, 8, width), jnp.float32),
        scratch_shapes=[pltpu.VMEM((rows + 2, cols + 2, 8, width), jnp.float32), pltpu.VMEM((rows + 4, cols + 4, 8, width), jnp.float32)],
        name="drift",
    )(top, center, above, below, left, right)


def dot_nt(left, right):
    return lax.dot_general(left, right, (((1,), (1,)), ((), ())), preferred_element_type=jnp.float32)


def setup_kernel(source, coef, edge_weight, inner_weight, fresh, out_a, out_b, sem):
    pltpu.sync_copy(source, fresh)
    for edge, weight in ((True, edge_weight), (False, inner_weight)):
        setup_list(edge, fresh, coef, weight, out_a, out_b, sem)


def setup_list(edge, fresh, coef, weight, out_a, out_b, sem):
    groups, size, width, _ = weight.shape
    rows, cols = fresh.shape[0] - 2, fresh.shape[1] - 2
    base = first_of(edge, rows, cols)

    def place(bin_id):
        return place_of(edge, bin_id // size, lax.rem(bin_id, size), rows, cols)

    index = row_index(width)

    def three_parts(tile):
        high = tile.astype(jnp.bfloat16).astype(jnp.float32)
        rest = tile - high
        middle = rest.astype(jnp.bfloat16).astype(jnp.float32)
        return high, middle, rest - middle

    def with_square(tile, off_x, off_y):
        if off_x or off_y:
            tile = tile + jnp.where(index == X, off_x, jnp.where(index == Y, off_y, 0.0))
        square = tile * tile
        square = pltpu.roll(square, 2, 0) + pltpu.roll(square, 1, 0)
        return jnp.where(index < 2, tile, jnp.where(index == 2, square, jnp.where(index == 3, 1.0, 0.0)))

    def blocks(bin_id, out):
        row, col = place(bin_id)
        values = coef.at[base + bin_id]
        own = with_square(fresh[row + 1, col + 1], 0.0, 0.0)
        swapped = jnp.where(index == 2, pltpu.roll(own, 7, 0), pltpu.roll(own, 1, 0))
        own = jnp.where(index < 2, -2.0 * own, jnp.where(index < 4, swapped, 0.0))
        high, middle, low = three_parts(own)
        own = jnp.concatenate([high, high, middle, high, low, middle], axis=0).T.astype(jnp.bfloat16)
        for first in range(0, 9, 2):
            codes = range(first, min(first + 2, 9))
            around = []
            for k in codes:
                high, middle, low = three_parts(
                    with_square(fresh[row + k // 3, col + k % 3], k // 3 - 1.0, k % 3 - 1.0)
                )
                around.append(jnp.concatenate([high, middle, high, low, high, middle], axis=0))
            distance = dot(own, jnp.concatenate(around, axis=1).astype(jnp.bfloat16))
            for k in codes:
                lanes = pl.ds(k * width, width)
                for part in range(width // CHUNK):
                    span = pl.ds(part * CHUNK, CHUNK)
                    at = (k - first) * width
                    square = distance[part * CHUNK : (part + 1) * CHUNK, at : at + width]
                    square = jnp.maximum(square, 1e-14)
                    remain = jnp.maximum(1.0 - square * lax.rsqrt(square), 0.0)
                    weights = (remain * remain * remain).astype(jnp.bfloat16)
                    square = square.astype(jnp.bfloat16)
                    ratio = square * pltpu.reciprocal(square + jnp.bfloat16(SOFT), approx=True)
                    out[span, lanes] = weights
                    values[span, lanes] = weights * ratio

    def copy_out(bin_id, out, slot):
        target = weight.at[bin_id // size, lax.rem(bin_id, size)]
        return pltpu.make_async_copy(out, target, sem.at[slot])

    count = groups * size

    def two_bins(step, carry):
        even = 2 * step

        @pl.when(step > 0)
        def _():
            copy_out(even - 2, out_a, 0).wait()

        blocks(even, out_a)
        copy_out(even, out_a, 0).start()

        @pl.when(step > 0)
        def _():
            copy_out(even - 1, out_b, 1).wait()

        blocks(even + 1, out_b)
        copy_out(even + 1, out_b, 1).start()
        return carry

    lax.fori_loop(0, count // 2, two_bins, 0)
    copy_out(count - 2, out_a, 0).wait()
    copy_out(count - 1, out_b, 1).wait()


def setup(fresh):
    rows, cols, _, width = fresh.shape
    edge, inner = (groups_of(kind, rows - 2, cols - 2) for kind in (True, False))
    vmem, hbm = pl.BlockSpec(memory_space=pltpu.VMEM), pl.BlockSpec(memory_space=pltpu.HBM)
    return call(
        setup_kernel,
        in_specs=[hbm],
        out_specs=(vmem, hbm, hbm),
        out_shape=(
            pltpu.VMEM((edge[0] * edge[1] + inner[0] * inner[1], width, 9 * width), jnp.bfloat16),
            pltpu.HBM((*edge, width, 9 * width), jnp.bfloat16),
            pltpu.HBM((*inner, width, 9 * width), jnp.bfloat16),
        ),
        scratch_shapes=[
            pltpu.VMEM(fresh.shape, jnp.float32),
            pltpu.VMEM((width, 9 * width), jnp.bfloat16),
            pltpu.VMEM((width, 9 * width), jnp.bfloat16),
            pltpu.SemaphoreType.DMA((2,)),
        ],
        name="setup",
    )(in_hbm(fresh))


def first_kernel(kappa, edge, fresh, coef, weight, sums, pv, *rest):
    feat = rest[-1]
    group = pl.program_id(0)
    size, width, _ = weight.shape

    @pl.when(group == 0)
    def _():
        def one_row(r, carry):
            tiles = []
            for col in range(fresh.shape[1]):
                tile = fresh[r, col]
                x, y, u, v = (tile[i : i + 1] for i in range(4))
                vol = tile[VOL : VOL + 1]
                zero = jnp.zeros_like(vol)
                vol_u, vol_v = vol * u, vol * v
                base = [vol, vol * x, vol * y, vol_u, vol_v, vol_u * x + vol_v * y, vol * tile[PRES : PRES + 1], zero]
                along_x = [zero, vol, zero, zero, zero, vol_u, zero, zero]
                along_y = [zero, zero, vol, zero, zero, vol_v, zero, zero]
                tiles.append([jnp.concatenate(rows, axis=0) for rows in (base, along_x, along_y)])
            for col in range(fresh.shape[1]):
                for i in range(3):
                    feat[r, col, i] = tiles[col][i]
            return carry

        lax.fori_loop(0, fresh.shape[0], one_row, 0)

    base = first_of(edge, fresh.shape[0] - 2, fresh.shape[1] - 2)
    outs = ([], [], [], [])
    for index in range(size):
        row, col = place_of(edge, group, index, fresh.shape[0] - 2, fresh.shape[1] - 2)
        around = []
        for k in range(9):
            off_x, off_y = k // 3 - 1, k % 3 - 1
            features = feat[row + k // 3, col + k % 3, 0]
            if off_x:
                features = features + float(off_x) * feat[row + k // 3, col + k % 3, 1]
            if off_y:
                features = features + float(off_y) * feat[row + k // 3, col + k % 3, 2]
            around.append(split(features))
        around = jnp.concatenate(around, axis=1)
        total_w = dot_nt(weight[index], around)
        total_c = dot_nt(coef[base + group * size + index], around)
        total_w = (total_w[:, :8] + total_w[:, 8:]).T
        total_c = (total_c[:, :8] + total_c[:, 8:]).T
        tile = fresh[row + 1, col + 1]
        x, y, u, v = (tile[i : i + 1] for i in range(4))
        vol = tile[VOL : VOL + 1]
        w_0, w_x, w_y, w_u, w_v, w_flow = (total_w[i : i + 1] for i in range(6))
        source = x * w_u + y * w_v - w_flow - (u * x + v * y) * w_0 + u * w_x + v * w_y
        source = kappa * 20.0 * source
        rden = 1.0 / (1.0 + kappa * 40.0 * total_c[0:1])
        first = (source + kappa * 40.0 * total_c[6:7]) * rden
        for out, value in zip(outs, (source, rden, vol, first * vol)):
            out.append(value)
    for place in range(3):
        sums[place, group] = jnp.concatenate(outs[place], axis=0)
    pv[group] = jnp.concatenate(outs[3], axis=0)
    if edge:

        @pl.when(group == 2)
        def _():
            write_sides(*rest[:2], pv)


def first_sweep(kappa, edge, fresh, coef, weight):
    groups, size, width, deep = weight.shape
    rows, cols = fresh.shape[:2]
    vmem = pl.BlockSpec(memory_space=pltpu.VMEM)
    return call(
        functools.partial(first_kernel, kappa, edge),
        grid=(groups,),
        in_specs=[once(fresh), vmem, pl.BlockSpec((None, size, width, deep), lambda group: (group, 0, 0, 0))],
        out_specs=[vmem] * (4 if edge else 2),
        out_shape=[
            pltpu.VMEM((3, groups, size, width), jnp.float32),
            pltpu.VMEM((groups, size, width), jnp.float32),
        ]
        + [pltpu.VMEM((rows - 2, 1, width), jnp.float32)] * (2 if edge else 0),
        scratch_shapes=[pltpu.VMEM((rows, cols, 3, 8, width), jnp.float32)],
        name="first_sweep",
    )(in_hbm(fresh), pltpu.with_memory_space_constraint(coef, pltpu.VMEM), in_hbm(weight))


def sweep_kernel(kappa, last, edge, rows, cols, count, *refs):
    before_edge, before_inner, *halo = refs[: count - 2]
    coef, sums = refs[count - 2 : count]
    pv, *rest = refs[count:-2]
    pressure = rest[-1] if last else None
    ext, tiles = refs[-2:]
    groups, size, width = pv.shape
    base = first_of(edge, rows, cols)
    join(ext, 1, before_edge, before_inner, rows, cols)
    if edge:
        frame(ext, *halo, rows, cols)

    def spread(row, carry):
        for col in range(cols + 2):
            tiles[row, col] = jnp.broadcast_to(ext[row, col : col + 1, :], (16, width)).astype(jnp.bfloat16)
        return carry

    if edge:
        lax.fori_loop(0, rows + 2, spread, 0)
    else:
        lax.fori_loop(1, rows + 1, spread, 0)
    ones = jnp.ones((16, width), jnp.bfloat16)

    def one_group(group, carry):
        totals = []
        for index in range(size):
            row, col = place_of(edge, group, index, rows, cols)
            around = [tiles[row + k // 3, col + k % 3] for k in range(9)]
            parts = []
            for part in range(width // 16):
                total = None
                for k in range(9):
                    term = coef[base + group * size + index, pl.ds(part * 16, 16), pl.ds(k * width, width)] * around[k]
                    total = term if total is None else total + term
                parts.append(total)
            totals.append(dot_nt(ones, jnp.concatenate(parts, axis=0))[0:1])
        total = jnp.concatenate(totals, axis=0)
        value = (sums[0, group] + kappa * 40.0 * total) * sums[1, group]
        vol = sums[2, group]
        pv[group] = value * vol
        if last:
            pressure[group] = jnp.where(vol > 0.0, value, 0.0)
        return carry

    lax.fori_loop(0, groups, one_group, 0)
    if edge:
        write_sides(*rest[:2], pv)


def sweep(kappa, last, edge, shape, pv, halo, coef, sums):
    rows, cols, width = shape
    groups, size = groups_of(edge, rows, cols)
    vmem = pl.BlockSpec(memory_space=pltpu.VMEM)
    out = pltpu.VMEM((groups, size, width), jnp.float32)
    side = pltpu.VMEM((rows, 1, width), jnp.float32)
    outs = [out] + [side] * (2 if edge else 0) + [out] * (1 if last else 0)
    args = (*pv, *(halo if edge else ()), pltpu.with_memory_space_constraint(coef, pltpu.VMEM), sums)
    return call(
        functools.partial(sweep_kernel, kappa, last, edge, rows, cols, len(args)),
        in_specs=[vmem] * len(args),
        out_specs=[vmem] * len(outs),
        out_shape=outs,
        scratch_shapes=[
            pltpu.VMEM((rows + 2, cols + 2, width), jnp.float32),
            pltpu.VMEM((rows + 2, cols + 2, 16, width), jnp.bfloat16),
        ],
        name="sweep",
    )(*args)


def push_kernel(kappa, edge, count, *refs):
    before_edge, before_inner, *halo = refs[: count - (5 if edge else 3)]
    fresh, weight, pressure = refs[count - (5 if edge else 3) : count][:3]
    ext, feat = refs[-2:]
    group = pl.program_id(0)
    size, width, _ = weight.shape
    rows, cols = fresh.shape[0] - 2, fresh.shape[1] - 2

    @pl.when(group == 0)
    def _():
        join(ext, 1, before_edge, before_inner, rows, cols)
        if edge:
            frame(ext, *halo, rows, cols)

        def one_row(r, carry):
            tiles = []
            for col in range(ext.shape[1]):
                value = ext[r, col : col + 1, :]
                tile = fresh[r, col]
                x, y, vol = tile[X : X + 1], tile[Y : Y + 1], tile[VOL : VOL + 1]
                zero = jnp.zeros_like(x)
                tiles.append(jnp.concatenate([value, value * x, value * y, zero, vol, vol * x, vol * y, zero], axis=0))
            for col in range(ext.shape[1]):
                feat[r, col] = tiles[col]
            return carry

        lax.fori_loop(0, rows + 2, one_row, 0)

    feature = row_index(width)
    news = ([], [])
    for index in range(size):
        row, col = place_of(edge, group, index, rows, cols)
        around = []
        for k in range(9):
            tile = feat[row + k // 3, col + k % 3]
            off_x, off_y = k // 3 - 1.0, k % 3 - 1.0
            pv, vol = tile[0:1], tile[4:5]
            if off_x:
                tile = tile + jnp.where(feature == 1, off_x * pv, jnp.where(feature == 5, off_x * vol, 0.0))
            if off_y:
                tile = tile + jnp.where(feature == 2, off_y * pv, jnp.where(feature == 6, off_y * vol, 0.0))
            around.append(split(tile))
        total = dot_nt(weight[index], jnp.concatenate(around, axis=1))
        total = (total[:, :8] + total[:, 8:]).T
        tile = fresh[row + 1, col + 1]
        own = pressure[group, index : index + 1, :]
        alive = tile[VOL : VOL + 1] > 0.0
        for axis in (0, 1):
            at = tile[axis : axis + 1]
            grad = at * total[0:1] - total[1 + axis : 2 + axis] - own * (at * total[4:5] - total[5 + axis : 6 + axis])
            news[axis].append(jnp.where(alive, tile[2 + axis : 3 + axis] + kappa * 20.0 * grad, 0.0))
    if not edge:
        out = refs[count]
        for axis in (0, 1):
            out[axis, group] = jnp.concatenate(news[axis], axis=0)
        return
    inner_pressure, inner_new = refs[count - 2 : count]
    out_pressure, out_new, new = refs[count:-2]
    for axis in (0, 1):
        new[axis, group] = jnp.concatenate(news[axis], axis=0)

    @pl.when(group == 2)
    def _():
        join(out_pressure, 0, pressure, inner_pressure, rows, cols)
        for axis in (0, 1):
            join(out_new.at[axis], 0, new.at[axis], inner_new.at[axis], rows, cols)


def push(kappa, edge, pv, halo, fresh, weight, pressure, inner):
    groups, size, width, deep = weight.shape
    rows, cols = fresh.shape[:2]
    vmem = pl.BlockSpec(memory_space=pltpu.VMEM)
    weight = in_hbm(weight)
    args = (*pv, *(halo if edge else ()), in_hbm(fresh), weight, pressure, *(inner if edge else ()))
    specs = [vmem] * len(args)
    specs[len(pv) + (len(halo) if edge else 0)] = once(fresh)
    specs[len(pv) + (len(halo) if edge else 0) + 1] = pl.BlockSpec(
        (None, size, width, deep), lambda group: (group, 0, 0, 0)
    )
    if edge:
        outs = [
            jax.ShapeDtypeStruct((rows - 2, cols - 2, width), jnp.float32),
            jax.ShapeDtypeStruct((2, rows - 2, cols - 2, width), jnp.float32),
        ]
    else:
        outs = [pltpu.VMEM((2, groups, size, width), jnp.float32)]
    return call(
        functools.partial(push_kernel, kappa, edge, len(args)),
        grid=(groups,),
        in_specs=specs,
        out_specs=[vmem] * len(outs),
        out_shape=outs,
        scratch_shapes=([pltpu.VMEM((2, groups, size, width), jnp.float32)] if edge else [])
        + [
            pltpu.VMEM((rows, cols, width), jnp.float32),
            pltpu.VMEM((rows, cols, 8, width), jnp.float32),
        ],
        name="push",
    )(*args)


def local(position, velocity, volume, pressure_prev, fill, drift_from):
    shape = volume.shape
    kappa = 1.0 / shape[2]
    even = [lax.axis_index(axis) % 2 == 0 for axis in ("gx", "gy")]
    position, even = lax.optimization_barrier((position, even))
    old, top = prepare(position, velocity, volume, pressure_prev, fill, drift_from)
    top = largest(top)
    fresh = drift(top, old, *exchange_old(even, old, 2))
    coef, edge_weight, inner_weight = setup(fresh)
    edge_sums, edge_pv, *sides = first_sweep(kappa, True, fresh, coef, edge_weight)
    inner_sums, inner_pv = first_sweep(kappa, False, fresh, coef, inner_weight)
    for step in range(1, SWEEPS):
        last = step == SWEEPS - 1
        before = (edge_pv, inner_pv)
        halo = exchange_edges(even, edge_pv, *sides)
        inner_pv, *inner_pressure = sweep(kappa, last, False, shape, before, halo, coef, inner_sums)
        edge_pv, *rest = sweep(kappa, last, True, shape, before, halo, coef, edge_sums)
        sides, edge_pressure = rest[:2], rest[2:]
    pv = (edge_pv, inner_pv)
    halo = exchange_edges(even, edge_pv, *sides)
    (inner_new,) = push(kappa, False, pv, halo, fresh, inner_weight, inner_pressure[0], ())
    inner = (inner_pressure[0], inner_new)
    pressure, velocity_new = push(kappa, True, pv, halo, fresh, edge_weight, edge_pressure[0], inner)
    return (pressure, velocity_new)


def solution(mesh):
    return jax.shard_map(
        local,
        mesh=mesh,
        in_specs=(
            P(None, "gx", "gy", None),
            P(None, "gx", "gy", None),
            P("gx", "gy", None),
            P("gx", "gy", None),
            P("gx", "gy"),
            P("gx", "gy"),
        ),
        out_specs=(P("gx", "gy", None), P(None, "gx", "gy", None)),
        check_vma=False,
    )
```

```python
import functools

import jax
import jax.numpy as jnp
from jax import lax
from jax.experimental import pallas as pl
from jax.experimental.pallas import tpu as pltpu
from jax.sharding import PartitionSpec as P

SWEEPS = 4
CFL = 0.25
SPEED_EPS = 1e-06
SOFT = 0.01
CHUNK = 64
VMEM_LIMIT = 16 * 1024 * 1024

X, Y, U, V, VOL, PRES, CODE = range(7)


def call(kernel, **kwargs):
    return pl.pallas_call(
        kernel, compiler_params=pltpu.CompilerParams(vmem_limit_bytes=VMEM_LIMIT), **kwargs
    )


def in_hbm(array):
    return pltpu.with_memory_space_constraint(array, pltpu.HBM)


def once(array):
    return pl.BlockSpec(array.shape, lambda group: (0,) * array.ndim)


def side_by_side(blocks):
    return jnp.concatenate([blocks[k] for k in range(9)], axis=1)


def row_index(width):
    return lax.broadcasted_iota(jnp.int32, (8, width), 0)


def split(value):
    high = value.astype(jnp.bfloat16).astype(jnp.float32)
    return jnp.concatenate([high, value - high], axis=0).astype(jnp.bfloat16)


def dot(left, right):
    return jnp.dot(left, right, preferred_element_type=jnp.float32)


def prepare_kernel(position, velocity, volume, pressure, fill, code, old, top):
    rows, cols, width = volume.shape
    slots = lax.broadcasted_iota(jnp.int32, (cols, width), 1)
    most = jnp.zeros((cols, width), jnp.float32)
    for row in range(rows):
        live = (slots < fill[row]).astype(jnp.float32)
        most = jnp.maximum(most, jnp.abs(velocity[0, row]) * live)
        most = jnp.maximum(most, jnp.abs(velocity[1, row]) * live)
        channels = [
            position[0, row],
            position[1, row],
            velocity[0, row],
            velocity[1, row],
            volume[row] * live,
            pressure[row],
            jnp.broadcast_to((code[row] + 1).astype(jnp.float32), (cols, width)),
            jnp.zeros((cols, width), jnp.float32),
        ]
        for channel, value in enumerate(channels):
            old[row, :, channel, :] = value
    top[...] = jnp.broadcast_to(jnp.max(most), top.shape)


def prepare(position, velocity, volume, pressure, fill, code):
    rows, cols, width = volume.shape
    return call(
        prepare_kernel,
        out_shape=(
            pltpu.VMEM((rows, cols, 8, width), jnp.float32),
            pltpu.VMEM((8, width), jnp.float32),
        ),
        name="prepare",
    )(position, velocity, volume, pressure, fill[:, :, None], code[:, :, None])


def neighbours(axis, even, low, high):
    devices = lax.axis_size(axis)

    def swap(value, first):
        pairs = [(i, i + 1) for i in range(first, devices - 1, 2)]
        return lax.ppermute(value, axis, pairs + [(j, i) for i, j in pairs])

    one = swap(jnp.where(even, high, low), 0)
    two = swap(jnp.where(even, low, high), 1)
    return jnp.where(even, two, one), jnp.where(even, one, two)


def exchange_old(even, shard, depth):
    above, below = neighbours("gx", even[0], shard[:depth], shard[-depth:])
    low = jnp.concatenate([above[:, :depth], shard[:, :depth], below[:, :depth]], axis=0)
    high = jnp.concatenate([above[:, -depth:], shard[:, -depth:], below[:, -depth:]], axis=0)
    left, right = neighbours("gy", even[1], low, high)
    return above, below, left, right


def exchange_edges(even, edge, left, right):
    above, below = neighbours("gx", even[0], edge[0][None], edge[1][None])
    low = jnp.concatenate([above[:, :1], left, below[:, :1]], axis=0)
    high = jnp.concatenate([above[:, -1:], right, below[:, -1:]], axis=0)
    return above, below, *neighbours("gy", even[1], low, high)


def groups_of(edge, rows, cols):
    return (3, cols) if edge else (rows - 2, cols - 2)


def first_of(edge, rows, cols):
    return 0 if edge else 3 * cols


def place_of(edge, group, index, rows, cols):
    if not edge:
        return group + 1, index + 1
    half = cols // 2
    left = index < half
    side_row = jnp.minimum(jnp.where(left, index, index - half) + 1, rows - 2)
    side_col = jnp.where(left, 0, cols - 1)
    row = jnp.where(group == 0, 0, jnp.where(group == 1, rows - 1, side_row))
    return row, jnp.where(group == 2, side_col, index)


def join(out, at, edge, inner, rows, cols):
    half = cols // 2
    out[at, at : at + cols] = edge[0]
    out[at + rows - 1, at : at + cols] = edge[1]
    for row in range(1, rows - 1):
        out[at + row, at : at + 1] = edge[2, row - 1 : row]
        out[at + row, at + cols - 1 : at + cols] = edge[2, half + row - 1 : half + row]
        out[at + row, at + 1 : at + cols - 1] = inner[row - 1]


def write_sides(left, right, edge):
    rows, half = left.shape[0], edge.shape[1] // 2
    for out, corner, first in ((left, 0, 0), (right, 2 * half - 1, half)):
        out[0] = edge[0, corner : corner + 1]
        out[rows - 1] = edge[1, corner : corner + 1]
        for row in range(1, rows - 1):
            out[row] = edge[2, first + row - 1 : first + row]


def frame(out, above, below, left, right, rows, cols):
    out[0, 1 : cols + 1] = above[0]
    out[rows + 1, 1 : cols + 1] = below[0]
    for row in range(rows + 2):
        out[row, 0:1] = left[row]
        out[row, cols + 1 : cols + 2] = right[row]


def largest(value):
    for axis in ("gy", "gx"):
        devices = lax.axis_size(axis)
        if devices & (devices - 1):
            value = lax.pmax(value, axis)
            continue
        for bit in range(devices.bit_length() - 1):
            pairs = [(i, i ^ (1 << bit)) for i in range(devices)]
            value = jnp.maximum(value, lax.ppermute(value, axis, pairs))
    return value


def assemble(out, center, above, below, left, right, depth):
    rows, cols = center.shape[:2]
    out[:depth, depth : depth + cols] = above[...]
    out[depth : depth + rows, depth : depth + cols] = center[...]
    out[depth + rows :, depth : depth + cols] = below[...]
    out[:, :depth] = left[...]
    out[:, depth + cols :] = right[...]


def drift_kernel(top, center, above, below, left, right, out, fresh, old):
    rows, cols, _, width = fresh.shape
    assemble(old, center, above, below, left, right, 2)
    step = CFL / (jnp.max(top[...]) + SPEED_EPS)
    index = row_index(width)

    def one_row(row, carry):
        for col in range(cols):
            code = old[row + 1, col + 1, CODE : CODE + 1, :]
            tile = jnp.zeros((8, width), jnp.float32)
            for k in range(9):
                off_x, off_y = k // 3, k % 3
                offset = jnp.where(index == X, off_x - 1.0, jnp.where(index == Y, off_y - 1.0, 0.0))
                source = old[row + off_x, col + off_y] + offset
                tile = jnp.where(code == k + 1.0, source, tile)
            moved = tile + step * pltpu.roll(tile, 6, 0)
            fresh[row, col] = jnp.where(index <= Y, moved, tile)
        return carry

    lax.fori_loop(0, rows, one_row, 0)
    pltpu.sync_copy(fresh, out)


def drift(top, center, above, below, left, right):
    rows, cols, _, width = center.shape
    return call(
        drift_kernel,
        out_specs=pl.BlockSpec(memory_space=pltpu.HBM),
        out_shape=pltpu.HBM((rows + 2, cols + 2, 8, width), jnp.float32),
        scratch_shapes=[pltpu.VMEM((rows + 2, cols + 2, 8, width), jnp.float32), pltpu.VMEM((rows + 4, cols + 4, 8, width), jnp.float32)],
        name="drift",
    )(top, center, above, below, left, right)


def dot_nt(left, right):
    return lax.dot_general(left, right, (((1,), (1,)), ((), ())), preferred_element_type=jnp.float32)


def setup_kernel(source, coef, edge_weight, inner_weight, fresh, xcol, ycol, out_a, out_b, sem):
    pltpu.sync_copy(source, fresh)
    for edge, weight in ((True, edge_weight), (False, inner_weight)):
        setup_list(edge, fresh, coef, weight, xcol, ycol, out_a, out_b, sem)


def setup_list(edge, fresh, coef, weight, xcol, ycol, out_a, out_b, sem):
    groups, size, _, width, _ = weight.shape
    rows, cols = fresh.shape[0] - 2, fresh.shape[1] - 2
    base = first_of(edge, rows, cols)

    def place(bin_id):
        return place_of(edge, bin_id // size, lax.rem(bin_id, size), rows, cols)

    def columns(bin_id, slot):
        row, col = place(bin_id)
        tile = fresh[row + 1, col + 1]
        xcol[slot] = jnp.broadcast_to(tile[X : X + 1], (width, width)).T
        ycol[slot] = jnp.broadcast_to(tile[Y : Y + 1], (width, width)).T

    def blocks(bin_id, slot, out):
        row, col = place(bin_id)
        values = coef.at[base + bin_id]
        around = [fresh[row + k // 3, col + k % 3] for k in range(9)]
        xj = [jnp.broadcast_to(around[k][X : X + 1] + (k // 3 - 1.0), (8, width)) for k in range(9)]
        yj = [jnp.broadcast_to(around[k][Y : Y + 1] + (k % 3 - 1.0), (8, width)) for k in range(9)]
        for part in range(width // CHUNK):
            span = pl.ds(part * CHUNK, CHUNK)
            spans = [pl.ds(part * CHUNK + 8 * i, 8) for i in range(CHUNK // 8)]
            xi = [xcol[slot, piece] for piece in spans]
            yi = [ycol[slot, piece] for piece in spans]
            for k in range(9):
                squares, weights = [], []
                for x, y in zip(xi, yi):
                    dx = x - xj[k]
                    dy = y - yj[k]
                    square = jnp.maximum(dx * dx + dy * dy, 1e-14)
                    remain = jnp.maximum(1.0 - square * lax.rsqrt(square), 0.0)
                    squares.append(square)
                    weights.append(remain * remain * remain)
                squares = jnp.concatenate(squares, axis=0).astype(jnp.bfloat16)
                weights = jnp.concatenate(weights, axis=0).astype(jnp.bfloat16)
                ratio = squares * pltpu.reciprocal(squares + jnp.bfloat16(SOFT), approx=True)
                out[k, span] = weights
                values[k, span] = weights * ratio

    def copy_out(bin_id, out, slot):
        target = weight.at[bin_id // size, lax.rem(bin_id, size)]
        return pltpu.make_async_copy(out, target, sem.at[slot])

    count = groups * size
    columns(0, 0)
    columns(1, 1)

    def two_bins(step, carry):
        even = 2 * step

        @pl.when(step > 0)
        def _():
            copy_out(even - 2, out_a, 0).wait()

        blocks(even, 0, out_a)
        columns(jnp.minimum(even + 2, count - 1), 0)
        copy_out(even, out_a, 0).start()

        @pl.when(step > 0)
        def _():
            copy_out(even - 1, out_b, 1).wait()

        blocks(even + 1, 1, out_b)
        columns(jnp.minimum(even + 3, count - 1), 1)
        copy_out(even + 1, out_b, 1).start()
        return carry

    lax.fori_loop(0, count // 2, two_bins, 0)
    copy_out(count - 2, out_a, 0).wait()
    copy_out(count - 1, out_b, 1).wait()


def setup(fresh):
    rows, cols, _, width = fresh.shape
    edge, inner = (groups_of(kind, rows - 2, cols - 2) for kind in (True, False))
    vmem, hbm = pl.BlockSpec(memory_space=pltpu.VMEM), pl.BlockSpec(memory_space=pltpu.HBM)
    return call(
        setup_kernel,
        in_specs=[hbm],
        out_specs=(vmem, hbm, hbm),
        out_shape=(
            pltpu.VMEM((edge[0] * edge[1] + inner[0] * inner[1], 9, width, width), jnp.bfloat16),
            pltpu.HBM((*edge, 9, width, width), jnp.bfloat16),
            pltpu.HBM((*inner, 9, width, width), jnp.bfloat16),
        ),
        scratch_shapes=[
            pltpu.VMEM(fresh.shape, jnp.float32),
            pltpu.VMEM((2, width, width), jnp.float32),
            pltpu.VMEM((2, width, width), jnp.float32),
            pltpu.VMEM((9, width, width), jnp.bfloat16),
            pltpu.VMEM((9, width, width), jnp.bfloat16),
            pltpu.SemaphoreType.DMA((2,)),
        ],
        name="setup",
    )(in_hbm(fresh))


def first_kernel(kappa, edge, fresh, coef, weight, sums, pv, *rest):
    feat = rest[-1]
    group = pl.program_id(0)
    size, _, width, _ = weight.shape

    @pl.when(group == 0)
    def _():
        def one_row(r, carry):
            tiles = []
            for col in range(fresh.shape[1]):
                tile = fresh[r, col]
                x, y, u, v = (tile[i : i + 1] for i in range(4))
                vol = tile[VOL : VOL + 1]
                zero = jnp.zeros_like(vol)
                vol_u, vol_v = vol * u, vol * v
                base = [vol, vol * x, vol * y, vol_u, vol_v, vol_u * x + vol_v * y, vol * tile[PRES : PRES + 1], zero]
                along_x = [zero, vol, zero, zero, zero, vol_u, zero, zero]
                along_y = [zero, zero, vol, zero, zero, vol_v, zero, zero]
                tiles.append([jnp.concatenate(rows, axis=0) for rows in (base, along_x, along_y)])
            for col in range(fresh.shape[1]):
                for i in range(3):
                    feat[r, col, i] = tiles[col][i]
            return carry

        lax.fori_loop(0, fresh.shape[0], one_row, 0)

    base = first_of(edge, fresh.shape[0] - 2, fresh.shape[1] - 2)
    outs = ([], [], [], [])
    for index in range(size):
        row, col = place_of(edge, group, index, fresh.shape[0] - 2, fresh.shape[1] - 2)
        around = []
        for k in range(9):
            off_x, off_y = k // 3 - 1, k % 3 - 1
            features = feat[row + k // 3, col + k % 3, 0]
            if off_x:
                features = features + float(off_x) * feat[row + k // 3, col + k % 3, 1]
            if off_y:
                features = features + float(off_y) * feat[row + k // 3, col + k % 3, 2]
            around.append(split(features))
        around = jnp.concatenate(around, axis=1)
        total_w = dot_nt(side_by_side(weight.at[index]), around)
        total_c = dot_nt(side_by_side(coef.at[base + group * size + index]), around)
        total_w = (total_w[:, :8] + total_w[:, 8:]).T
        total_c = (total_c[:, :8] + total_c[:, 8:]).T
        tile = fresh[row + 1, col + 1]
        x, y, u, v = (tile[i : i + 1] for i in range(4))
        vol = tile[VOL : VOL + 1]
        w_0, w_x, w_y, w_u, w_v, w_flow = (total_w[i : i + 1] for i in range(6))
        source = x * w_u + y * w_v - w_flow - (u * x + v * y) * w_0 + u * w_x + v * w_y
        source = kappa * 20.0 * source
        rden = 1.0 / (1.0 + kappa * 40.0 * total_c[0:1])
        first = (source + kappa * 40.0 * total_c[6:7]) * rden
        for out, value in zip(outs, (source, rden, vol, first * vol)):
            out.append(value)
    for place in range(3):
        sums[place, group] = jnp.concatenate(outs[place], axis=0)
    pv[group] = jnp.concatenate(outs[3], axis=0)
    if edge:

        @pl.when(group == 2)
        def _():
            write_sides(*rest[:2], pv)


def first_sweep(kappa, edge, fresh, coef, weight):
    groups, size, _, width, _ = weight.shape
    rows, cols = fresh.shape[:2]
    vmem = pl.BlockSpec(memory_space=pltpu.VMEM)
    return call(
        functools.partial(first_kernel, kappa, edge),
        grid=(groups,),
        in_specs=[once(fresh), vmem, pl.BlockSpec((None, size, 9, width, width), lambda group: (group, 0, 0, 0, 0))],
        out_specs=[vmem] * (4 if edge else 2),
        out_shape=[
            pltpu.VMEM((3, groups, size, width), jnp.float32),
            pltpu.VMEM((groups, size, width), jnp.float32),
        ]
        + [pltpu.VMEM((rows - 2, 1, width), jnp.float32)] * (2 if edge else 0),
        scratch_shapes=[pltpu.VMEM((rows, cols, 3, 8, width), jnp.float32)],
        name="first_sweep",
    )(in_hbm(fresh), pltpu.with_memory_space_constraint(coef, pltpu.VMEM), in_hbm(weight))


def sweep_kernel(kappa, last, edge, rows, cols, count, *refs):
    before_edge, before_inner, *halo = refs[: count - 2]
    coef, sums = refs[count - 2 : count]
    pv, *rest = refs[count:-2]
    pressure = rest[-1] if last else None
    ext, tiles = refs[-2:]
    groups, size, width = pv.shape
    base = first_of(edge, rows, cols)
    join(ext, 1, before_edge, before_inner, rows, cols)
    if edge:
        frame(ext, *halo, rows, cols)

    def spread(row, carry):
        for col in range(cols + 2):
            tiles[row, col] = jnp.broadcast_to(ext[row, col : col + 1, :], (16, width)).astype(jnp.bfloat16)
        return carry

    if edge:
        lax.fori_loop(0, rows + 2, spread, 0)
    else:
        lax.fori_loop(1, rows + 1, spread, 0)
    ones = jnp.ones((16, width), jnp.bfloat16)

    def one_group(group, carry):
        totals = []
        for index in range(size):
            row, col = place_of(edge, group, index, rows, cols)
            around = [tiles[row + k // 3, col + k % 3] for k in range(9)]
            parts = []
            for part in range(width // 16):
                total = None
                for k in range(9):
                    term = coef[base + group * size + index, k, pl.ds(part * 16, 16)] * around[k]
                    total = term if total is None else total + term
                parts.append(total)
            totals.append(dot_nt(ones, jnp.concatenate(parts, axis=0))[0:1])
        total = jnp.concatenate(totals, axis=0)
        value = (sums[0, group] + kappa * 40.0 * total) * sums[1, group]
        vol = sums[2, group]
        pv[group] = value * vol
        if last:
            pressure[group] = jnp.where(vol > 0.0, value, 0.0)
        return carry

    lax.fori_loop(0, groups, one_group, 0)
    if edge:
        write_sides(*rest[:2], pv)


def sweep(kappa, last, edge, shape, pv, halo, coef, sums):
    rows, cols, width = shape
    groups, size = groups_of(edge, rows, cols)
    vmem = pl.BlockSpec(memory_space=pltpu.VMEM)
    out = pltpu.VMEM((groups, size, width), jnp.float32)
    side = pltpu.VMEM((rows, 1, width), jnp.float32)
    outs = [out] + [side] * (2 if edge else 0) + [out] * (1 if last else 0)
    args = (*pv, *(halo if edge else ()), pltpu.with_memory_space_constraint(coef, pltpu.VMEM), sums)
    return call(
        functools.partial(sweep_kernel, kappa, last, edge, rows, cols, len(args)),
        in_specs=[vmem] * len(args),
        out_specs=[vmem] * len(outs),
        out_shape=outs,
        scratch_shapes=[
            pltpu.VMEM((rows + 2, cols + 2, width), jnp.float32),
            pltpu.VMEM((rows + 2, cols + 2, 16, width), jnp.bfloat16),
        ],
        name="sweep",
    )(*args)


def push_kernel(kappa, edge, count, *refs):
    before_edge, before_inner, *halo = refs[: count - (5 if edge else 3)]
    fresh, weight, pressure = refs[count - (5 if edge else 3) : count][:3]
    ext, feat = refs[-2:]
    group = pl.program_id(0)
    size, _, width, _ = weight.shape
    rows, cols = fresh.shape[0] - 2, fresh.shape[1] - 2

    @pl.when(group == 0)
    def _():
        join(ext, 1, before_edge, before_inner, rows, cols)
        if edge:
            frame(ext, *halo, rows, cols)

        def one_row(r, carry):
            tiles = []
            for col in range(ext.shape[1]):
                value = ext[r, col : col + 1, :]
                tile = fresh[r, col]
                x, y, vol = tile[X : X + 1], tile[Y : Y + 1], tile[VOL : VOL + 1]
                zero = jnp.zeros_like(x)
                tiles.append(jnp.concatenate([value, value * x, value * y, zero, vol, vol * x, vol * y, zero], axis=0))
            for col in range(ext.shape[1]):
                feat[r, col] = tiles[col]
            return carry

        lax.fori_loop(0, rows + 2, one_row, 0)

    feature = row_index(width)
    news = ([], [])
    for index in range(size):
        row, col = place_of(edge, group, index, rows, cols)
        around = []
        for k in range(9):
            tile = feat[row + k // 3, col + k % 3]
            off_x, off_y = k // 3 - 1.0, k % 3 - 1.0
            pv, vol = tile[0:1], tile[4:5]
            if off_x:
                tile = tile + jnp.where(feature == 1, off_x * pv, jnp.where(feature == 5, off_x * vol, 0.0))
            if off_y:
                tile = tile + jnp.where(feature == 2, off_y * pv, jnp.where(feature == 6, off_y * vol, 0.0))
            around.append(split(tile))
        total = dot_nt(side_by_side(weight.at[index]), jnp.concatenate(around, axis=1))
        total = (total[:, :8] + total[:, 8:]).T
        tile = fresh[row + 1, col + 1]
        own = pressure[group, index : index + 1, :]
        alive = tile[VOL : VOL + 1] > 0.0
        for axis in (0, 1):
            at = tile[axis : axis + 1]
            grad = at * total[0:1] - total[1 + axis : 2 + axis] - own * (at * total[4:5] - total[5 + axis : 6 + axis])
            news[axis].append(jnp.where(alive, tile[2 + axis : 3 + axis] + kappa * 20.0 * grad, 0.0))
    if not edge:
        out = refs[count]
        for axis in (0, 1):
            out[axis, group] = jnp.concatenate(news[axis], axis=0)
        return
    inner_pressure, inner_new = refs[count - 2 : count]
    out_pressure, out_new, new = refs[count:-2]
    for axis in (0, 1):
        new[axis, group] = jnp.concatenate(news[axis], axis=0)

    @pl.when(group == 2)
    def _():
        join(out_pressure, 0, pressure, inner_pressure, rows, cols)
        for axis in (0, 1):
            join(out_new.at[axis], 0, new.at[axis], inner_new.at[axis], rows, cols)


def push(kappa, edge, pv, halo, fresh, weight, pressure, inner):
    groups, size, _, width, _ = weight.shape
    rows, cols = fresh.shape[:2]
    vmem = pl.BlockSpec(memory_space=pltpu.VMEM)
    weight = in_hbm(weight)
    args = (*pv, *(halo if edge else ()), in_hbm(fresh), weight, pressure, *(inner if edge else ()))
    specs = [vmem] * len(args)
    specs[len(pv) + (len(halo) if edge else 0)] = once(fresh)
    specs[len(pv) + (len(halo) if edge else 0) + 1] = pl.BlockSpec(
        (None, size, 9, width, width), lambda group: (group, 0, 0, 0, 0)
    )
    if edge:
        outs = [
            jax.ShapeDtypeStruct((rows - 2, cols - 2, width), jnp.float32),
            jax.ShapeDtypeStruct((2, rows - 2, cols - 2, width), jnp.float32),
        ]
    else:
        outs = [pltpu.VMEM((2, groups, size, width), jnp.float32)]
    return call(
        functools.partial(push_kernel, kappa, edge, len(args)),
        grid=(groups,),
        in_specs=specs,
        out_specs=[vmem] * len(outs),
        out_shape=outs,
        scratch_shapes=([pltpu.VMEM((2, groups, size, width), jnp.float32)] if edge else [])
        + [
            pltpu.VMEM((rows, cols, width), jnp.float32),
            pltpu.VMEM((rows, cols, 8, width), jnp.float32),
        ],
        name="push",
    )(*args)


def local(position, velocity, volume, pressure_prev, fill, drift_from):
    shape = volume.shape
    kappa = 1.0 / shape[2]
    even = [lax.axis_index(axis) % 2 == 0 for axis in ("gx", "gy")]
    position, even = lax.optimization_barrier((position, even))
    old, top = prepare(position, velocity, volume, pressure_prev, fill, drift_from)
    top = largest(top)
    fresh = drift(top, old, *exchange_old(even, old, 2))
    coef, edge_weight, inner_weight = setup(fresh)
    edge_sums, edge_pv, *sides = first_sweep(kappa, True, fresh, coef, edge_weight)
    inner_sums, inner_pv = first_sweep(kappa, False, fresh, coef, inner_weight)
    for step in range(1, SWEEPS):
        last = step == SWEEPS - 1
        before = (edge_pv, inner_pv)
        halo = exchange_edges(even, edge_pv, *sides)
        inner_pv, *inner_pressure = sweep(kappa, last, False, shape, before, halo, coef, inner_sums)
        edge_pv, *rest = sweep(kappa, last, True, shape, before, halo, coef, edge_sums)
        sides, edge_pressure = rest[:2], rest[2:]
    pv = (edge_pv, inner_pv)
    halo = exchange_edges(even, edge_pv, *sides)
    (inner_new,) = push(kappa, False, pv, halo, fresh, inner_weight, inner_pressure[0], ())
    inner = (inner_pressure[0], inner_new)
    pressure, velocity_new = push(kappa, True, pv, halo, fresh, edge_weight, edge_pressure[0], inner)
    return (pressure, velocity_new)


def solution(mesh):
    return jax.shard_map(
        local,
        mesh=mesh,
        in_specs=(
            P(None, "gx", "gy", None),
            P(None, "gx", "gy", None),
            P("gx", "gy", None),
            P("gx", "gy", None),
            P("gx", "gy"),
            P("gx", "gy"),
        ),
        out_specs=(P("gx", "gy", None), P(None, "gx", "gy", None)),
        check_vma=False,
    )
```

```python
import functools

import jax
import jax.numpy as jnp
from jax import lax
from jax.experimental import pallas as pl
from jax.experimental.pallas import tpu as pltpu
from jax.sharding import PartitionSpec as P

SWEEPS = 4
CFL = 0.25
SPEED_EPS = 1e-06
SOFT = 0.01
CHUNK = 64
BUFFERS = 4
VMEM_LIMIT = 16 * 1024 * 1024

X, Y, U, V, VOL, PRES, CODE = range(7)


def call(kernel, **kwargs):
    return pl.pallas_call(
        kernel, compiler_params=pltpu.CompilerParams(vmem_limit_bytes=VMEM_LIMIT), **kwargs
    )


def in_hbm(array):
    return pltpu.with_memory_space_constraint(array, pltpu.HBM)


def once(array):
    return pl.BlockSpec(array.shape, lambda group: (0,) * array.ndim)


def side_by_side(*blocks):
    return jnp.concatenate([part[k] for part in blocks for k in range(part.shape[0])], axis=1)


def thirds(size, width):
    return [pl.BlockSpec((None, size, 3, width, width), lambda group, i=i: (group, 0, i, 0, 0)) for i in range(3)]


def row_index(width):
    return lax.broadcasted_iota(jnp.int32, (8, width), 0)


def split(value):
    high = value.astype(jnp.bfloat16).astype(jnp.float32)
    return jnp.concatenate([high, value - high], axis=0).astype(jnp.bfloat16)


def dot(left, right):
    return jnp.dot(left, right, preferred_element_type=jnp.float32)


def prepare_kernel(position, velocity, volume, pressure, fill, code, old, top):
    rows, cols, width = volume.shape
    slots = lax.broadcasted_iota(jnp.int32, (cols, width), 1)
    most = jnp.zeros((cols, width), jnp.float32)
    for row in range(rows):
        live = (slots < fill[row]).astype(jnp.float32)
        most = jnp.maximum(most, jnp.abs(velocity[0, row]) * live)
        most = jnp.maximum(most, jnp.abs(velocity[1, row]) * live)
        channels = [
            position[0, row],
            position[1, row],
            velocity[0, row],
            velocity[1, row],
            volume[row] * live,
            pressure[row],
            jnp.broadcast_to((code[row] + 1).astype(jnp.float32), (cols, width)),
            jnp.zeros((cols, width), jnp.float32),
        ]
        for channel, value in enumerate(channels):
            old[row, :, channel, :] = value
    top[...] = jnp.broadcast_to(jnp.max(most), top.shape)


def prepare(position, velocity, volume, pressure, fill, code):
    rows, cols, width = volume.shape
    return call(
        prepare_kernel,
        out_shape=(
            pltpu.VMEM((rows, cols, 8, width), jnp.float32),
            pltpu.VMEM((8, width), jnp.float32),
        ),
        name="prepare",
    )(position, velocity, volume, pressure, fill[:, :, None], code[:, :, None])


def neighbours(axis, even, low, high):
    devices = lax.axis_size(axis)

    def swap(value, first):
        pairs = [(i, i + 1) for i in range(first, devices - 1, 2)]
        return lax.ppermute(value, axis, pairs + [(j, i) for i, j in pairs])

    one = swap(jnp.where(even, high, low), 0)
    two = swap(jnp.where(even, low, high), 1)
    return jnp.where(even, two, one), jnp.where(even, one, two)


def exchange_old(even, shard, depth):
    above, below = neighbours("gx", even[0], shard[:depth], shard[-depth:])
    low = jnp.concatenate([above[:, :depth], shard[:, :depth], below[:, :depth]], axis=0)
    high = jnp.concatenate([above[:, -depth:], shard[:, -depth:], below[:, -depth:]], axis=0)
    left, right = neighbours("gy", even[1], low, high)
    return above, below, left, right


def exchange_edges(even, edge, left, right):
    above, below = neighbours("gx", even[0], edge[0][None], edge[1][None])
    low = jnp.concatenate([above[:, :1], left, below[:, :1]], axis=0)
    high = jnp.concatenate([above[:, -1:], right, below[:, -1:]], axis=0)
    return above, below, *neighbours("gy", even[1], low, high)


def groups_of(edge, rows, cols):
    return (3, cols) if edge else (rows - 2, cols - 2)


def first_of(edge, rows, cols):
    return 0 if edge else 3 * cols


def place_of(edge, group, index, rows, cols):
    if not edge:
        return group + 1, index + 1
    half = cols // 2
    left = index < half
    side_row = jnp.minimum(jnp.where(left, index, index - half) + 1, rows - 2)
    side_col = jnp.where(left, 0, cols - 1)
    row = jnp.where(group == 0, 0, jnp.where(group == 1, rows - 1, side_row))
    return row, jnp.where(group == 2, side_col, index)


def join(out, at, edge, inner, rows, cols):
    half = cols // 2
    out[at, at : at + cols] = edge[0]
    out[at + rows - 1, at : at + cols] = edge[1]
    for row in range(1, rows - 1):
        out[at + row, at : at + 1] = edge[2, row - 1 : row]
        out[at + row, at + cols - 1 : at + cols] = edge[2, half + row - 1 : half + row]
        out[at + row, at + 1 : at + cols - 1] = inner[row - 1]


def write_sides(left, right, edge):
    rows, half = left.shape[0], edge.shape[1] // 2
    for out, corner, first in ((left, 0, 0), (right, 2 * half - 1, half)):
        out[0] = edge[0, corner : corner + 1]
        out[rows - 1] = edge[1, corner : corner + 1]
        for row in range(1, rows - 1):
            out[row] = edge[2, first + row - 1 : first + row]


def frame(out, above, below, left, right, rows, cols):
    out[0, 1 : cols + 1] = above[0]
    out[rows + 1, 1 : cols + 1] = below[0]
    for row in range(rows + 2):
        out[row, 0:1] = left[row]
        out[row, cols + 1 : cols + 2] = right[row]


def largest(value):
    for axis in ("gy", "gx"):
        devices = lax.axis_size(axis)
        if devices & (devices - 1):
            value = lax.pmax(value, axis)
            continue
        for bit in range(devices.bit_length() - 1):
            pairs = [(i, i ^ (1 << bit)) for i in range(devices)]
            value = jnp.maximum(value, lax.ppermute(value, axis, pairs))
    return value


def assemble(out, center, above, below, left, right, depth):
    rows, cols = center.shape[:2]
    out[:depth, depth : depth + cols] = above[...]
    out[depth : depth + rows, depth : depth + cols] = center[...]
    out[depth + rows :, depth : depth + cols] = below[...]
    out[:, :depth] = left[...]
    out[:, depth + cols :] = right[...]


def drift_kernel(top, center, above, below, left, right, out, fresh, old):
    rows, cols, _, width = fresh.shape
    assemble(old, center, above, below, left, right, 2)
    step = CFL / (jnp.max(top[...]) + SPEED_EPS)
    index = row_index(width)

    def one_row(row, carry):
        for col in range(cols):
            code = old[row + 1, col + 1, CODE : CODE + 1, :]
            tile = jnp.zeros((8, width), jnp.float32)
            for k in range(9):
                off_x, off_y = k // 3, k % 3
                offset = jnp.where(index == X, off_x - 1.0, jnp.where(index == Y, off_y - 1.0, 0.0))
                source = old[row + off_x, col + off_y] + offset
                tile = jnp.where(code == k + 1.0, source, tile)
            moved = tile + step * pltpu.roll(tile, 6, 0)
            fresh[row, col] = jnp.where(index <= Y, moved, tile)
        return carry

    lax.fori_loop(0, rows, one_row, 0)
    pltpu.sync_copy(fresh, out)


def drift(top, center, above, below, left, right):
    rows, cols, _, width = center.shape
    return call(
        drift_kernel,
        out_specs=pl.BlockSpec(memory_space=pltpu.HBM),
        out_shape=pltpu.HBM((rows + 2, cols + 2, 8, width), jnp.float32),
        scratch_shapes=[pltpu.VMEM((rows + 2, cols + 2, 8, width), jnp.float32), pltpu.VMEM((rows + 4, cols + 4, 8, width), jnp.float32)],
        name="drift",
    )(top, center, above, below, left, right)


def dot_nt(left, right):
    return lax.dot_general(left, right, (((1,), (1,)), ((), ())), preferred_element_type=jnp.float32)


def setup_kernel(source, coef, edge_weight, inner_weight, fresh, xcol, ycol, sem, *outs):
    pltpu.sync_copy(source, fresh)
    for edge, weight in ((True, edge_weight), (False, inner_weight)):
        setup_list(edge, fresh, coef, weight, xcol, ycol, sem, outs)


def setup_list(edge, fresh, coef, weight, xcol, ycol, sem, outs):
    groups, size, _, width, _ = weight.shape
    rows, cols = fresh.shape[0] - 2, fresh.shape[1] - 2
    base = first_of(edge, rows, cols)

    def place(bin_id):
        return place_of(edge, bin_id // size, lax.rem(bin_id, size), rows, cols)

    def columns(bin_id, slot):
        row, col = place(bin_id)
        tile = fresh[row + 1, col + 1]
        xcol[slot] = jnp.broadcast_to(tile[X : X + 1], (width, width)).T
        ycol[slot] = jnp.broadcast_to(tile[Y : Y + 1], (width, width)).T

    def blocks(bin_id, slot, out):
        row, col = place(bin_id)
        values = coef.at[base + bin_id]
        around = [fresh[row + k // 3, col + k % 3] for k in range(9)]
        xj = [jnp.broadcast_to(around[k][X : X + 1] + (k // 3 - 1.0), (8, width)) for k in range(9)]
        yj = [jnp.broadcast_to(around[k][Y : Y + 1] + (k % 3 - 1.0), (8, width)) for k in range(9)]
        for part in range(width // CHUNK):
            span = pl.ds(part * CHUNK, CHUNK)
            spans = [pl.ds(part * CHUNK + 8 * i, 8) for i in range(CHUNK // 8)]
            xi = [xcol[slot, piece] for piece in spans]
            yi = [ycol[slot, piece] for piece in spans]
            for k in range(9):
                squares, weights = [], []
                for x, y in zip(xi, yi):
                    dx = x - xj[k]
                    dy = y - yj[k]
                    square = jnp.maximum(dx * dx + dy * dy, 1e-14)
                    remain = jnp.maximum(1.0 - square * lax.rsqrt(square), 0.0)
                    squares.append(square)
                    weights.append(remain * remain * remain)
                squares = jnp.concatenate(squares, axis=0).astype(jnp.bfloat16)
                weights = jnp.concatenate(weights, axis=0).astype(jnp.bfloat16)
                ratio = squares * pltpu.reciprocal(squares + jnp.bfloat16(SOFT), approx=True)
                out[k, span] = weights
                values[k, span] = weights * ratio

    def copies(bin_id, slot):
        target = weight.at[bin_id // size, lax.rem(bin_id, size)]
        third = [pl.ds(3 * i, 3) for i in range(3)]
        return [pltpu.make_async_copy(outs[slot].at[at], target.at[at], sem.at[slot, i]) for i, at in enumerate(third)]

    count = groups * size
    columns(0, 0)
    columns(1, 1)

    def some_bins(step, carry):
        for slot in range(BUFFERS):
            bin_id = BUFFERS * step + slot

            @pl.when(step > 0)
            def _():
                for copy in copies(bin_id - BUFFERS, slot):
                    copy.wait()

            blocks(bin_id, slot % 2, outs[slot])
            columns(jnp.minimum(bin_id + 2, count - 1), slot % 2)
            for copy in copies(bin_id, slot):
                copy.start()
        return carry

    lax.fori_loop(0, count // BUFFERS, some_bins, 0)
    for slot in range(BUFFERS):
        for copy in copies(count - BUFFERS + slot, slot):
            copy.wait()


def setup(fresh):
    rows, cols, _, width = fresh.shape
    edge, inner = (groups_of(kind, rows - 2, cols - 2) for kind in (True, False))
    vmem, hbm = pl.BlockSpec(memory_space=pltpu.VMEM), pl.BlockSpec(memory_space=pltpu.HBM)
    return call(
        setup_kernel,
        in_specs=[hbm],
        out_specs=(vmem, hbm, hbm),
        out_shape=(
            pltpu.VMEM((edge[0] * edge[1] + inner[0] * inner[1], 9, width, width), jnp.bfloat16),
            pltpu.HBM((*edge, 9, width, width), jnp.bfloat16),
            pltpu.HBM((*inner, 9, width, width), jnp.bfloat16),
        ),
        scratch_shapes=[
            pltpu.VMEM(fresh.shape, jnp.float32),
            pltpu.VMEM((2, width, width), jnp.float32),
            pltpu.VMEM((2, width, width), jnp.float32),
            pltpu.SemaphoreType.DMA((BUFFERS, 3)),
        ]
        + [pltpu.VMEM((9, width, width), jnp.bfloat16)] * BUFFERS,
        name="setup",
    )(in_hbm(fresh))


def first_kernel(kappa, edge, fresh, coef, weight, second, third, sums, pv, *rest):
    feat = rest[-1]
    group = pl.program_id(0)
    size, _, width, _ = weight.shape

    @pl.when(group == 0)
    def _():
        def one_row(r, carry):
            tiles = []
            for col in range(fresh.shape[1]):
                tile = fresh[r, col]
                x, y, u, v = (tile[i : i + 1] for i in range(4))
                vol = tile[VOL : VOL + 1]
                zero = jnp.zeros_like(vol)
                vol_u, vol_v = vol * u, vol * v
                base = [vol, vol * x, vol * y, vol_u, vol_v, vol_u * x + vol_v * y, vol * tile[PRES : PRES + 1], zero]
                along_x = [zero, vol, zero, zero, zero, vol_u, zero, zero]
                along_y = [zero, zero, vol, zero, zero, vol_v, zero, zero]
                tiles.append([jnp.concatenate(rows, axis=0) for rows in (base, along_x, along_y)])
            for col in range(fresh.shape[1]):
                for i in range(3):
                    feat[r, col, i] = tiles[col][i]
            return carry

        lax.fori_loop(0, fresh.shape[0], one_row, 0)

    base = first_of(edge, fresh.shape[0] - 2, fresh.shape[1] - 2)
    outs = ([], [], [], [])
    for index in range(size):
        row, col = place_of(edge, group, index, fresh.shape[0] - 2, fresh.shape[1] - 2)
        around = []
        for k in range(9):
            off_x, off_y = k // 3 - 1, k % 3 - 1
            features = feat[row + k // 3, col + k % 3, 0]
            if off_x:
                features = features + float(off_x) * feat[row + k // 3, col + k % 3, 1]
            if off_y:
                features = features + float(off_y) * feat[row + k // 3, col + k % 3, 2]
            around.append(split(features))
        around = jnp.concatenate(around, axis=1)
        total_w = dot_nt(side_by_side(*(part.at[index] for part in (weight, second, third))), around)
        total_c = dot_nt(side_by_side(coef.at[base + group * size + index]), around)
        total_w = (total_w[:, :8] + total_w[:, 8:]).T
        total_c = (total_c[:, :8] + total_c[:, 8:]).T
        tile = fresh[row + 1, col + 1]
        x, y, u, v = (tile[i : i + 1] for i in range(4))
        vol = tile[VOL : VOL + 1]
        w_0, w_x, w_y, w_u, w_v, w_flow = (total_w[i : i + 1] for i in range(6))
        source = x * w_u + y * w_v - w_flow - (u * x + v * y) * w_0 + u * w_x + v * w_y
        source = kappa * 20.0 * source
        rden = 1.0 / (1.0 + kappa * 40.0 * total_c[0:1])
        first = (source + kappa * 40.0 * total_c[6:7]) * rden
        for out, value in zip(outs, (source, rden, vol, first * vol)):
            out.append(value)
    for place in range(3):
        sums[place, group] = jnp.concatenate(outs[place], axis=0)
    pv[group] = jnp.concatenate(outs[3], axis=0)
    if edge:

        @pl.when(group == 2)
        def _():
            write_sides(*rest[:2], pv)


def first_sweep(kappa, edge, fresh, coef, weight):
    groups, size, _, width, _ = weight.shape
    rows, cols = fresh.shape[:2]
    vmem = pl.BlockSpec(memory_space=pltpu.VMEM)
    return call(
        functools.partial(first_kernel, kappa, edge),
        grid=(groups,),
        in_specs=[once(fresh), vmem, *thirds(size, width)],
        out_specs=[vmem] * (4 if edge else 2),
        out_shape=[
            pltpu.VMEM((3, groups, size, width), jnp.float32),
            pltpu.VMEM((groups, size, width), jnp.float32),
        ]
        + [pltpu.VMEM((rows - 2, 1, width), jnp.float32)] * (2 if edge else 0),
        scratch_shapes=[pltpu.VMEM((rows, cols, 3, 8, width), jnp.float32)],
        name="first_sweep",
    )(in_hbm(fresh), pltpu.with_memory_space_constraint(coef, pltpu.VMEM), *[in_hbm(weight)] * 3)


def sweep_kernel(kappa, last, edge, rows, cols, count, *refs):
    before_edge, before_inner, *halo = refs[: count - 2]
    coef, sums = refs[count - 2 : count]
    pv, *rest = refs[count:-2]
    pressure = rest[-1] if last else None
    ext, tiles = refs[-2:]
    groups, size, width = pv.shape
    base = first_of(edge, rows, cols)
    join(ext, 1, before_edge, before_inner, rows, cols)
    if edge:
        frame(ext, *halo, rows, cols)

    def spread(row, carry):
        for col in range(cols + 2):
            tiles[row, col] = jnp.broadcast_to(ext[row, col : col + 1, :], (16, width)).astype(jnp.bfloat16)
        return carry

    if edge:
        lax.fori_loop(0, rows + 2, spread, 0)
    else:
        lax.fori_loop(1, rows + 1, spread, 0)
    ones = jnp.ones((16, width), jnp.bfloat16)

    def one_group(group, carry):
        totals = []
        for index in range(size):
            row, col = place_of(edge, group, index, rows, cols)
            around = [tiles[row + k // 3, col + k % 3] for k in range(9)]
            parts = []
            for part in range(width // 16):
                total = None
                for k in range(9):
                    term = coef[base + group * size + index, k, pl.ds(part * 16, 16)] * around[k]
                    total = term if total is None else total + term
                parts.append(total)
            totals.append(dot_nt(ones, jnp.concatenate(parts, axis=0))[0:1])
        total = jnp.concatenate(totals, axis=0)
        value = (sums[0, group] + kappa * 40.0 * total) * sums[1, group]
        vol = sums[2, group]
        pv[group] = value * vol
        if last:
            pressure[group] = jnp.where(vol > 0.0, value, 0.0)
        return carry

    lax.fori_loop(0, groups, one_group, 0)
    if edge:
        write_sides(*rest[:2], pv)


def sweep(kappa, last, edge, shape, pv, halo, coef, sums):
    rows, cols, width = shape
    groups, size = groups_of(edge, rows, cols)
    vmem = pl.BlockSpec(memory_space=pltpu.VMEM)
    out = pltpu.VMEM((groups, size, width), jnp.float32)
    side = pltpu.VMEM((rows, 1, width), jnp.float32)
    outs = [out] + [side] * (2 if edge else 0) + [out] * (1 if last else 0)
    args = (*pv, *(halo if edge else ()), pltpu.with_memory_space_constraint(coef, pltpu.VMEM), sums)
    return call(
        functools.partial(sweep_kernel, kappa, last, edge, rows, cols, len(args)),
        in_specs=[vmem] * len(args),
        out_specs=[vmem] * len(outs),
        out_shape=outs,
        scratch_shapes=[
            pltpu.VMEM((rows + 2, cols + 2, width), jnp.float32),
            pltpu.VMEM((rows + 2, cols + 2, 16, width), jnp.bfloat16),
        ],
        name="sweep",
    )(*args)


def push_kernel(kappa, edge, count, *refs):
    before_edge, before_inner, *halo = refs[: count - (7 if edge else 5)]
    fresh, weight, second, third, pressure = refs[count - (7 if edge else 5) : count][:5]
    ext, feat = refs[-2:]
    group = pl.program_id(0)
    size, _, width, _ = weight.shape
    rows, cols = fresh.shape[0] - 2, fresh.shape[1] - 2

    @pl.when(group == 0)
    def _():
        join(ext, 1, before_edge, before_inner, rows, cols)
        if edge:
            frame(ext, *halo, rows, cols)

        def one_row(r, carry):
            tiles = []
            for col in range(ext.shape[1]):
                value = ext[r, col : col + 1, :]
                tile = fresh[r, col]
                x, y, vol = tile[X : X + 1], tile[Y : Y + 1], tile[VOL : VOL + 1]
                zero = jnp.zeros_like(x)
                tiles.append(jnp.concatenate([value, value * x, value * y, zero, vol, vol * x, vol * y, zero], axis=0))
            for col in range(ext.shape[1]):
                feat[r, col] = tiles[col]
            return carry

        lax.fori_loop(0, rows + 2, one_row, 0)

    feature = row_index(width)
    news = ([], [])
    for index in range(size):
        row, col = place_of(edge, group, index, rows, cols)
        around = []
        for k in range(9):
            tile = feat[row + k // 3, col + k % 3]
            off_x, off_y = k // 3 - 1.0, k % 3 - 1.0
            pv, vol = tile[0:1], tile[4:5]
            if off_x:
                tile = tile + jnp.where(feature == 1, off_x * pv, jnp.where(feature == 5, off_x * vol, 0.0))
            if off_y:
                tile = tile + jnp.where(feature == 2, off_y * pv, jnp.where(feature == 6, off_y * vol, 0.0))
            around.append(split(tile))
        total = dot_nt(side_by_side(*(part.at[index] for part in (weight, second, third))), jnp.concatenate(around, axis=1))
        total = (total[:, :8] + total[:, 8:]).T
        tile = fresh[row + 1, col + 1]
        own = pressure[group, index : index + 1, :]
        alive = tile[VOL : VOL + 1] > 0.0
        for axis in (0, 1):
            at = tile[axis : axis + 1]
            grad = at * total[0:1] - total[1 + axis : 2 + axis] - own * (at * total[4:5] - total[5 + axis : 6 + axis])
            news[axis].append(jnp.where(alive, tile[2 + axis : 3 + axis] + kappa * 20.0 * grad, 0.0))
    if not edge:
        out = refs[count]
        for axis in (0, 1):
            out[axis, group] = jnp.concatenate(news[axis], axis=0)
        return
    inner_pressure, inner_new = refs[count - 2 : count]
    out_pressure, out_new, new = refs[count:-2]
    for axis in (0, 1):
        new[axis, group] = jnp.concatenate(news[axis], axis=0)

    @pl.when(group == 2)
    def _():
        join(out_pressure, 0, pressure, inner_pressure, rows, cols)
        for axis in (0, 1):
            join(out_new.at[axis], 0, new.at[axis], inner_new.at[axis], rows, cols)


def push(kappa, edge, pv, halo, fresh, weight, pressure, inner):
    groups, size, _, width, _ = weight.shape
    rows, cols = fresh.shape[:2]
    vmem = pl.BlockSpec(memory_space=pltpu.VMEM)
    weight = in_hbm(weight)
    args = (*pv, *(halo if edge else ()), in_hbm(fresh), *[weight] * 3, pressure, *(inner if edge else ()))
    specs = [vmem] * len(args)
    first = len(pv) + (len(halo) if edge else 0)
    specs[first : first + 4] = [once(fresh), *thirds(size, width)]
    if edge:
        outs = [
            jax.ShapeDtypeStruct((rows - 2, cols - 2, width), jnp.float32),
            jax.ShapeDtypeStruct((2, rows - 2, cols - 2, width), jnp.float32),
        ]
    else:
        outs = [pltpu.VMEM((2, groups, size, width), jnp.float32)]
    return call(
        functools.partial(push_kernel, kappa, edge, len(args)),
        grid=(groups,),
        in_specs=specs,
        out_specs=[vmem] * len(outs),
        out_shape=outs,
        scratch_shapes=([pltpu.VMEM((2, groups, size, width), jnp.float32)] if edge else [])
        + [
            pltpu.VMEM((rows, cols, width), jnp.float32),
            pltpu.VMEM((rows, cols, 8, width), jnp.float32),
        ],
        name="push",
    )(*args)


def local(position, velocity, volume, pressure_prev, fill, drift_from):
    shape = volume.shape
    kappa = 1.0 / shape[2]
    even = [lax.axis_index(axis) % 2 == 0 for axis in ("gx", "gy")]
    position, even = lax.optimization_barrier((position, even))
    old, top = prepare(position, velocity, volume, pressure_prev, fill, drift_from)
    top = largest(top)
    fresh = drift(top, old, *exchange_old(even, old, 2))
    coef, edge_weight, inner_weight = setup(fresh)
    edge_sums, edge_pv, *sides = first_sweep(kappa, True, fresh, coef, edge_weight)
    inner_sums, inner_pv = first_sweep(kappa, False, fresh, coef, inner_weight)
    for step in range(1, SWEEPS):
        last = step == SWEEPS - 1
        before = (edge_pv, inner_pv)
        halo = exchange_edges(even, edge_pv, *sides)
        inner_pv, *inner_pressure = sweep(kappa, last, False, shape, before, halo, coef, inner_sums)
        edge_pv, *rest = sweep(kappa, last, True, shape, before, halo, coef, edge_sums)
        sides, edge_pressure = rest[:2], rest[2:]
    pv = (edge_pv, inner_pv)
    halo = exchange_edges(even, edge_pv, *sides)
    (inner_new,) = push(kappa, False, pv, halo, fresh, inner_weight, inner_pressure[0], ())
    inner = (inner_pressure[0], inner_new)
    pressure, velocity_new = push(kappa, True, pv, halo, fresh, edge_weight, edge_pressure[0], inner)
    return (pressure, velocity_new)


def solution(mesh):
    return jax.shard_map(
        local,
        mesh=mesh,
        in_specs=(
            P(None, "gx", "gy", None),
            P(None, "gx", "gy", None),
            P("gx", "gy", None),
            P("gx", "gy", None),
            P("gx", "gy"),
            P("gx", "gy"),
        ),
        out_specs=(P("gx", "gy", None), P(None, "gx", "gy", None)),
        check_vma=False,
    )
```

```python
import functools

import jax
import jax.numpy as jnp
from jax import lax
from jax.experimental import pallas as pl
from jax.experimental.pallas import tpu as pltpu
from jax.sharding import PartitionSpec as P

SWEEPS = 4
CFL = 0.25
SPEED_EPS = 1e-06
SOFT = 0.01
CHUNK = 64
BUFFERS = 4
VMEM_LIMIT = 16 * 1024 * 1024

X, Y, U, V, VOL, PRES, CODE = range(7)


def call(kernel, **kwargs):
    return pl.pallas_call(
        kernel, compiler_params=pltpu.CompilerParams(vmem_limit_bytes=VMEM_LIMIT), **kwargs
    )


def in_hbm(array):
    return pltpu.with_memory_space_constraint(array, pltpu.HBM)


def once(array):
    return pl.BlockSpec(array.shape, lambda group: (0,) * array.ndim)


def side_by_side(*blocks):
    return jnp.concatenate([part[k] for part in blocks for k in range(part.shape[0])], axis=1)


def thirds(size, width):
    return [pl.BlockSpec((None, size, 3, width, width), lambda group, i=i: (group, 0, i, 0, 0)) for i in range(3)]


def row_index(width):
    return lax.broadcasted_iota(jnp.int32, (8, width), 0)


def split(value):
    high = value.astype(jnp.bfloat16).astype(jnp.float32)
    return jnp.concatenate([high, value - high], axis=0).astype(jnp.bfloat16)


def dot(left, right):
    return jnp.dot(left, right, preferred_element_type=jnp.float32)


def prepare_kernel(*refs):
    sources, (fill, code, old, top) = refs[:4], refs[4:8]
    arrays, sem = refs[8:12], refs[12]
    copies = [pltpu.make_async_copy(source, array, sem.at[i]) for i, (source, array) in enumerate(zip(sources, arrays))]
    for copy in copies:
        copy.start()
    for copy in copies:
        copy.wait()
    position, velocity, volume, pressure = arrays
    rows, cols, width = volume.shape
    slots = lax.broadcasted_iota(jnp.int32, (cols, width), 1).astype(jnp.float32)
    most = jnp.zeros((cols, width), jnp.float32)

    def along_lanes(values):
        return jnp.broadcast_to(values.astype(jnp.float32), (width, cols)).T

    for row in range(rows):
        live = (slots < along_lanes(fill[row : row + 1])).astype(jnp.float32)
        most = jnp.maximum(most, jnp.abs(velocity[0, row]) * live)
        most = jnp.maximum(most, jnp.abs(velocity[1, row]) * live)
        channels = [
            position[0, row],
            position[1, row],
            velocity[0, row],
            velocity[1, row],
            volume[row] * live,
            pressure[row],
            along_lanes(code[row : row + 1] + 1),
            jnp.zeros((cols, width), jnp.float32),
        ]
        for channel, value in enumerate(channels):
            old[row, :, channel, :] = value
    top[...] = jnp.broadcast_to(jnp.max(most), top.shape)


def prepare(position, velocity, volume, pressure, fill, code):
    rows, cols, width = volume.shape
    arrays = (position, velocity, volume, pressure)
    vmem, hbm = pl.BlockSpec(memory_space=pltpu.VMEM), pl.BlockSpec(memory_space=pltpu.HBM)
    return call(
        prepare_kernel,
        in_specs=[hbm] * 4 + [vmem] * 2,
        out_specs=[vmem] * 2,
        out_shape=(
            pltpu.VMEM((rows, cols, 8, width), jnp.float32),
            pltpu.VMEM((8, width), jnp.float32),
        ),
        scratch_shapes=[pltpu.VMEM(array.shape, jnp.float32) for array in arrays] + [pltpu.SemaphoreType.DMA((4,))],
        name="prepare",
    )(*(in_hbm(array) for array in arrays), fill, code)


def neighbours(axis, even, low, high):
    devices = lax.axis_size(axis)

    def swap(value, first):
        pairs = [(i, i + 1) for i in range(first, devices - 1, 2)]
        return lax.ppermute(value, axis, pairs + [(j, i) for i, j in pairs])

    one = swap(jnp.where(even, high, low), 0)
    two = swap(jnp.where(even, low, high), 1)
    return jnp.where(even, two, one), jnp.where(even, one, two)


def exchange_old(even, shard, top, depth):
    above, below = neighbours("gx", even[0], shard[:depth], shard[-depth:])
    top = largest(top, "gy")
    above, below, top = lax.optimization_barrier((above, below, top))
    low = jnp.concatenate([above[:, :depth], shard[:, :depth], below[:, :depth]], axis=0)
    high = jnp.concatenate([above[:, -depth:], shard[:, -depth:], below[:, -depth:]], axis=0)
    left, right = neighbours("gy", even[1], low, high)
    return (above, below, left, right), largest(top, "gx")


def exchange_rows(even, edge):
    return neighbours("gx", even[0], edge[0][None], edge[1][None])


def exchange_sides(even, above, below, left, right):
    low = jnp.concatenate([above[:, :1], left, below[:, :1]], axis=0)
    high = jnp.concatenate([above[:, -1:], right, below[:, -1:]], axis=0)
    return neighbours("gy", even[1], low, high)


def groups_of(edge, rows, cols):
    return (3, cols) if edge else (rows - 2, cols - 2)


def first_of(edge, rows, cols):
    return 0 if edge else 3 * cols


def place_of(edge, group, index, rows, cols):
    if not edge:
        return group + 1, index + 1
    half = cols // 2
    left = index < half
    side_row = jnp.minimum(jnp.where(left, index, index - half) + 1, rows - 2)
    side_col = jnp.where(left, 0, cols - 1)
    row = jnp.where(group == 0, 0, jnp.where(group == 1, rows - 1, side_row))
    return row, jnp.where(group == 2, side_col, index)


def join(out, at, edge, inner, rows, cols):
    half = cols // 2
    out[at, at : at + cols] = edge[0]
    out[at + rows - 1, at : at + cols] = edge[1]
    for row in range(1, rows - 1):
        out[at + row, at : at + 1] = edge[2, row - 1 : row]
        out[at + row, at + cols - 1 : at + cols] = edge[2, half + row - 1 : half + row]
        out[at + row, at + 1 : at + cols - 1] = inner[row - 1]


def write_sides(left, right, edge):
    rows, half = left.shape[0], edge.shape[1] // 2
    for out, corner, first in ((left, 0, 0), (right, 2 * half - 1, half)):
        out[0] = edge[0, corner : corner + 1]
        out[rows - 1] = edge[1, corner : corner + 1]
        for row in range(1, rows - 1):
            out[row] = edge[2, first + row - 1 : first + row]


def frame(out, above, below, left, right, rows, cols):
    out[0, 1 : cols + 1] = above[0]
    out[rows + 1, 1 : cols + 1] = below[0]
    for row in range(rows + 2):
        out[row, 0:1] = left[row]
        out[row, cols + 1 : cols + 2] = right[row]


def largest(value, axis):
    devices = lax.axis_size(axis)
    if devices & (devices - 1):
        return lax.pmax(value, axis)
    for bit in range(devices.bit_length() - 1):
        pairs = [(i, i ^ (1 << bit)) for i in range(devices)]
        value = jnp.maximum(value, lax.ppermute(value, axis, pairs))
    return value


def assemble(out, center, above, below, left, right, depth):
    rows, cols = center.shape[:2]
    out[:depth, depth : depth + cols] = above[...]
    out[depth : depth + rows, depth : depth + cols] = center[...]
    out[depth + rows :, depth : depth + cols] = below[...]
    out[:, :depth] = left[...]
    out[:, depth + cols :] = right[...]


def drift_kernel(top, center, above, below, left, right, out, fresh, old):
    rows, cols, _, width = fresh.shape
    assemble(old, center, above, below, left, right, 2)
    step = CFL / (jnp.max(top[...]) + SPEED_EPS)
    index = row_index(width)

    def one_row(row, carry):
        for col in range(cols):
            code = old[row + 1, col + 1, CODE : CODE + 1, :]
            tile = jnp.zeros((8, width), jnp.float32)
            for k in range(9):
                off_x, off_y = k // 3, k % 3
                offset = jnp.where(index == X, off_x - 1.0, jnp.where(index == Y, off_y - 1.0, 0.0))
                source = old[row + off_x, col + off_y] + offset
                tile = jnp.where(code == k + 1.0, source, tile)
            moved = tile + step * pltpu.roll(tile, 6, 0)
            fresh[row, col] = jnp.where(index <= Y, moved, tile)
        return carry

    lax.fori_loop(0, rows, one_row, 0)
    pltpu.sync_copy(fresh, out)


def drift(top, center, above, below, left, right):
    rows, cols, _, width = center.shape
    return call(
        drift_kernel,
        out_specs=pl.BlockSpec(memory_space=pltpu.HBM),
        out_shape=pltpu.HBM((rows + 2, cols + 2, 8, width), jnp.float32),
        scratch_shapes=[pltpu.VMEM((rows + 2, cols + 2, 8, width), jnp.float32), pltpu.VMEM((rows + 4, cols + 4, 8, width), jnp.float32)],
        name="drift",
    )(top, center, above, below, left, right)


def dot_nt(left, right):
    return lax.dot_general(left, right, (((1,), (1,)), ((), ())), preferred_element_type=jnp.float32)


def setup_kernel(source, coef, edge_weight, inner_weight, fresh, xcol, ycol, sem, *outs):
    pltpu.sync_copy(source, fresh)
    for edge, weight in ((True, edge_weight), (False, inner_weight)):
        setup_list(edge, fresh, coef, weight, xcol, ycol, sem, outs)


def setup_list(edge, fresh, coef, weight, xcol, ycol, sem, outs):
    groups, size, _, width, _ = weight.shape
    rows, cols = fresh.shape[0] - 2, fresh.shape[1] - 2
    base = first_of(edge, rows, cols)

    def place(bin_id):
        return place_of(edge, bin_id // size, lax.rem(bin_id, size), rows, cols)

    def columns(bin_id, slot):
        row, col = place(bin_id)
        tile = fresh[row + 1, col + 1]
        xcol[slot] = jnp.broadcast_to(tile[X : X + 1], (width, width)).T
        ycol[slot] = jnp.broadcast_to(tile[Y : Y + 1], (width, width)).T

    def blocks(bin_id, slot, out):
        row, col = place(bin_id)
        values = coef.at[base + bin_id]
        around = [fresh[row + k // 3, col + k % 3] for k in range(9)]
        xj = [jnp.broadcast_to(around[k][X : X + 1] + (k // 3 - 1.0), (8, width)) for k in range(9)]
        yj = [jnp.broadcast_to(around[k][Y : Y + 1] + (k % 3 - 1.0), (8, width)) for k in range(9)]
        for part in range(width // CHUNK):
            span = pl.ds(part * CHUNK, CHUNK)
            spans = [pl.ds(part * CHUNK + 8 * i, 8) for i in range(CHUNK // 8)]
            xi = [xcol[slot, piece] for piece in spans]
            yi = [ycol[slot, piece] for piece in spans]
            for k in range(9):
                squares, weights = [], []
                for x, y in zip(xi, yi):
                    dx = x - xj[k]
                    dy = y - yj[k]
                    square = jnp.maximum(dx * dx + dy * dy, 1e-14)
                    remain = jnp.maximum(1.0 - square * lax.rsqrt(square), 0.0)
                    squares.append(square)
                    weights.append(remain * remain * remain)
                squares = jnp.concatenate(squares, axis=0).astype(jnp.bfloat16)
                weights = jnp.concatenate(weights, axis=0).astype(jnp.bfloat16)
                ratio = squares * pltpu.reciprocal(squares + jnp.bfloat16(SOFT), approx=True)
                out[k, span] = weights
                values[k, span] = weights * ratio

    def copies(bin_id, slot):
        target = weight.at[bin_id // size, lax.rem(bin_id, size)]
        third = [pl.ds(3 * i, 3) for i in range(3)]
        return [pltpu.make_async_copy(outs[slot].at[at], target.at[at], sem.at[slot, i]) for i, at in enumerate(third)]

    count = groups * size
    columns(0, 0)
    columns(1, 1)

    def some_bins(step, carry):
        for slot in range(BUFFERS):
            bin_id = BUFFERS * step + slot

            @pl.when(step > 0)
            def _():
                for copy in copies(bin_id - BUFFERS, slot):
                    copy.wait()

            blocks(bin_id, slot % 2, outs[slot])
            columns(jnp.minimum(bin_id + 2, count - 1), slot % 2)
            for copy in copies(bin_id, slot):
                copy.start()
        return carry

    lax.fori_loop(0, count // BUFFERS, some_bins, 0)
    for slot in range(BUFFERS):
        for copy in copies(count - BUFFERS + slot, slot):
            copy.wait()


def setup(fresh):
    rows, cols, _, width = fresh.shape
    edge, inner = (groups_of(kind, rows - 2, cols - 2) for kind in (True, False))
    vmem, hbm = pl.BlockSpec(memory_space=pltpu.VMEM), pl.BlockSpec(memory_space=pltpu.HBM)
    return call(
        setup_kernel,
        in_specs=[hbm],
        out_specs=(vmem, hbm, hbm),
        out_shape=(
            pltpu.VMEM((edge[0] * edge[1] + inner[0] * inner[1], 9, width, width), jnp.bfloat16),
            pltpu.HBM((*edge, 9, width, width), jnp.bfloat16),
            pltpu.HBM((*inner, 9, width, width), jnp.bfloat16),
        ),
        scratch_shapes=[
            pltpu.VMEM(fresh.shape, jnp.float32),
            pltpu.VMEM((2, width, width), jnp.float32),
            pltpu.VMEM((2, width, width), jnp.float32),
            pltpu.SemaphoreType.DMA((BUFFERS, 3)),
        ]
        + [pltpu.VMEM((9, width, width), jnp.bfloat16)] * BUFFERS,
        name="setup",
    )(in_hbm(fresh))


def first_kernel(kappa, edge, fresh, coef, weight, second, third, sums, pv, *rest):
    feat = rest[-1]
    group = pl.program_id(0)
    size, _, width, _ = weight.shape

    @pl.when(group == 0)
    def _():
        def one_row(r, carry):
            tiles = []
            for col in range(fresh.shape[1]):
                tile = fresh[r, col]
                x, y, u, v = (tile[i : i + 1] for i in range(4))
                vol = tile[VOL : VOL + 1]
                zero = jnp.zeros_like(vol)
                vol_u, vol_v = vol * u, vol * v
                base = [vol, vol * x, vol * y, vol_u, vol_v, vol_u * x + vol_v * y, vol * tile[PRES : PRES + 1], zero]
                along_x = [zero, vol, zero, zero, zero, vol_u, zero, zero]
                along_y = [zero, zero, vol, zero, zero, vol_v, zero, zero]
                tiles.append([jnp.concatenate(rows, axis=0) for rows in (base, along_x, along_y)])
            for col in range(fresh.shape[1]):
                for i in range(3):
                    feat[r, col, i] = tiles[col][i]
            return carry

        lax.fori_loop(0, fresh.shape[0], one_row, 0)

    base = first_of(edge, fresh.shape[0] - 2, fresh.shape[1] - 2)
    outs = ([], [], [], [])
    for index in range(size):
        row, col = place_of(edge, group, index, fresh.shape[0] - 2, fresh.shape[1] - 2)
        around = []
        for k in range(9):
            off_x, off_y = k // 3 - 1, k % 3 - 1
            features = feat[row + k // 3, col + k % 3, 0]
            if off_x:
                features = features + float(off_x) * feat[row + k // 3, col + k % 3, 1]
            if off_y:
                features = features + float(off_y) * feat[row + k // 3, col + k % 3, 2]
            around.append(split(features))
        around = jnp.concatenate(around, axis=1)
        both = [
            side_by_side(*(part.at[index] for part in (weight, second, third))),
            side_by_side(coef.at[base + group * size + index]),
        ]
        total = dot_nt(jnp.concatenate(both, axis=0), around)
        total = (total[:, :8] + total[:, 8:]).T
        total_w, total_c = total[:, :width], total[:, width:]
        tile = fresh[row + 1, col + 1]
        x, y, u, v = (tile[i : i + 1] for i in range(4))
        vol = tile[VOL : VOL + 1]
        w_0, w_x, w_y, w_u, w_v, w_flow = (total_w[i : i + 1] for i in range(6))
        source = x * w_u + y * w_v - w_flow - (u * x + v * y) * w_0 + u * w_x + v * w_y
        source = kappa * 20.0 * source
        rden = 1.0 / (1.0 + kappa * 40.0 * total_c[0:1])
        first = (source + kappa * 40.0 * total_c[6:7]) * rden
        for out, value in zip(outs, (source, rden, vol, first * vol)):
            out.append(value)
    for place in range(3):
        sums[place, group] = jnp.concatenate(outs[place], axis=0)
    pv[group] = jnp.concatenate(outs[3], axis=0)
    if edge:

        @pl.when(group == 2)
        def _():
            write_sides(*rest[:2], pv)


def first_sweep(kappa, edge, fresh, coef, weight):
    groups, size, _, width, _ = weight.shape
    rows, cols = fresh.shape[:2]
    vmem = pl.BlockSpec(memory_space=pltpu.VMEM)
    return call(
        functools.partial(first_kernel, kappa, edge),
        grid=(groups,),
        in_specs=[once(fresh), vmem, *thirds(size, width)],
        out_specs=[vmem] * (4 if edge else 2),
        out_shape=[
            pltpu.VMEM((3, groups, size, width), jnp.float32),
            pltpu.VMEM((groups, size, width), jnp.float32),
        ]
        + [pltpu.VMEM((rows - 2, 1, width), jnp.float32)] * (2 if edge else 0),
        scratch_shapes=[pltpu.VMEM((rows, cols, 3, 8, width), jnp.float32)],
        name="first_sweep",
    )(in_hbm(fresh), pltpu.with_memory_space_constraint(coef, pltpu.VMEM), *[in_hbm(weight)] * 3)


def sweep_kernel(kappa, last, edge, rows, cols, count, *refs):
    before_edge, before_inner, *halo = refs[: count - 2]
    coef, sums = refs[count - 2 : count]
    pv, *rest = refs[count:-2]
    pressure = rest[-1] if last else None
    ext, tiles = refs[-2:]
    groups, size, width = pv.shape
    base = first_of(edge, rows, cols)
    join(ext, 1, before_edge, before_inner, rows, cols)
    if edge:
        frame(ext, *halo, rows, cols)

    def spread(row, carry):
        for col in range(cols + 2):
            tiles[row, col] = jnp.broadcast_to(ext[row, col : col + 1, :], (16, width)).astype(jnp.bfloat16)
        return carry

    if edge:
        lax.fori_loop(0, rows + 2, spread, 0)
    else:
        lax.fori_loop(1, rows + 1, spread, 0)
    ones = jnp.ones((16, width), jnp.bfloat16)

    def one_group(group, carry):
        totals = []
        for index in range(size):
            row, col = place_of(edge, group, index, rows, cols)
            around = [tiles[row + k // 3, col + k % 3] for k in range(9)]
            parts = []
            for part in range(width // 16):
                total = None
                for k in range(9):
                    term = coef[base + group * size + index, k, pl.ds(part * 16, 16)] * around[k]
                    total = term if total is None else total + term
                parts.append(total)
            totals.append(dot_nt(ones, jnp.concatenate(parts, axis=0))[0:1])
        total = jnp.concatenate(totals, axis=0)
        value = (sums[0, group] + kappa * 40.0 * total) * sums[1, group]
        vol = sums[2, group]
        pv[group] = value * vol
        if last:
            pressure[group] = jnp.where(vol > 0.0, value, 0.0)
        return carry

    lax.fori_loop(0, groups, one_group, 0)
    if edge:
        write_sides(*rest[:2], pv)


def sweep(kappa, last, edge, shape, pv, halo, coef, sums):
    rows, cols, width = shape
    groups, size = groups_of(edge, rows, cols)
    vmem = pl.BlockSpec(memory_space=pltpu.VMEM)
    out = pltpu.VMEM((groups, size, width), jnp.float32)
    side = pltpu.VMEM((rows, 1, width), jnp.float32)
    outs = [out] + [side] * (2 if edge else 0) + [out] * (1 if last else 0)
    args = (*pv, *(halo if edge else ()), pltpu.with_memory_space_constraint(coef, pltpu.VMEM), sums)
    return call(
        functools.partial(sweep_kernel, kappa, last, edge, rows, cols, len(args)),
        in_specs=[vmem] * len(args),
        out_specs=[vmem] * len(outs),
        out_shape=outs,
        scratch_shapes=[
            pltpu.VMEM((rows + 2, cols + 2, width), jnp.float32),
            pltpu.VMEM((rows + 2, cols + 2, 16, width), jnp.bfloat16),
        ],
        name="sweep",
    )(*args)


def push_kernel(kappa, edge, count, *refs):
    before_edge, before_inner, *halo = refs[: count - (7 if edge else 5)]
    fresh, weight, second, third, pressure = refs[count - (7 if edge else 5) : count][:5]
    ext, feat = refs[-2:]
    group = pl.program_id(0)
    size, _, width, _ = weight.shape
    rows, cols = fresh.shape[0] - 2, fresh.shape[1] - 2

    @pl.when(group == 0)
    def _():
        join(ext, 1, before_edge, before_inner, rows, cols)
        if edge:
            frame(ext, *halo, rows, cols)

        def one_row(r, carry):
            tiles = []
            for col in range(ext.shape[1]):
                value = ext[r, col : col + 1, :]
                tile = fresh[r, col]
                x, y, vol = tile[X : X + 1], tile[Y : Y + 1], tile[VOL : VOL + 1]
                zero = jnp.zeros_like(x)
                tiles.append(jnp.concatenate([value, value * x, value * y, zero, vol, vol * x, vol * y, zero], axis=0))
            for col in range(ext.shape[1]):
                feat[r, col] = tiles[col]
            return carry

        lax.fori_loop(0, rows + 2, one_row, 0)

    feature = row_index(width)
    news = ([], [])
    for index in range(size):
        row, col = place_of(edge, group, index, rows, cols)
        around = []
        for k in range(9):
            tile = feat[row + k // 3, col + k % 3]
            off_x, off_y = k // 3 - 1.0, k % 3 - 1.0
            pv, vol = tile[0:1], tile[4:5]
            if off_x:
                tile = tile + jnp.where(feature == 1, off_x * pv, jnp.where(feature == 5, off_x * vol, 0.0))
            if off_y:
                tile = tile + jnp.where(feature == 2, off_y * pv, jnp.where(feature == 6, off_y * vol, 0.0))
            around.append(split(tile))
        total = dot_nt(side_by_side(*(part.at[index] for part in (weight, second, third))), jnp.concatenate(around, axis=1))
        total = (total[:, :8] + total[:, 8:]).T
        tile = fresh[row + 1, col + 1]
        own = pressure[group, index : index + 1, :]
        alive = tile[VOL : VOL + 1] > 0.0
        for axis in (0, 1):
            at = tile[axis : axis + 1]
            grad = at * total[0:1] - total[1 + axis : 2 + axis] - own * (at * total[4:5] - total[5 + axis : 6 + axis])
            news[axis].append(jnp.where(alive, tile[2 + axis : 3 + axis] + kappa * 20.0 * grad, 0.0))
    if not edge:
        out = refs[count]
        for axis in (0, 1):
            out[axis, group] = jnp.concatenate(news[axis], axis=0)
        return
    inner_pressure, inner_new = refs[count - 2 : count]
    out_pressure, out_new, new = refs[count:-2]
    for axis in (0, 1):
        new[axis, group] = jnp.concatenate(news[axis], axis=0)

    @pl.when(group == 2)
    def _():
        join(out_pressure, 0, pressure, inner_pressure, rows, cols)
        for axis in (0, 1):
            join(out_new.at[axis], 0, new.at[axis], inner_new.at[axis], rows, cols)


def push(kappa, edge, pv, halo, fresh, weight, pressure, inner):
    groups, size, _, width, _ = weight.shape
    rows, cols = fresh.shape[:2]
    vmem = pl.BlockSpec(memory_space=pltpu.VMEM)
    weight = in_hbm(weight)
    args = (*pv, *(halo if edge else ()), in_hbm(fresh), *[weight] * 3, pressure, *(inner if edge else ()))
    specs = [vmem] * len(args)
    first = len(pv) + (len(halo) if edge else 0)
    specs[first : first + 4] = [once(fresh), *thirds(size, width)]
    if edge:
        outs = [
            jax.ShapeDtypeStruct((rows - 2, cols - 2, width), jnp.float32),
            jax.ShapeDtypeStruct((2, rows - 2, cols - 2, width), jnp.float32),
        ]
    else:
        outs = [pltpu.VMEM((2, groups, size, width), jnp.float32)]
    return call(
        functools.partial(push_kernel, kappa, edge, len(args)),
        grid=(groups,),
        in_specs=specs,
        out_specs=[vmem] * len(outs),
        out_shape=outs,
        scratch_shapes=([pltpu.VMEM((2, groups, size, width), jnp.float32)] if edge else [])
        + [
            pltpu.VMEM((rows, cols, width), jnp.float32),
            pltpu.VMEM((rows, cols, 8, width), jnp.float32),
        ],
        name="push",
    )(*args)


def local(position, velocity, volume, pressure_prev, fill, drift_from):
    shape = volume.shape
    kappa = 1.0 / shape[2]
    even = [lax.axis_index(axis) % 2 == 0 for axis in ("gx", "gy")]
    position, even = lax.optimization_barrier((position, even))
    old, top = prepare(position, velocity, volume, pressure_prev, fill, drift_from)
    around, top = exchange_old(even, old, top, 2)
    fresh = drift(top, old, *around)
    coef, edge_weight, inner_weight = setup(fresh)
    edge_sums, edge_pv, *sides = first_sweep(kappa, True, fresh, coef, edge_weight)
    above, below = exchange_rows(even, edge_pv)
    inner_sums, inner_pv = first_sweep(kappa, False, fresh, coef, inner_weight)
    above, below, inner_pv = lax.optimization_barrier((above, below, inner_pv))
    for step in range(1, SWEEPS):
        last = step == SWEEPS - 1
        before = (edge_pv, inner_pv)
        left, right = exchange_sides(even, above, below, *sides)
        inner_pv, *inner_pressure = sweep(kappa, last, False, shape, before, (), coef, inner_sums)
        left, right, inner_pv = lax.optimization_barrier((left, right, inner_pv))
        halo = (above, below, left, right)
        edge_pv, *rest = sweep(kappa, last, True, shape, before, halo, coef, edge_sums)
        sides, edge_pressure = rest[:2], rest[2:]
        above, below = exchange_rows(even, edge_pv)
    pv = (edge_pv, inner_pv)
    halo = (above, below, *exchange_sides(even, above, below, *sides))
    (inner_new,) = push(kappa, False, pv, halo, fresh, inner_weight, inner_pressure[0], ())
    inner = (inner_pressure[0], inner_new)
    pressure, velocity_new = push(kappa, True, pv, halo, fresh, edge_weight, edge_pressure[0], inner)
    return (pressure, velocity_new)


def solution(mesh):
    return jax.shard_map(
        local,
        mesh=mesh,
        in_specs=(
            P(None, "gx", "gy", None),
            P(None, "gx", "gy", None),
            P("gx", "gy", None),
            P("gx", "gy", None),
            P("gx", "gy"),
            P("gx", "gy"),
        ),
        out_specs=(P("gx", "gy", None), P(None, "gx", "gy", None)),
        check_vma=False,
    )
```

```python
import functools

import jax
import jax.numpy as jnp
from jax import lax
from jax.experimental import pallas as pl
from jax.experimental.pallas import tpu as pltpu
from jax.sharding import PartitionSpec as P

SWEEPS = 4
CFL = 0.25
SPEED_EPS = 1e-06
SOFT = 0.01
CHUNK = 32
BUFFERS = 6
VMEM_LIMIT = 16 * 1024 * 1024

X, Y, U, V, VOL, PRES, CODE = range(7)


def call(kernel, **kwargs):
    return pl.pallas_call(
        kernel, compiler_params=pltpu.CompilerParams(vmem_limit_bytes=VMEM_LIMIT), **kwargs
    )


def in_hbm(array):
    return pltpu.with_memory_space_constraint(array, pltpu.HBM)


def once(array):
    return pl.BlockSpec(array.shape, lambda group: (0,) * array.ndim)


def side_by_side(*blocks):
    return jnp.concatenate([part[k] for part in blocks for k in range(part.shape[0])], axis=1)


def thirds(size, width):
    return [pl.BlockSpec((None, size, 3, width, width), lambda group, i=i: (group, 0, i, 0, 0)) for i in range(3)]


def row_index(width):
    return lax.broadcasted_iota(jnp.int32, (8, width), 0)


def split(value):
    high = value.astype(jnp.bfloat16).astype(jnp.float32)
    return jnp.concatenate([high, value - high], axis=0).astype(jnp.bfloat16)


def dot(left, right):
    return jnp.dot(left, right, preferred_element_type=jnp.float32)


def prepare_kernel(*refs):
    sources, (fill, code, old, top) = refs[:4], refs[4:8]
    arrays, sem = refs[8:12], refs[12]
    copies = [pltpu.make_async_copy(source, array, sem.at[i]) for i, (source, array) in enumerate(zip(sources, arrays))]
    for copy in copies:
        copy.start()
    for copy in copies:
        copy.wait()
    position, velocity, volume, pressure = arrays
    rows, cols, width = volume.shape
    slots = lax.broadcasted_iota(jnp.int32, (cols, width), 1).astype(jnp.float32)
    most = jnp.zeros((cols, width), jnp.float32)

    def along_lanes(values):
        return jnp.broadcast_to(values.astype(jnp.float32), (width, cols)).T

    for row in range(rows):
        live = (slots < along_lanes(fill[row : row + 1])).astype(jnp.float32)
        most = jnp.maximum(most, jnp.abs(velocity[0, row]) * live)
        most = jnp.maximum(most, jnp.abs(velocity[1, row]) * live)
        channels = [
            position[0, row],
            position[1, row],
            velocity[0, row],
            velocity[1, row],
            volume[row] * live,
            pressure[row],
            along_lanes(code[row : row + 1] + 1),
            jnp.zeros((cols, width), jnp.float32),
        ]
        for channel, value in enumerate(channels):
            old[row, :, channel, :] = value
    top[...] = jnp.broadcast_to(jnp.max(most), top.shape)


def prepare(position, velocity, volume, pressure, fill, code):
    rows, cols, width = volume.shape
    arrays = (position, velocity, volume, pressure)
    vmem, hbm = pl.BlockSpec(memory_space=pltpu.VMEM), pl.BlockSpec(memory_space=pltpu.HBM)
    return call(
        prepare_kernel,
        in_specs=[hbm] * 4 + [vmem] * 2,
        out_specs=[vmem] * 2,
        out_shape=(
            pltpu.VMEM((rows, cols, 8, width), jnp.float32),
            pltpu.VMEM((8, width), jnp.float32),
        ),
        scratch_shapes=[pltpu.VMEM(array.shape, jnp.float32) for array in arrays] + [pltpu.SemaphoreType.DMA((4,))],
        name="prepare",
    )(*(in_hbm(array) for array in arrays), fill, code)


def neighbours(axis, even, low, high):
    devices = lax.axis_size(axis)

    def swap(value, first):
        pairs = [(i, i + 1) for i in range(first, devices - 1, 2)]
        return lax.ppermute(value, axis, pairs + [(j, i) for i, j in pairs])

    one = swap(jnp.where(even, high, low), 0)
    two = swap(jnp.where(even, low, high), 1)
    return jnp.where(even, two, one), jnp.where(even, one, two)


def exchange_old(even, shard, top, depth):
    above, below = neighbours("gx", even[0], shard[:depth], shard[-depth:])
    top = largest(top, "gy")
    above, below, top = lax.optimization_barrier((above, below, top))
    low = jnp.concatenate([above[:, :depth], shard[:, :depth], below[:, :depth]], axis=0)
    high = jnp.concatenate([above[:, -depth:], shard[:, -depth:], below[:, -depth:]], axis=0)
    left, right = neighbours("gy", even[1], low, high)
    return (above, below, left, right), largest(top, "gx")


def exchange_rows(even, edge):
    return neighbours("gx", even[0], edge[0][None], edge[1][None])


def exchange_sides(even, above, below, left, right):
    low = jnp.concatenate([above[:, :1], left, below[:, :1]], axis=0)
    high = jnp.concatenate([above[:, -1:], right, below[:, -1:]], axis=0)
    return neighbours("gy", even[1], low, high)


def groups_of(edge, rows, cols):
    return (3, cols) if edge else (rows - 2, cols - 2)


def first_of(edge, rows, cols):
    return 0 if edge else 3 * cols


def place_of(edge, group, index, rows, cols):
    if not edge:
        return group + 1, index + 1
    half = cols // 2
    left = index < half
    side_row = jnp.minimum(jnp.where(left, index, index - half) + 1, rows - 2)
    side_col = jnp.where(left, 0, cols - 1)
    row = jnp.where(group == 0, 0, jnp.where(group == 1, rows - 1, side_row))
    return row, jnp.where(group == 2, side_col, index)


def join(out, at, edge, inner, rows, cols):
    half = cols // 2
    out[at, at : at + cols] = edge[0]
    out[at + rows - 1, at : at + cols] = edge[1]
    for row in range(1, rows - 1):
        out[at + row, at : at + 1] = edge[2, row - 1 : row]
        out[at + row, at + cols - 1 : at + cols] = edge[2, half + row - 1 : half + row]
        out[at + row, at + 1 : at + cols - 1] = inner[row - 1]


def write_sides(left, right, edge):
    rows, half = left.shape[0], edge.shape[1] // 2
    for out, corner, first in ((left, 0, 0), (right, 2 * half - 1, half)):
        out[0] = edge[0, corner : corner + 1]
        out[rows - 1] = edge[1, corner : corner + 1]
        for row in range(1, rows - 1):
            out[row] = edge[2, first + row - 1 : first + row]


def frame(out, above, below, left, right, rows, cols):
    out[0, 1 : cols + 1] = above[0]
    out[rows + 1, 1 : cols + 1] = below[0]
    for row in range(rows + 2):
        out[row, 0:1] = left[row]
        out[row, cols + 1 : cols + 2] = right[row]


def largest(value, axis):
    devices = lax.axis_size(axis)
    if devices & (devices - 1):
        return lax.pmax(value, axis)
    for bit in range(devices.bit_length() - 1):
        pairs = [(i, i ^ (1 << bit)) for i in range(devices)]
        value = jnp.maximum(value, lax.ppermute(value, axis, pairs))
    return value


def assemble(out, center, above, below, left, right, depth):
    rows, cols = center.shape[:2]
    out[:depth, depth : depth + cols] = above[...]
    out[depth : depth + rows, depth : depth + cols] = center[...]
    out[depth + rows :, depth : depth + cols] = below[...]
    out[:, :depth] = left[...]
    out[:, depth + cols :] = right[...]


def drift_kernel(top, center, above, below, left, right, out, fresh, old):
    rows, cols, _, width = fresh.shape
    assemble(old, center, above, below, left, right, 2)
    step = CFL / (jnp.max(top[...]) + SPEED_EPS)
    index = row_index(width)

    def one_row(row, carry):
        for col in range(cols):
            code = old[row + 1, col + 1, CODE : CODE + 1, :]
            tile = jnp.zeros((8, width), jnp.float32)
            for k in range(9):
                off_x, off_y = k // 3, k % 3
                offset = jnp.where(index == X, off_x - 1.0, jnp.where(index == Y, off_y - 1.0, 0.0))
                source = old[row + off_x, col + off_y] + offset
                tile = jnp.where(code == k + 1.0, source, tile)
            moved = tile + step * pltpu.roll(tile, 6, 0)
            fresh[row, col] = jnp.where(index <= Y, moved, tile)
        return carry

    lax.fori_loop(0, rows, one_row, 0)
    pltpu.sync_copy(fresh, out)


def drift(top, center, above, below, left, right):
    rows, cols, _, width = center.shape
    return call(
        drift_kernel,
        out_specs=pl.BlockSpec(memory_space=pltpu.HBM),
        out_shape=pltpu.HBM((rows + 2, cols + 2, 8, width), jnp.float32),
        scratch_shapes=[pltpu.VMEM((rows + 2, cols + 2, 8, width), jnp.float32), pltpu.VMEM((rows + 4, cols + 4, 8, width), jnp.float32)],
        name="drift",
    )(top, center, above, below, left, right)


def dot_nt(left, right):
    return lax.dot_general(left, right, (((1,), (1,)), ((), ())), preferred_element_type=jnp.float32)


def setup_kernel(source, coef, edge_weight, inner_weight, fresh, xcol, ycol, sem, *outs):
    pltpu.sync_copy(source, fresh)
    for edge, weight in ((True, edge_weight), (False, inner_weight)):
        setup_list(edge, fresh, coef, weight, xcol, ycol, sem, outs)


def setup_list(edge, fresh, coef, weight, xcol, ycol, sem, outs):
    groups, size, _, width, _ = weight.shape
    rows, cols = fresh.shape[0] - 2, fresh.shape[1] - 2
    base = first_of(edge, rows, cols)

    def place(bin_id):
        return place_of(edge, bin_id // size, lax.rem(bin_id, size), rows, cols)

    def columns(bin_id, slot):
        row, col = place(bin_id)
        tile = fresh[row + 1, col + 1]
        xcol[slot] = jnp.broadcast_to(tile[X : X + 1], (width, width)).T
        ycol[slot] = jnp.broadcast_to(tile[Y : Y + 1], (width, width)).T

    def blocks(bin_id, slot, out):
        row, col = place(bin_id)
        values = coef.at[base + bin_id]
        around = [fresh[row + k // 3, col + k % 3] for k in range(9)]
        xj = [jnp.broadcast_to(around[k][X : X + 1] + (k // 3 - 1.0), (8, width)) for k in range(9)]
        yj = [jnp.broadcast_to(around[k][Y : Y + 1] + (k % 3 - 1.0), (8, width)) for k in range(9)]
        for part in range(width // CHUNK):
            span = pl.ds(part * CHUNK, CHUNK)
            spans = [pl.ds(part * CHUNK + 8 * i, 8) for i in range(CHUNK // 8)]
            xi = [xcol[slot, piece] for piece in spans]
            yi = [ycol[slot, piece] for piece in spans]
            for k in range(9):
                squares, weights = [], []
                for x, y in zip(xi, yi):
                    dx = x - xj[k]
                    dy = y - yj[k]
                    square = jnp.maximum(dx * dx + dy * dy, 1e-14)
                    remain = jnp.maximum(1.0 - square * lax.rsqrt(square), 0.0)
                    squares.append(square)
                    weights.append(remain * remain * remain)
                squares = jnp.concatenate(squares, axis=0).astype(jnp.bfloat16)
                weights = jnp.concatenate(weights, axis=0).astype(jnp.bfloat16)
                ratio = squares * pltpu.reciprocal(squares + jnp.bfloat16(SOFT), approx=True)
                out[k, span] = weights
                values[k, span] = weights * ratio

    def copies(bin_id, slot):
        target = weight.at[bin_id // size, lax.rem(bin_id, size)]
        third = [pl.ds(3 * i, 3) for i in range(3)]
        return [pltpu.make_async_copy(outs[slot].at[at], target.at[at], sem.at[slot, i]) for i, at in enumerate(third)]

    count = groups * size
    columns(0, 0)
    columns(1, 1)

    def some_bins(step, carry):
        for slot in range(BUFFERS):
            bin_id = BUFFERS * step + slot

            @pl.when(step > 0)
            def _():
                for copy in copies(bin_id - BUFFERS, slot):
                    copy.wait()

            blocks(bin_id, slot % 2, outs[slot])
            columns(jnp.minimum(bin_id + 2, count - 1), slot % 2)
            for copy in copies(bin_id, slot):
                copy.start()
        return carry

    lax.fori_loop(0, count // BUFFERS, some_bins, 0)
    for slot in range(BUFFERS):
        for copy in copies(count - BUFFERS + slot, slot):
            copy.wait()


def setup(fresh):
    rows, cols, _, width = fresh.shape
    edge, inner = (groups_of(kind, rows - 2, cols - 2) for kind in (True, False))
    vmem, hbm = pl.BlockSpec(memory_space=pltpu.VMEM), pl.BlockSpec(memory_space=pltpu.HBM)
    return call(
        setup_kernel,
        in_specs=[hbm],
        out_specs=(vmem, hbm, hbm),
        out_shape=(
            pltpu.VMEM((edge[0] * edge[1] + inner[0] * inner[1], 9, width, width), jnp.bfloat16),
            pltpu.HBM((*edge, 9, width, width), jnp.bfloat16),
            pltpu.HBM((*inner, 9, width, width), jnp.bfloat16),
        ),
        scratch_shapes=[
            pltpu.VMEM(fresh.shape, jnp.float32),
            pltpu.VMEM((2, width, width), jnp.float32),
            pltpu.VMEM((2, width, width), jnp.float32),
            pltpu.SemaphoreType.DMA((BUFFERS, 3)),
        ]
        + [pltpu.VMEM((9, width, width), jnp.bfloat16)] * BUFFERS,
        name="setup",
    )(in_hbm(fresh))


def first_kernel(kappa, edge, fresh, coef, weight, second, third, sums, pv, *rest):
    feat = rest[-1]
    group = pl.program_id(0)
    size, _, width, _ = weight.shape

    @pl.when(group == 0)
    def _():
        def one_row(r, carry):
            tiles = []
            for col in range(fresh.shape[1]):
                tile = fresh[r, col]
                x, y, u, v = (tile[i : i + 1] for i in range(4))
                vol = tile[VOL : VOL + 1]
                zero = jnp.zeros_like(vol)
                vol_u, vol_v = vol * u, vol * v
                base = [vol, vol * x, vol * y, vol_u, vol_v, vol_u * x + vol_v * y, vol * tile[PRES : PRES + 1], zero]
                along_x = [zero, vol, zero, zero, zero, vol_u, zero, zero]
                along_y = [zero, zero, vol, zero, zero, vol_v, zero, zero]
                tiles.append([jnp.concatenate(rows, axis=0) for rows in (base, along_x, along_y)])
            for col in range(fresh.shape[1]):
                for i in range(3):
                    feat[r, col, i] = tiles[col][i]
            return carry

        lax.fori_loop(0, fresh.shape[0], one_row, 0)

    base = first_of(edge, fresh.shape[0] - 2, fresh.shape[1] - 2)
    outs = ([], [], [], [])
    for index in range(size):
        row, col = place_of(edge, group, index, fresh.shape[0] - 2, fresh.shape[1] - 2)
        around = []
        for k in range(9):
            off_x, off_y = k // 3 - 1, k % 3 - 1
            features = feat[row + k // 3, col + k % 3, 0]
            if off_x:
                features = features + float(off_x) * feat[row + k // 3, col + k % 3, 1]
            if off_y:
                features = features + float(off_y) * feat[row + k // 3, col + k % 3, 2]
            around.append(split(features))
        around = jnp.concatenate(around, axis=1)
        both = [
            side_by_side(*(part.at[index] for part in (weight, second, third))),
            side_by_side(coef.at[base + group * size + index]),
        ]
        total = dot_nt(jnp.concatenate(both, axis=0), around)
        total = (total[:, :8] + total[:, 8:]).T
        total_w, total_c = total[:, :width], total[:, width:]
        tile = fresh[row + 1, col + 1]
        x, y, u, v = (tile[i : i + 1] for i in range(4))
        vol = tile[VOL : VOL + 1]
        w_0, w_x, w_y, w_u, w_v, w_flow = (total_w[i : i + 1] for i in range(6))
        source = x * w_u + y * w_v - w_flow - (u * x + v * y) * w_0 + u * w_x + v * w_y
        source = kappa * 20.0 * source
        rden = 1.0 / (1.0 + kappa * 40.0 * total_c[0:1])
        first = (source + kappa * 40.0 * total_c[6:7]) * rden
        for out, value in zip(outs, (source, rden, vol, first * vol)):
            out.append(value)
    for place in range(3):
        sums[place, group] = jnp.concatenate(outs[place], axis=0)
    pv[group] = jnp.concatenate(outs[3], axis=0)
    if edge:

        @pl.when(group == 2)
        def _():
            write_sides(*rest[:2], pv)


def first_sweep(kappa, edge, fresh, coef, weight):
    groups, size, _, width, _ = weight.shape
    rows, cols = fresh.shape[:2]
    vmem = pl.BlockSpec(memory_space=pltpu.VMEM)
    return call(
        functools.partial(first_kernel, kappa, edge),
        grid=(groups,),
        in_specs=[once(fresh), vmem, *thirds(size, width)],
        out_specs=[vmem] * (4 if edge else 2),
        out_shape=[
            pltpu.VMEM((3, groups, size, width), jnp.float32),
            pltpu.VMEM((groups, size, width), jnp.float32),
        ]
        + [pltpu.VMEM((rows - 2, 1, width), jnp.float32)] * (2 if edge else 0),
        scratch_shapes=[pltpu.VMEM((rows, cols, 3, 8, width), jnp.float32)],
        name="first_sweep",
    )(in_hbm(fresh), pltpu.with_memory_space_constraint(coef, pltpu.VMEM), *[in_hbm(weight)] * 3)


def sweep_kernel(kappa, last, edge, rows, cols, count, *refs):
    before_edge, before_inner, *halo = refs[: count - 2]
    coef, sums = refs[count - 2 : count]
    pv, *rest = refs[count:-2]
    pressure = rest[-1] if last else None
    ext, tiles = refs[-2:]
    groups, size, width = pv.shape
    base = first_of(edge, rows, cols)
    join(ext, 1, before_edge, before_inner, rows, cols)
    if edge:
        frame(ext, *halo, rows, cols)

    def spread(row, carry):
        for col in range(cols + 2):
            tiles[row, col] = jnp.broadcast_to(ext[row, col : col + 1, :], (16, width)).astype(jnp.bfloat16)
        return carry

    if edge:
        lax.fori_loop(0, rows + 2, spread, 0)
    else:
        lax.fori_loop(1, rows + 1, spread, 0)
    ones = jnp.ones((16, width), jnp.bfloat16)

    def one_group(group, carry):
        totals = []
        for index in range(size):
            row, col = place_of(edge, group, index, rows, cols)
            around = [tiles[row + k // 3, col + k % 3] for k in range(9)]
            parts = []
            for part in range(width // 16):
                total = None
                for k in range(9):
                    term = coef[base + group * size + index, k, pl.ds(part * 16, 16)] * around[k]
                    total = term if total is None else total + term
                parts.append(total)
            totals.append(dot_nt(ones, jnp.concatenate(parts, axis=0))[0:1])
        total = jnp.concatenate(totals, axis=0)
        value = (sums[0, group] + kappa * 40.0 * total) * sums[1, group]
        vol = sums[2, group]
        pv[group] = value * vol
        if last:
            pressure[group] = jnp.where(vol > 0.0, value, 0.0)
        return carry

    lax.fori_loop(0, groups, one_group, 0)
    if edge:
        write_sides(*rest[:2], pv)


def sweep(kappa, last, edge, shape, pv, halo, coef, sums):
    rows, cols, width = shape
    groups, size = groups_of(edge, rows, cols)
    vmem = pl.BlockSpec(memory_space=pltpu.VMEM)
    out = pltpu.VMEM((groups, size, width), jnp.float32)
    side = pltpu.VMEM((rows, 1, width), jnp.float32)
    outs = [out] + [side] * (2 if edge else 0) + [out] * (1 if last else 0)
    args = (*pv, *(halo if edge else ()), pltpu.with_memory_space_constraint(coef, pltpu.VMEM), sums)
    return call(
        functools.partial(sweep_kernel, kappa, last, edge, rows, cols, len(args)),
        in_specs=[vmem] * len(args),
        out_specs=[vmem] * len(outs),
        out_shape=outs,
        scratch_shapes=[
            pltpu.VMEM((rows + 2, cols + 2, width), jnp.float32),
            pltpu.VMEM((rows + 2, cols + 2, 16, width), jnp.bfloat16),
        ],
        name="sweep",
    )(*args)


def push_kernel(kappa, edge, count, *refs):
    before_edge, before_inner, *halo = refs[: count - (7 if edge else 5)]
    fresh, weight, second, third, pressure = refs[count - (7 if edge else 5) : count][:5]
    ext, feat = refs[-2:]
    group = pl.program_id(0)
    size, _, width, _ = weight.shape
    rows, cols = fresh.shape[0] - 2, fresh.shape[1] - 2

    @pl.when(group == 0)
    def _():
        join(ext, 1, before_edge, before_inner, rows, cols)
        if edge:
            frame(ext, *halo, rows, cols)

        def one_row(r, carry):
            tiles = []
            for col in range(ext.shape[1]):
                value = ext[r, col : col + 1, :]
                tile = fresh[r, col]
                x, y, vol = tile[X : X + 1], tile[Y : Y + 1], tile[VOL : VOL + 1]
                zero = jnp.zeros_like(x)
                tiles.append(jnp.concatenate([value, value * x, value * y, zero, vol, vol * x, vol * y, zero], axis=0))
            for col in range(ext.shape[1]):
                feat[r, col] = tiles[col]
            return carry

        lax.fori_loop(0, rows + 2, one_row, 0)

    feature = row_index(width)
    news = ([], [])
    for index in range(size):
        row, col = place_of(edge, group, index, rows, cols)
        around = []
        for k in range(9):
            tile = feat[row + k // 3, col + k % 3]
            off_x, off_y = k // 3 - 1.0, k % 3 - 1.0
            pv, vol = tile[0:1], tile[4:5]
            if off_x:
                tile = tile + jnp.where(feature == 1, off_x * pv, jnp.where(feature == 5, off_x * vol, 0.0))
            if off_y:
                tile = tile + jnp.where(feature == 2, off_y * pv, jnp.where(feature == 6, off_y * vol, 0.0))
            around.append(split(tile))
        total = dot_nt(side_by_side(*(part.at[index] for part in (weight, second, third))), jnp.concatenate(around, axis=1))
        total = (total[:, :8] + total[:, 8:]).T
        tile = fresh[row + 1, col + 1]
        own = pressure[group, index : index + 1, :]
        alive = tile[VOL : VOL + 1] > 0.0
        for axis in (0, 1):
            at = tile[axis : axis + 1]
            grad = at * total[0:1] - total[1 + axis : 2 + axis] - own * (at * total[4:5] - total[5 + axis : 6 + axis])
            news[axis].append(jnp.where(alive, tile[2 + axis : 3 + axis] + kappa * 20.0 * grad, 0.0))
    if not edge:
        out = refs[count]
        for axis in (0, 1):
            out[axis, group] = jnp.concatenate(news[axis], axis=0)
        return
    inner_pressure, inner_new = refs[count - 2 : count]
    out_pressure, out_new, new = refs[count:-2]
    for axis in (0, 1):
        new[axis, group] = jnp.concatenate(news[axis], axis=0)

    @pl.when(group == 2)
    def _():
        join(out_pressure, 0, pressure, inner_pressure, rows, cols)
        for axis in (0, 1):
            join(out_new.at[axis], 0, new.at[axis], inner_new.at[axis], rows, cols)


def push(kappa, edge, pv, halo, fresh, weight, pressure, inner):
    groups, size, _, width, _ = weight.shape
    rows, cols = fresh.shape[:2]
    vmem = pl.BlockSpec(memory_space=pltpu.VMEM)
    weight = in_hbm(weight)
    args = (*pv, *(halo if edge else ()), in_hbm(fresh), *[weight] * 3, pressure, *(inner if edge else ()))
    specs = [vmem] * len(args)
    first = len(pv) + (len(halo) if edge else 0)
    specs[first : first + 4] = [once(fresh), *thirds(size, width)]
    if edge:
        outs = [
            jax.ShapeDtypeStruct((rows - 2, cols - 2, width), jnp.float32),
            jax.ShapeDtypeStruct((2, rows - 2, cols - 2, width), jnp.float32),
        ]
    else:
        outs = [pltpu.VMEM((2, groups, size, width), jnp.float32)]
    return call(
        functools.partial(push_kernel, kappa, edge, len(args)),
        grid=(groups,),
        in_specs=specs,
        out_specs=[vmem] * len(outs),
        out_shape=outs,
        scratch_shapes=([pltpu.VMEM((2, groups, size, width), jnp.float32)] if edge else [])
        + [
            pltpu.VMEM((rows, cols, width), jnp.float32),
            pltpu.VMEM((rows, cols, 8, width), jnp.float32),
        ],
        name="push",
    )(*args)


def local(position, velocity, volume, pressure_prev, fill, drift_from):
    shape = volume.shape
    kappa = 1.0 / shape[2]
    even = [lax.axis_index(axis) % 2 == 0 for axis in ("gx", "gy")]
    position, even = lax.optimization_barrier((position, even))
    old, top = prepare(position, velocity, volume, pressure_prev, fill, drift_from)
    around, top = exchange_old(even, old, top, 2)
    fresh = drift(top, old, *around)
    coef, edge_weight, inner_weight = setup(fresh)
    edge_sums, edge_pv, *sides = first_sweep(kappa, True, fresh, coef, edge_weight)
    above, below = exchange_rows(even, edge_pv)
    inner_sums, inner_pv = first_sweep(kappa, False, fresh, coef, inner_weight)
    above, below, inner_pv = lax.optimization_barrier((above, below, inner_pv))
    for step in range(1, SWEEPS):
        last = step == SWEEPS - 1
        before = (edge_pv, inner_pv)
        left, right = exchange_sides(even, above, below, *sides)
        inner_pv, *inner_pressure = sweep(kappa, last, False, shape, before, (), coef, inner_sums)
        left, right, inner_pv = lax.optimization_barrier((left, right, inner_pv))
        halo = (above, below, left, right)
        edge_pv, *rest = sweep(kappa, last, True, shape, before, halo, coef, edge_sums)
        sides, edge_pressure = rest[:2], rest[2:]
        above, below = exchange_rows(even, edge_pv)
    pv = (edge_pv, inner_pv)
    halo = (above, below, *exchange_sides(even, above, below, *sides))
    (inner_new,) = push(kappa, False, pv, halo, fresh, inner_weight, inner_pressure[0], ())
    inner = (inner_pressure[0], inner_new)
    pressure, velocity_new = push(kappa, True, pv, halo, fresh, edge_weight, edge_pressure[0], inner)
    return (pressure, velocity_new)


def solution(mesh):
    return jax.shard_map(
        local,
        mesh=mesh,
        in_specs=(
            P(None, "gx", "gy", None),
            P(None, "gx", "gy", None),
            P("gx", "gy", None),
            P("gx", "gy", None),
            P("gx", "gy"),
            P("gx", "gy"),
        ),
        out_specs=(P("gx", "gy", None), P(None, "gx", "gy", None)),
        check_vma=False,
    )
```

```python
import functools

import jax
import jax.numpy as jnp
from jax import lax
from jax.experimental import pallas as pl
from jax.experimental.pallas import tpu as pltpu
from jax.sharding import PartitionSpec as P

SWEEPS = 4
CFL = 0.25
SPEED_EPS = 1e-06
SOFT = 0.01
CHUNK = 64
BUFFERS = 4
VMEM_LIMIT = 16 * 1024 * 1024

X, Y, U, V, VOL, PRES, CODE = range(7)


def call(kernel, **kwargs):
    return pl.pallas_call(
        kernel, compiler_params=pltpu.CompilerParams(vmem_limit_bytes=VMEM_LIMIT), **kwargs
    )


def in_hbm(array):
    return pltpu.with_memory_space_constraint(array, pltpu.HBM)


def once(array):
    return pl.BlockSpec(array.shape, lambda group: (0,) * array.ndim)


def side_by_side(*blocks):
    return jnp.concatenate([part[k] for part in blocks for k in range(part.shape[0])], axis=1)


def thirds(size, width):
    return [pl.BlockSpec((None, size, 3, width, width), lambda group, i=i: (group, 0, i, 0, 0)) for i in range(3)]


def row_index(width):
    return lax.broadcasted_iota(jnp.int32, (8, width), 0)


def split(value):
    high = value.astype(jnp.bfloat16).astype(jnp.float32)
    return jnp.concatenate([high, value - high], axis=0).astype(jnp.bfloat16)


def dot(left, right):
    return jnp.dot(left, right, preferred_element_type=jnp.float32)


def prepare_kernel(*refs):
    sources, (fill, code, old, top) = refs[:4], refs[4:8]
    arrays, sem = refs[8:12], refs[12]
    copies = [pltpu.make_async_copy(source, array, sem.at[i]) for i, (source, array) in enumerate(zip(sources, arrays))]
    for copy in copies:
        copy.start()
    for copy in copies:
        copy.wait()
    position, velocity, volume, pressure = arrays
    rows, cols, width = volume.shape
    slots = lax.broadcasted_iota(jnp.int32, (cols, width), 1).astype(jnp.float32)
    most = jnp.zeros((cols, width), jnp.float32)

    def along_lanes(values):
        return jnp.broadcast_to(values.astype(jnp.float32), (width, cols)).T

    for row in range(rows):
        live = (slots < along_lanes(fill[row : row + 1])).astype(jnp.float32)
        most = jnp.maximum(most, jnp.abs(velocity[0, row]) * live)
        most = jnp.maximum(most, jnp.abs(velocity[1, row]) * live)
        channels = [
            position[0, row],
            position[1, row],
            velocity[0, row],
            velocity[1, row],
            volume[row] * live,
            pressure[row],
            along_lanes(code[row : row + 1] + 1),
            jnp.zeros((cols, width), jnp.float32),
        ]
        for channel, value in enumerate(channels):
            old[row, :, channel, :] = value
    top[...] = jnp.broadcast_to(jnp.max(most), top.shape)


def prepare(position, velocity, volume, pressure, fill, code):
    rows, cols, width = volume.shape
    arrays = (position, velocity, volume, pressure)
    vmem, hbm = pl.BlockSpec(memory_space=pltpu.VMEM), pl.BlockSpec(memory_space=pltpu.HBM)
    return call(
        prepare_kernel,
        in_specs=[hbm] * 4 + [vmem] * 2,
        out_specs=[vmem] * 2,
        out_shape=(
            pltpu.VMEM((rows, cols, 8, width), jnp.float32),
            pltpu.VMEM((8, width), jnp.float32),
        ),
        scratch_shapes=[pltpu.VMEM(array.shape, jnp.float32) for array in arrays] + [pltpu.SemaphoreType.DMA((4,))],
        name="prepare",
    )(*(in_hbm(array) for array in arrays), fill, code)


def neighbours(axis, even, low, high):
    devices = lax.axis_size(axis)

    def swap(value, first):
        pairs = [(i, i + 1) for i in range(first, devices - 1, 2)]
        return lax.ppermute(value, axis, pairs + [(j, i) for i, j in pairs])

    one = swap(jnp.where(even, high, low), 0)
    two = swap(jnp.where(even, low, high), 1)
    return jnp.where(even, two, one), jnp.where(even, one, two)


def exchange_old(even, shard, top, depth):
    above, below = neighbours("gx", even[0], shard[:depth], shard[-depth:])
    top = largest(top, "gy")
    above, below, top = lax.optimization_barrier((above, below, top))
    low = jnp.concatenate([above[:, :depth], shard[:, :depth], below[:, :depth]], axis=0)
    high = jnp.concatenate([above[:, -depth:], shard[:, -depth:], below[:, -depth:]], axis=0)
    left, right = neighbours("gy", even[1], low, high)
    return (above, below, left, right), largest(top, "gx")


def exchange_rows(even, edge):
    return neighbours("gx", even[0], edge[0][None], edge[1][None])


def exchange_sides(even, above, below, left, right):
    low = jnp.concatenate([above[:, :1], left, below[:, :1]], axis=0)
    high = jnp.concatenate([above[:, -1:], right, below[:, -1:]], axis=0)
    return neighbours("gy", even[1], low, high)


def groups_of(edge, rows, cols):
    return (3, cols) if edge else (rows - 2, cols - 2)


def first_of(edge, rows, cols):
    return 0 if edge else 3 * cols


def place_of(edge, group, index, rows, cols):
    if not edge:
        return group + 1, index + 1
    half = cols // 2
    left = index < half
    side_row = jnp.minimum(jnp.where(left, index, index - half) + 1, rows - 2)
    side_col = jnp.where(left, 0, cols - 1)
    row = jnp.where(group == 0, 0, jnp.where(group == 1, rows - 1, side_row))
    return row, jnp.where(group == 2, side_col, index)


def join(out, at, edge, inner, rows, cols):
    half = cols // 2
    out[at, at : at + cols] = edge[0]
    out[at + rows - 1, at : at + cols] = edge[1]
    for row in range(1, rows - 1):
        out[at + row, at : at + 1] = edge[2, row - 1 : row]
        out[at + row, at + cols - 1 : at + cols] = edge[2, half + row - 1 : half + row]
        out[at + row, at + 1 : at + cols - 1] = inner[row - 1]


def write_sides(left, right, edge):
    rows, half = left.shape[0], edge.shape[1] // 2
    for out, corner, first in ((left, 0, 0), (right, 2 * half - 1, half)):
        out[0] = edge[0, corner : corner + 1]
        out[rows - 1] = edge[1, corner : corner + 1]
        for row in range(1, rows - 1):
            out[row] = edge[2, first + row - 1 : first + row]


def frame(out, above, below, left, right, rows, cols):
    out[0, 1 : cols + 1] = above[0]
    out[rows + 1, 1 : cols + 1] = below[0]
    for row in range(rows + 2):
        out[row, 0:1] = left[row]
        out[row, cols + 1 : cols + 2] = right[row]


def largest(value, axis):
    devices = lax.axis_size(axis)
    if devices & (devices - 1):
        return lax.pmax(value, axis)
    for bit in range(devices.bit_length() - 1):
        pairs = [(i, i ^ (1 << bit)) for i in range(devices)]
        value = jnp.maximum(value, lax.ppermute(value, axis, pairs))
    return value


def assemble(out, center, above, below, left, right, depth):
    rows, cols = center.shape[:2]
    out[:depth, depth : depth + cols] = above[...]
    out[depth : depth + rows, depth : depth + cols] = center[...]
    out[depth + rows :, depth : depth + cols] = below[...]
    out[:, :depth] = left[...]
    out[:, depth + cols :] = right[...]


def drift_kernel(top, center, above, below, left, right, out, fresh, old):
    rows, cols, _, width = fresh.shape
    assemble(old, center, above, below, left, right, 2)
    step = CFL / (jnp.max(top[...]) + SPEED_EPS)
    index = row_index(width)

    def one_row(row, carry):
        for col in range(cols):
            code = old[row + 1, col + 1, CODE : CODE + 1, :]
            tile = jnp.zeros((8, width), jnp.float32)
            for k in range(9):
                off_x, off_y = k // 3, k % 3
                offset = jnp.where(index == X, off_x - 1.0, jnp.where(index == Y, off_y - 1.0, 0.0))
                source = old[row + off_x, col + off_y] + offset
                tile = jnp.where(code == k + 1.0, source, tile)
            moved = tile + step * pltpu.roll(tile, 6, 0)
            fresh[row, col] = jnp.where(index <= Y, moved, tile)
        return carry

    lax.fori_loop(0, rows, one_row, 0)
    pltpu.sync_copy(fresh, out)


def drift(top, center, above, below, left, right):
    rows, cols, _, width = center.shape
    return call(
        drift_kernel,
        out_specs=pl.BlockSpec(memory_space=pltpu.HBM),
        out_shape=pltpu.HBM((rows + 2, cols + 2, 8, width), jnp.float32),
        scratch_shapes=[pltpu.VMEM((rows + 2, cols + 2, 8, width), jnp.float32), pltpu.VMEM((rows + 4, cols + 4, 8, width), jnp.float32)],
        name="drift",
    )(top, center, above, below, left, right)


def dot_nt(left, right):
    return lax.dot_general(left, right, (((1,), (1,)), ((), ())), preferred_element_type=jnp.float32)


def setup_kernel(source, coef, edge_weight, inner_weight, fresh, xcol, ycol, sem, *outs):
    pltpu.sync_copy(source, fresh)
    for edge, weight in ((True, edge_weight), (False, inner_weight)):
        setup_list(edge, fresh, coef, weight, xcol, ycol, sem, outs)


def setup_list(edge, fresh, coef, weight, xcol, ycol, sem, outs):
    groups, size, _, width, _ = weight.shape
    rows, cols = fresh.shape[0] - 2, fresh.shape[1] - 2
    base = first_of(edge, rows, cols)

    def place(bin_id):
        return place_of(edge, bin_id // size, lax.rem(bin_id, size), rows, cols)

    def columns(bin_id, slot):
        row, col = place(bin_id)
        tile = fresh[row + 1, col + 1]
        xcol[slot] = jnp.broadcast_to(tile[X : X + 1], (width, width)).T
        ycol[slot] = jnp.broadcast_to(tile[Y : Y + 1], (width, width)).T

    def blocks(bin_id, slot, out):
        row, col = place(bin_id)
        values = coef.at[base + bin_id]
        around = [fresh[row + k // 3, col + k % 3] for k in range(9)]
        xj = [jnp.broadcast_to(around[k][X : X + 1] + (k // 3 - 1.0), (8, width)) for k in range(9)]
        yj = [jnp.broadcast_to(around[k][Y : Y + 1] + (k % 3 - 1.0), (8, width)) for k in range(9)]
        for part in range(width // CHUNK):
            span = pl.ds(part * CHUNK, CHUNK)
            spans = [pl.ds(part * CHUNK + 8 * i, 8) for i in range(CHUNK // 8)]
            xi = [xcol[slot, piece] for piece in spans]
            yi = [ycol[slot, piece] for piece in spans]
            for k in range(9):
                squares, weights = [], []
                for x, y in zip(xi, yi):
                    dx = x - xj[k]
                    dy = y - yj[k]
                    square = jnp.maximum(dx * dx + dy * dy, 1e-14)
                    remain = jnp.maximum(1.0 - square * lax.rsqrt(square), 0.0)
                    squares.append(square)
                    weights.append(remain * remain * remain)
                squares = jnp.concatenate(squares, axis=0).astype(jnp.bfloat16)
                weights = jnp.concatenate(weights, axis=0).astype(jnp.bfloat16)
                ratio = squares * pltpu.reciprocal(squares + jnp.bfloat16(SOFT), approx=True)
                out[k, span] = weights
                values[k, span] = weights * ratio

    def copies(bin_id, slot):
        target = weight.at[bin_id // size, lax.rem(bin_id, size)]
        third = [pl.ds(3 * i, 3) for i in range(3)]
        return [pltpu.make_async_copy(outs[slot].at[at], target.at[at], sem.at[slot, i]) for i, at in enumerate(third)]

    count = groups * size
    columns(0, 0)
    columns(1, 1)

    def some_bins(step, carry):
        for slot in range(BUFFERS):
            bin_id = BUFFERS * step + slot

            @pl.when(step > 0)
            def _():
                for copy in copies(bin_id - BUFFERS, slot):
                    copy.wait()

            blocks(bin_id, slot % 2, outs[slot])
            columns(jnp.minimum(bin_id + 2, count - 1), slot % 2)
            for copy in copies(bin_id, slot):
                copy.start()
        return carry

    lax.fori_loop(0, count // BUFFERS, some_bins, 0)
    for slot in range(BUFFERS):
        for copy in copies(count - BUFFERS + slot, slot):
            copy.wait()


def setup(fresh):
    rows, cols, _, width = fresh.shape
    edge, inner = (groups_of(kind, rows - 2, cols - 2) for kind in (True, False))
    vmem, hbm = pl.BlockSpec(memory_space=pltpu.VMEM), pl.BlockSpec(memory_space=pltpu.HBM)
    return call(
        setup_kernel,
        in_specs=[hbm],
        out_specs=(vmem, hbm, hbm),
        out_shape=(
            pltpu.VMEM((edge[0] * edge[1] + inner[0] * inner[1], 9, width, width), jnp.bfloat16),
            pltpu.HBM((*edge, 9, width, width), jnp.bfloat16),
            pltpu.HBM((*inner, 9, width, width), jnp.bfloat16),
        ),
        scratch_shapes=[
            pltpu.VMEM(fresh.shape, jnp.float32),
            pltpu.VMEM((2, width, width), jnp.float32),
            pltpu.VMEM((2, width, width), jnp.float32),
            pltpu.SemaphoreType.DMA((BUFFERS, 3)),
        ]
        + [pltpu.VMEM((9, width, width), jnp.bfloat16)] * BUFFERS,
        name="setup",
    )(in_hbm(fresh))


def first_kernel(kappa, edge, fresh, coef, weight, second, third, sums, pv, *rest):
    feat = rest[-1]
    group = pl.program_id(0)
    size, _, width, _ = weight.shape

    @pl.when(group == 0)
    def _():
        def one_row(r, carry):
            tiles = []
            for col in range(fresh.shape[1]):
                tile = fresh[r, col]
                x, y, u, v = (tile[i : i + 1] for i in range(4))
                vol = tile[VOL : VOL + 1]
                zero = jnp.zeros_like(vol)
                vol_u, vol_v = vol * u, vol * v
                base = [vol, vol * x, vol * y, vol_u, vol_v, vol_u * x + vol_v * y, vol * tile[PRES : PRES + 1], zero]
                along_x = [zero, vol, zero, zero, zero, vol_u, zero, zero]
                along_y = [zero, zero, vol, zero, zero, vol_v, zero, zero]
                tiles.append([jnp.concatenate(rows, axis=0) for rows in (base, along_x, along_y)])
            for col in range(fresh.shape[1]):
                for i in range(3):
                    feat[r, col, i] = tiles[col][i]
            return carry

        lax.fori_loop(0, fresh.shape[0], one_row, 0)

    base = first_of(edge, fresh.shape[0] - 2, fresh.shape[1] - 2)
    outs = ([], [], [], [])
    for index in range(size):
        row, col = place_of(edge, group, index, fresh.shape[0] - 2, fresh.shape[1] - 2)
        around = []
        for k in range(9):
            off_x, off_y = k // 3 - 1, k % 3 - 1
            features = feat[row + k // 3, col + k % 3, 0]
            if off_x:
                features = features + float(off_x) * feat[row + k // 3, col + k % 3, 1]
            if off_y:
                features = features + float(off_y) * feat[row + k // 3, col + k % 3, 2]
            around.append(split(features))
        around = jnp.concatenate(around, axis=1)
        both = [
            side_by_side(*(part.at[index] for part in (weight, second, third))),
            side_by_side(coef.at[base + group * size + index]),
        ]
        total = dot_nt(jnp.concatenate(both, axis=0), around)
        total = (total[:, :8] + total[:, 8:]).T
        total_w, total_c = total[:, :width], total[:, width:]
        tile = fresh[row + 1, col + 1]
        x, y, u, v = (tile[i : i + 1] for i in range(4))
        vol = tile[VOL : VOL + 1]
        w_0, w_x, w_y, w_u, w_v, w_flow = (total_w[i : i + 1] for i in range(6))
        source = x * w_u + y * w_v - w_flow - (u * x + v * y) * w_0 + u * w_x + v * w_y
        source = kappa * 20.0 * source
        rden = 1.0 / (1.0 + kappa * 40.0 * total_c[0:1])
        first = (source + kappa * 40.0 * total_c[6:7]) * rden
        for out, value in zip(outs, (source, rden, vol, first * vol)):
            out.append(value)
    for place in range(3):
        sums[place, group] = jnp.concatenate(outs[place], axis=0)
    pv[group] = jnp.concatenate(outs[3], axis=0)
    if edge:

        @pl.when(group == 2)
        def _():
            write_sides(*rest[:2], pv)


def first_sweep(kappa, edge, fresh, coef, weight):
    groups, size, _, width, _ = weight.shape
    rows, cols = fresh.shape[:2]
    vmem = pl.BlockSpec(memory_space=pltpu.VMEM)
    return call(
        functools.partial(first_kernel, kappa, edge),
        grid=(groups,),
        in_specs=[once(fresh), vmem, *thirds(size, width)],
        out_specs=[vmem] * (4 if edge else 2),
        out_shape=[
            pltpu.VMEM((3, groups, size, width), jnp.float32),
            pltpu.VMEM((groups, size, width), jnp.float32),
        ]
        + [pltpu.VMEM((rows - 2, 1, width), jnp.float32)] * (2 if edge else 0),
        scratch_shapes=[pltpu.VMEM((rows, cols, 3, 8, width), jnp.float32)],
        name="first_sweep",
    )(in_hbm(fresh), pltpu.with_memory_space_constraint(coef, pltpu.VMEM), *[in_hbm(weight)] * 3)


def sweep_kernel(kappa, last, edge, rows, cols, count, *refs):
    before_edge, before_inner, *halo = refs[: count - 2]
    coef, sums = refs[count - 2 : count]
    pv, *rest = refs[count:-2]
    pressure = rest[-1] if last else None
    ext, tiles = refs[-2:]
    groups, size, width = pv.shape
    base = first_of(edge, rows, cols)
    join(ext, 1, before_edge, before_inner, rows, cols)
    if edge:
        frame(ext, *halo, rows, cols)

    def spread(row, carry):
        for col in range(cols + 2):
            tiles[row, col] = jnp.broadcast_to(ext[row, col : col + 1, :], (16, width)).astype(jnp.bfloat16)
        return carry

    if edge:
        lax.fori_loop(0, rows + 2, spread, 0)
    else:
        lax.fori_loop(1, rows + 1, spread, 0)
    ones = jnp.ones((16, width), jnp.bfloat16)

    def one_group(group, carry):
        totals = []
        for index in range(size):
            row, col = place_of(edge, group, index, rows, cols)
            around = [tiles[row + k // 3, col + k % 3] for k in range(9)]
            parts = []
            for part in range(width // 16):
                total = None
                for k in range(9):
                    term = coef[base + group * size + index, k, pl.ds(part * 16, 16)] * around[k]
                    total = term if total is None else total + term
                parts.append(total)
            totals.append(dot_nt(ones, jnp.concatenate(parts, axis=0))[0:1])
        total = jnp.concatenate(totals, axis=0)
        value = (sums[0, group] + kappa * 40.0 * total) * sums[1, group]
        vol = sums[2, group]
        pv[group] = value * vol
        if last:
            pressure[group] = jnp.where(vol > 0.0, value, 0.0)
        return carry

    lax.fori_loop(0, groups, one_group, 0)
    if edge:
        write_sides(*rest[:2], pv)


def sweep(kappa, last, edge, shape, pv, halo, coef, sums):
    rows, cols, width = shape
    groups, size = groups_of(edge, rows, cols)
    vmem = pl.BlockSpec(memory_space=pltpu.VMEM)
    out = pltpu.VMEM((groups, size, width), jnp.float32)
    side = pltpu.VMEM((rows, 1, width), jnp.float32)
    outs = [out] + [side] * (2 if edge else 0) + [out] * (1 if last else 0)
    args = (*pv, *(halo if edge else ()), pltpu.with_memory_space_constraint(coef, pltpu.VMEM), sums)
    return call(
        functools.partial(sweep_kernel, kappa, last, edge, rows, cols, len(args)),
        in_specs=[vmem] * len(args),
        out_specs=[vmem] * len(outs),
        out_shape=outs,
        scratch_shapes=[
            pltpu.VMEM((rows + 2, cols + 2, width), jnp.float32),
            pltpu.VMEM((rows + 2, cols + 2, 16, width), jnp.bfloat16),
        ],
        name="sweep",
    )(*args)


def push_kernel(kappa, edge, count, *refs):
    before_edge, before_inner, *halo = refs[: count - (7 if edge else 5)]
    fresh, weight, second, third, pressure = refs[count - (7 if edge else 5) : count][:5]
    ext, feat = refs[-2:]
    group = pl.program_id(0)
    size, _, width, _ = weight.shape
    rows, cols = fresh.shape[0] - 2, fresh.shape[1] - 2

    @pl.when(group == 0)
    def _():
        join(ext, 1, before_edge, before_inner, rows, cols)
        if edge:
            frame(ext, *halo, rows, cols)

        def one_row(r, carry):
            tiles = []
            for col in range(ext.shape[1]):
                value = ext[r, col : col + 1, :]
                tile = fresh[r, col]
                x, y, vol = tile[X : X + 1], tile[Y : Y + 1], tile[VOL : VOL + 1]
                zero = jnp.zeros_like(x)
                tiles.append(jnp.concatenate([value, value * x, value * y, zero, vol, vol * x, vol * y, zero], axis=0))
            for col in range(ext.shape[1]):
                feat[r, col] = tiles[col]
            return carry

        lax.fori_loop(0, rows + 2, one_row, 0)

    feature = row_index(width)
    news = ([], [])
    for index in range(size):
        row, col = place_of(edge, group, index, rows, cols)
        around = []
        for k in range(9):
            tile = feat[row + k // 3, col + k % 3]
            off_x, off_y = k // 3 - 1.0, k % 3 - 1.0
            pv, vol = tile[0:1], tile[4:5]
            if off_x:
                tile = tile + jnp.where(feature == 1, off_x * pv, jnp.where(feature == 5, off_x * vol, 0.0))
            if off_y:
                tile = tile + jnp.where(feature == 2, off_y * pv, jnp.where(feature == 6, off_y * vol, 0.0))
            around.append(split(tile))
        total = dot_nt(side_by_side(*(part.at[index] for part in (weight, second, third))), jnp.concatenate(around, axis=1))
        total = (total[:, :8] + total[:, 8:]).T
        tile = fresh[row + 1, col + 1]
        own = pressure[group, index : index + 1, :]
        alive = tile[VOL : VOL + 1] > 0.0
        for axis in (0, 1):
            at = tile[axis : axis + 1]
            grad = at * total[0:1] - total[1 + axis : 2 + axis] - own * (at * total[4:5] - total[5 + axis : 6 + axis])
            news[axis].append(jnp.where(alive, tile[2 + axis : 3 + axis] + kappa * 20.0 * grad, 0.0))
    if not edge:
        out = refs[count]
        for axis in (0, 1):
            out[axis, group] = jnp.concatenate(news[axis], axis=0)
        return
    inner_pressure, inner_new = refs[count - 2 : count]
    out_pressure, out_new, new = refs[count:-2]
    for axis in (0, 1):
        new[axis, group] = jnp.concatenate(news[axis], axis=0)

    @pl.when(group == 2)
    def _():
        join(out_pressure, 0, pressure, inner_pressure, rows, cols)
        for axis in (0, 1):
            join(out_new.at[axis], 0, new.at[axis], inner_new.at[axis], rows, cols)


def push(kappa, edge, pv, halo, fresh, weight, pressure, inner):
    groups, size, _, width, _ = weight.shape
    rows, cols = fresh.shape[:2]
    vmem = pl.BlockSpec(memory_space=pltpu.VMEM)
    weight = in_hbm(weight)
    args = (*pv, *(halo if edge else ()), in_hbm(fresh), *[weight] * 3, pressure, *(inner if edge else ()))
    specs = [vmem] * len(args)
    first = len(pv) + (len(halo) if edge else 0)
    specs[first : first + 4] = [once(fresh), *thirds(size, width)]
    if edge:
        outs = [
            jax.ShapeDtypeStruct((rows - 2, cols - 2, width), jnp.float32),
            jax.ShapeDtypeStruct((2, rows - 2, cols - 2, width), jnp.float32),
        ]
    else:
        outs = [pltpu.VMEM((2, groups, size, width), jnp.float32)]
    return call(
        functools.partial(push_kernel, kappa, edge, len(args)),
        grid=(groups,),
        in_specs=specs,
        out_specs=[vmem] * len(outs),
        out_shape=outs,
        scratch_shapes=([pltpu.VMEM((2, groups, size, width), jnp.float32)] if edge else [])
        + [
            pltpu.VMEM((rows, cols, width), jnp.float32),
            pltpu.VMEM((rows, cols, 8, width), jnp.float32),
        ],
        name="push",
    )(*args)


def local(position, velocity, volume, pressure_prev, fill, drift_from):
    shape = volume.shape
    kappa = 1.0 / shape[2]
    even = [lax.axis_index(axis) % 2 == 0 for axis in ("gx", "gy")]
    position, even = lax.optimization_barrier((position, even))
    old, top = prepare(position, velocity, volume, pressure_prev, fill, drift_from)
    around, top = exchange_old(even, old, top, 2)
    fresh = drift(top, old, *around)
    coef, edge_weight, inner_weight = setup(fresh)
    edge_sums, edge_pv, *sides = first_sweep(kappa, True, fresh, coef, edge_weight)
    above, below = exchange_rows(even, edge_pv)
    inner_sums, inner_pv = first_sweep(kappa, False, fresh, coef, inner_weight)
    above, below, inner_pv = lax.optimization_barrier((above, below, inner_pv))
    for step in range(1, SWEEPS):
        last = step == SWEEPS - 1
        before = (edge_pv, inner_pv)
        inner_pv, *inner_pressure = sweep(kappa, last, False, shape, before, (), coef, inner_sums)
        if step > 1:
            above, below, inner_pv = lax.optimization_barrier((above, below, inner_pv))
        left, right = exchange_sides(even, above, below, *sides)
        left, right, inner_pv = lax.optimization_barrier((left, right, inner_pv))
        halo = (above, below, left, right)
        edge_pv, *rest = sweep(kappa, last, True, shape, before, halo, coef, edge_sums)
        sides, edge_pressure = rest[:2], rest[2:]
        above, below = exchange_rows(even, edge_pv)
    pv = (edge_pv, inner_pv)
    halo = (above, below, *exchange_sides(even, above, below, *sides))
    (inner_new,) = push(kappa, False, pv, halo, fresh, inner_weight, inner_pressure[0], ())
    inner = (inner_pressure[0], inner_new)
    pressure, velocity_new = push(kappa, True, pv, halo, fresh, edge_weight, edge_pressure[0], inner)
    return (pressure, velocity_new)


def solution(mesh):
    return jax.shard_map(
        local,
        mesh=mesh,
        in_specs=(
            P(None, "gx", "gy", None),
            P(None, "gx", "gy", None),
            P("gx", "gy", None),
            P("gx", "gy", None),
            P("gx", "gy"),
            P("gx", "gy"),
        ),
        out_specs=(P("gx", "gy", None), P(None, "gx", "gy", None)),
        check_vma=False,
    )
```
